32 devices in a mesh: section: 2 (over y), fsdp: 16 (over z, x, core).
Axes of the slice: x: 2, y: 2, z: 4, core: 2. Of those that a mesh axis runs over, the one named last changes fastest.
Arguments:
- block_input: bfloat16 [2, 4096, 1536], P(None, 'fsdp'), may hold values from -6 to 6
- cotangent: bfloat16 [2, 4096, 1536], P(None, 'fsdp'), may hold values from -6 to 6
- lengths: int32 [2, 16], P(None, 'fsdp'), may hold values from 128 to 256, as said below
- in_weight: bfloat16 [2, 1536, 6448], P('section', 'fsdp'), may hold values from -0.15625 to 0.15625
- out_weight: bfloat16 [2, 3072, 1536], P('section', 'fsdp'), may hold values from -0.109375 to 0.109375
- conv_weight: bfloat16 [2, 4, 3328], P('section', None, 'fsdp'), may hold values from -3 to 3
- conv_bias: bfloat16 [2, 3328], P('section', 'fsdp'), may hold values from -0.5 to 0.5
- norm_gain: bfloat16 [2, 1536], P('section', 'fsdp'), may hold values from 0.5 to 1.5
- gate_gain: bfloat16 [2, 3072], P('section', 'fsdp'), may hold values from 0.5 to 1.5
- dt_bias: float32 [2, 48], P('section'), may hold values from -6.5 to -2.3
- a_log: float32 [2, 48], P('section'), may hold values from 0 to 2.77
- skip_d: float32 [2, 48], P('section'), may hold values from 0.5 to 1.5
Outputs:
- layer_outputs: bfloat16 [2, 2, 4096, 1536], P('section', None, 'fsdp')
- input_grads: bfloat16 [2, 2, 4096, 1536], P('section', None, 'fsdp')
- in_weight_grad: float32 [2, 1536, 6448], P('section', 'fsdp')
- out_weight_grad: float32 [2, 3072, 1536], P('section', 'fsdp')
- conv_weight_grad: float32 [2, 4, 3328], P('section', None, 'fsdp')
- conv_bias_grad: float32 [2, 3328], P('section', 'fsdp')
- norm_gain_grad: float32 [2, 1536], P('section', 'fsdp')
- gate_gain_grad: float32 [2, 3072], P('section', 'fsdp')
- dt_bias_grad: float32 [2, 48], P('section')
- a_log_grad: float32 [2, 48], P('section')
- skip_d_grad: float32 [2, 48], P('section')
The draws below stay inside these ranges and needn't reach their ends.
Inputs may be any that keep to these rules, and one draw needn't show every extreme that they name: Each slot's sequence fills its first lengths[b, f] rows; some entry equals 256 and some equals 128.
All inputs are finite; a program needn't handle non-finite values.
Results may differ from the reference program's by a relative error of at most 0.012.
The reference program's roundings to bfloat16 on the way count: a program that leaves them out, or rounds other values in their place, can miss the bound.
Values may be sent and summed in bfloat16 or wider, within the bound.
No kernel may reach another device: no remote copies, remote signals or barrier semaphores. Data moves between devices by JAX's collectives and lax.ppermute only.
A program may use at most 256 MiB of HBM per device.

```python
import jax
import jax.numpy as jnp
from jax import lax

D = 1536
INNER = 3072
HEADS = 48
HEAD_DIM = 64
STATE = 128
CONV = 4
MB = 2
ROWS = 256
MIN_LEN = 128
PROJ = 6448
XBC = 3328
TOKENS = 4096
N_SECTION = 2


def draw_lengths(key, part):
    key = jax.random.fold_in(key, 7)
    first_key, second_key, third_key = jax.random.split(key, 3)
    slot_count = MB * (TOKENS // ROWS)
    drawn = jax.random.randint(first_key, (slot_count,), MIN_LEN, ROWS + 1)
    longest = jax.random.randint(second_key, (), 0, slot_count)
    shortest = (longest + 1 + jax.random.randint(third_key, (), 0, slot_count - 1)) % slot_count
    places = jnp.arange(slot_count, dtype=jnp.int32)
    drawn = jnp.where(places == longest, ROWS, drawn)
    drawn = jnp.where(places == shortest, MIN_LEN, drawn)
    return drawn.reshape(MB, TOKENS // ROWS).astype(jnp.int32)


def block_levels(stream_key, shape, cuts, smallest, top_value):
    def one(axis_at, parts):
        heights = jax.random.uniform(jax.random.fold_in(jax.random.fold_in(stream_key, 6), axis_at), (parts,), jnp.float32, smallest / len(cuts), top_value / len(cuts))
        return jnp.repeat(jnp.exp(heights), shape[axis_at] // parts).reshape((-1,) + (1,) * (len(shape) - axis_at - 1))

    factor_of = one(*cuts[0])
    for cut in cuts[1:]:
        factor_of = factor_of * one(*cut)
    return factor_of


def bell_draw(stream_key, dims, width, reach, cuts=(), held_as=jnp.bfloat16):
    entries = jax.random.normal(stream_key, dims, jnp.float32) * width
    if len(cuts) > 0:
        entries = block_levels(stream_key, dims, cuts, -0.22, 0.18) * entries
    return jnp.clip(entries, min=-reach, max=reach).astype(held_as)


def setup_inputs(seed: int = 0) -> dict:
    arg_keys = jax.random.split(jax.random.key(seed), 13)
    return {
        "block_input": bell_draw(arg_keys[0], (MB, TOKENS, D), 1.0, 6.0, ((1, 16),)),
        "cotangent": bell_draw(arg_keys[1], (MB, TOKENS, D), 1.0, 6.0, ((1, 16),)),
        "lengths": draw_lengths(jax.random.fold_in(arg_keys[12], 71), 0),
        "in_weight": bell_draw(arg_keys[3], (N_SECTION, D, PROJ), D ** -0.5, 0.15625, ((0, 2), (1, 16))),
        "out_weight": bell_draw(arg_keys[4], (N_SECTION, INNER, D), INNER ** -0.5, 0.109375, ((0, 2), (1, 16))),
        "conv_weight": bell_draw(arg_keys[5], (N_SECTION, CONV, XBC), CONV ** -0.5, 3.0, ((0, 2), (2, 16))),
        "conv_bias": jnp.clip(jax.random.uniform(arg_keys[6], (N_SECTION, XBC), jnp.float32, -0.5, 0.5) * block_levels(arg_keys[6], (N_SECTION, XBC), ((0, 2), (1, 16)), -0.4, 0.0), -0.5, 0.5).astype(jnp.bfloat16),
        "norm_gain": jnp.clip(1.0 + 0.1 * jax.random.normal(arg_keys[7], (N_SECTION, D), jnp.float32), 0.5, 1.5).astype(jnp.bfloat16),
        "gate_gain": jnp.clip(1.0 + 0.1 * jax.random.normal(arg_keys[8], (N_SECTION, INNER), jnp.float32), 0.5, 1.5).astype(jnp.bfloat16),
        "dt_bias": jnp.clip(-6.5 + 4.2 * jax.random.uniform(arg_keys[9], (N_SECTION, HEADS), jnp.float32) ** block_levels(arg_keys[9], (N_SECTION, HEADS), ((0, 2),), -0.2, 0.2), -6.5, -2.3),
        "a_log": jnp.clip(2.77 * jax.random.uniform(arg_keys[10], (N_SECTION, HEADS), jnp.float32) ** block_levels(arg_keys[10], (N_SECTION, HEADS), ((0, 2),), -0.2, 0.2), 0.0, 2.77),
        "skip_d": jnp.clip(0.5 + 1.0 * jax.random.uniform(arg_keys[11], (N_SECTION, HEADS), jnp.float32) ** block_levels(arg_keys[11], (N_SECTION, HEADS), ((0, 2),), -0.2, 0.2), 0.5, 1.5),
    }


EPS = 1e-05
exact_mode = lax.Precision.HIGHEST

@jax.custom_vjp
def low(v):
    return lax.optimization_barrier(v.astype(jnp.bfloat16)).astype(jnp.float32)

@jax.custom_vjp
def low_back(v):
    return v

def low_keep(v):
    return (low(v), None)

def low_pass(kept, grad):
    return (grad,)

def back_keep(v):
    return (v, None)

def back_low(kept, grad):
    return (low(grad),)
low.defvjp(low_keep, low_pass)
low_back.defvjp(back_keep, back_low)

def rms_rows(values, scale_gain):
    factor = lax.rsqrt(lax.optimization_barrier(jnp.mean(values * values, axis=-1, keepdims=True)) + EPS)
    return values * factor * scale_gain

def mixer_rows(projected, conv_kernel, conv_shift, gate_scale, step_bias, decay_log, skip_scale):
    row_count = projected.shape[0]
    split_end = 2 * INNER + 2 * STATE
    gate_part = projected[:, :INNER]
    conv_in = projected[:, INNER:split_end]
    step_raw = projected[:, split_end:]
    padded = jnp.concatenate([jnp.zeros((CONV - 1, conv_in.shape[1]), jnp.float32), conv_in], axis=0)
    conv_total = jnp.zeros_like(conv_in) + conv_shift
    for offset in range(CONV):
        conv_total = conv_total + conv_kernel[offset] * padded[offset:offset + row_count]
    activated = jax.nn.silu(conv_total)
    x_heads = activated[:, :INNER].reshape(row_count, HEADS, HEAD_DIM)
    b_mat = activated[:, INNER:INNER + STATE]
    c_mat = activated[:, INNER + STATE:]
    step_size = jax.nn.softplus(step_raw + step_bias)
    log_decay = step_size * -jnp.exp(decay_log)
    cumulative = jnp.cumsum(log_decay, axis=0).T
    places = jnp.arange(row_count, dtype=jnp.int32)
    causal = places[:, None] >= places[None, :]
    spread_log = cumulative[:, :, None] - cumulative[:, None, :]
    decays = jnp.where(causal[None], jnp.exp(jnp.where(causal[None], spread_log, 0.0)), 0.0)
    contact = jnp.dot(c_mat, b_mat.T, precision=exact_mode)
    mixing = decays * contact[None] * step_size.T[:, None, :]
    mixed = jnp.einsum('hts,shp->thp', mixing, x_heads, precision=exact_mode)
    mixed = mixed + skip_scale[None, :, None] * x_heads
    gated_rows = mixed.reshape(row_count, INNER) * jax.nn.silu(gate_part)
    return rms_rows(gated_rows, gate_scale)

def layer_slot(inputs_f, length, params):
    in_matrix, out_matrix, conv_kernel, conv_shift, norm_scale, gate_scale, step_bias, decay_log, skip_scale = params
    live_rows = (jnp.arange(inputs_f.shape[0], dtype=jnp.int32) < length).astype(jnp.float32)[:, None]
    normed = low(rms_rows(inputs_f, norm_scale))
    projected = low_back(jnp.dot(normed, in_matrix, precision=exact_mode))
    gated_rows = low(mixer_rows(projected, conv_kernel, conv_shift, gate_scale, step_bias, decay_log, skip_scale))
    branch = low_back(jnp.dot(gated_rows, out_matrix, precision=exact_mode))
    return inputs_f + live_rows * branch

def layer_group(params, group_in, group_len):
    return jax.vmap(lambda one_in, one_len: layer_slot(one_in, one_len, params))(group_in, group_len)

def layer_all(slot_in, slot_len, params):
    per_step = 4
    grouped = slot_in.reshape((slot_in.shape[0] // per_step, per_step) + slot_in.shape[1:])
    lens_grouped = slot_len.reshape(-1, per_step)
    stored = jax.checkpoint(layer_group)
    result = lax.map(lambda paired: stored(params, paired[0], paired[1]), (grouped, lens_grouped))
    return result.reshape(slot_in.shape)

def reference(block_input, cotangent, lengths, in_weight, out_weight, conv_weight, conv_bias, norm_gain, gate_gain, dt_bias, a_log, skip_d):
    slot_count = lengths.shape[0] * lengths.shape[1]
    inputs_f = block_input.astype(jnp.float32).reshape(slot_count, ROWS, D)
    slot_len = lengths.reshape(slot_count)
    params = tuple((weight_arr.astype(jnp.float32) for weight_arr in (in_weight, out_weight, conv_weight, conv_bias, norm_gain, gate_gain, dt_bias, a_log, skip_d)))
    probe = jnp.zeros_like(inputs_f)

    def forward(first_in, all_params, probe_in):
        first = layer_all(first_in, slot_len, tuple((weight_arr[0] for weight_arr in all_params)))
        second_in = low_back(low(first)) + probe_in
        second = layer_all(second_in, slot_len, tuple((weight_arr[1] for weight_arr in all_params)))
        return (second, first)
    second, backward, first = jax.vjp(forward, inputs_f, params, probe, has_aux=True)
    grad_first, grad_params, grad_probe = backward(cotangent.astype(jnp.float32).reshape(slot_count, ROWS, D))
    shape_out = (2, lengths.shape[0], lengths.shape[1] * ROWS, D)
    outputs = jnp.stack([first, second]).reshape(shape_out).astype(jnp.bfloat16)
    input_grads = jnp.stack([grad_first, grad_probe]).reshape(shape_out).astype(jnp.bfloat16)
    return (outputs, input_grads, grad_params[0], grad_params[1], grad_params[2], grad_params[3], grad_params[4], grad_params[5], grad_params[6], grad_params[7], grad_params[8])
```

```python
import jax
import jax.numpy as jnp
from jax import lax
from jax.experimental import pallas as pl
from jax.experimental.pallas import tpu as pltpu
from jax.sharding import PartitionSpec as P

HEAD_DIM = 64
STATE = 128
CONV = 4
EPS = 1e-05
LOG2E = 1.4426950408889634
HALF = 128
WIDE = 512
GROUP = WIDE // HEAD_DIM
TINY = 1e-30
NEG = -1e30
VMEM = 56 * 1024 * 1024
F32 = jnp.float32
BF16 = jnp.bfloat16
EXACT = lax.Precision.HIGHEST


def nt_dot(a, b):
    return lax.dot_general(a, b, (((1,), (1,)), ((), ())), preferred_element_type=F32)


def nn_dot(a, b):
    return jnp.dot(a, b, preferred_element_type=F32)


def sigmoid(v):
    return 0.5 * jnp.tanh(0.5 * v) + 0.5


def conv_rows(values, taps, bias):
    rows = lax.broadcasted_iota(jnp.int32, values.shape, 0)
    total = bias + taps[CONV - 1 : CONV, :] * values
    for back in range(1, CONV):
        moved = jnp.where(rows >= back, pltpu.roll(values, back, 0), 0.0)
        total = total + taps[CONV - 1 - back : CONV - back, :] * moved
    return total


def softplus(v):
    return jnp.maximum(v, 0.0) + jnp.log1p(jnp.exp(-jnp.abs(v)))


def step_terms(step_raw, head_ref):
    rows = step_raw.shape[0]
    step = jnp.maximum(softplus(step_raw + head_ref[0:1, :]), TINY)
    rate = -jnp.exp(head_ref[1:2, :])
    at = lax.broadcasted_iota(jnp.int32, (rows, rows), 0)
    of = lax.broadcasted_iota(jnp.int32, (rows, rows), 1)
    lower = (at >= of).astype(F32)
    sums = jnp.dot(lower, step * rate, precision=EXACT, preferred_element_type=F32) * LOG2E
    return step, rate, sums, sums - jnp.log2(step)


def spread(target, values, groups):
    for g in range(groups):
        target[g] = pltpu.roll(values, (HALF - g * GROUP) % HALF, 1) if g else values


def forward_kernel(
    u_ref, wz_ref, wx_ref, wr_ref, norm_ref, chan_ref, chanr_ref, head_ref, *rest
):
    (nb_ref, gb_ref, z_ref, v_ref, c_ref, y_ref, vr_ref, cr_ref, w_scr, sq_scr, s_scr, col_scr, row_scr) = rest[-13:]
    step_at = pl.program_id(0)
    groups = pl.num_programs(0)
    rows = u_ref.shape[0]

    @pl.when(step_at == 0)
    def _():
        u = u_ref[...].astype(F32)
        scale = lax.rsqrt(jnp.mean(u * u, axis=1, keepdims=True) + EPS)
        nb_ref[0] = (u * scale * norm_ref[...]).astype(BF16)
        raw = nn_dot(nb_ref[0], wr_ref[...])
        vr_ref[0] = raw
        pre = conv_rows(raw[:, : 2 * STATE], chanr_ref[0:4, :], chanr_ref[4:5, :])
        cr_ref[0] = pre
        act = pre * sigmoid(pre)
        s_scr[...] = lax.dot_general(
            act[:, STATE:], act[:, :STATE], (((1,), (1,)), ((), ())), precision=EXACT, preferred_element_type=F32
        )
        _, _, sums, shifted = step_terms(raw[:, 2 * STATE : 3 * STATE], head_ref)
        spread(col_scr, sums, w_scr.shape[0])
        row_scr[...] = shifted.T
        sq_scr[...] = jnp.zeros_like(sq_scr)

    nb = nb_ref[0]
    z = nn_dot(nb, wz_ref[...])
    z_ref[0] = z
    v = nn_dot(nb, wx_ref[...])
    v_ref[0] = v
    c = conv_rows(v, chan_ref[0:4, :], chan_ref[4:5, :])
    c_ref[0] = c
    x = c * sigmoid(c)
    x_low = x.astype(BF16)
    cols = col_scr[step_at]
    rws = row_scr[pl.ds(pl.multiple_of(step_at * GROUP, GROUP), GROUP), :]
    lane = lax.broadcasted_iota(jnp.int32, (HALF, HALF), 1)
    causal = lax.broadcasted_iota(jnp.int32, (HALF, HALF), 0) >= lane
    first = lane < HEAD_DIM
    parts = []
    for pair in range(GROUP // 2):
        here = slice(pair * HALF, (pair + 1) * HALF)
        pieces = []
        for tb in range(rows // HALF):
            t_here = slice(tb * HALF, (tb + 1) * HALF)
            both = []
            for h in (2 * pair, 2 * pair + 1):
                col = cols[t_here, h : h + 1]
                mix = []
                for sb in range(tb + 1):
                    s_here = slice(sb * HALF, (sb + 1) * HALF)
                    gap = col - rws[h : h + 1, s_here]
                    if sb == tb:
                        gap = jnp.where(causal, gap, NEG)
                    mix.append((jnp.exp2(gap) * s_scr[t_here, s_here]).astype(BF16))
                mix = jnp.concatenate(mix, axis=1) if len(mix) > 1 else mix[0]
                both.append(nn_dot(mix, x_low[: (tb + 1) * HALF, here]))
            pieces.append(jnp.where(first, both[0], both[1]))
        parts.append(jnp.concatenate(pieces, axis=0))
    y = jnp.concatenate(parts, axis=1) + chan_ref[6:7, :] * x
    y_ref[0] = y
    w = y * (z * sigmoid(z))
    w_scr[step_at] = w
    sq_scr[...] += jnp.sum(w * w, axis=1, keepdims=True)

    @pl.when(step_at == groups - 1)
    def _():
        inner = w_scr.shape[0] * WIDE
        scale = lax.rsqrt(sq_scr[...] * (1.0 / inner) + EPS)
        for g in range(w_scr.shape[0]):
            here = slice(g * WIDE, (g + 1) * WIDE)
            gb_ref[0, :, here] = (w_scr[g] * scale * gain_of(norm_ref, rest[0], g)).astype(BF16)


def gain_of(_, gain_ref, g):
    return gain_ref[:, g * WIDE : (g + 1) * WIDE]


def forward_slot(place, kept, u, w_in, norm_gain, chan, chan_r, heads, gate_gain, slots):
    rows, width = u.shape
    inner = chan.shape[1]
    groups = inner // WIDE
    tail = w_in.shape[1] - 2 * inner
    shapes = [
        ((rows, width), BF16),
        ((rows, inner), BF16),
        ((rows, inner), F32),
        ((rows, inner), F32),
        ((rows, inner), F32),
        ((rows, inner), F32),
        ((rows, tail), F32),
        ((rows, 2 * STATE), F32),
    ]
    wide_out = lambda: pl.BlockSpec((1, rows, WIDE), lambda i: (place, 0, i))
    whole = lambda a, b: pl.BlockSpec((a, b), lambda i: (0, 0))
    whole_out = lambda b: pl.BlockSpec((1, rows, b), lambda i: (place, 0, 0))
    in_specs = [
        whole(rows, width),
        pl.BlockSpec((width, WIDE), lambda i: (0, i)),
        pl.BlockSpec((width, WIDE), lambda i: (0, groups + i)),
        pl.BlockSpec((width, tail), lambda i: (0, 2 * inner // tail)),
        whole(1, width),
        pl.BlockSpec((8, WIDE), lambda i: (0, i)),
        whole(8, 2 * STATE),
        whole(8, HALF),
        whole(1, inner),
    ]
    args = [u, w_in, w_in, w_in, norm_gain, chan, chan_r, heads, gate_gain]
    aliases = {}
    if kept is not None:
        for k, arr in enumerate(kept):
            aliases[len(args)] = k
            args.append(arr)
            in_specs.append(pl.BlockSpec(memory_space=pl.ANY))
    out_specs = [whole_out(width), whole_out(inner)] + [wide_out() for _ in range(4)] + [whole_out(tail), whole_out(2 * STATE)]
    return pl.pallas_call(
        forward_kernel,
        grid=(groups,),
        in_specs=in_specs,
        out_specs=out_specs,
        out_shape=[jax.ShapeDtypeStruct((slots,) + s, d) for s, d in shapes],
        scratch_shapes=[
            pltpu.VMEM((groups, rows, WIDE), F32),
            pltpu.VMEM((rows, 1), F32),
            pltpu.VMEM((rows, rows), F32),
            pltpu.VMEM((groups, rows, HALF), F32),
            pltpu.VMEM((HALF, rows), F32),
        ],
        input_output_aliases=aliases,
        compiler_params=pltpu.CompilerParams(vmem_limit_bytes=VMEM),
        name="forward_slot",
    )(*args)


def backward_kernel(
    at_ref,
    g_ref,
    u_ref,
    wo_ref,
    wz_ref,
    wx_ref,
    wr_ref,
    z_ref,
    v_ref,
    c_ref,
    y_ref,
    vr_ref,
    cr_ref,
    norm_ref,
    chan_ref,
    chanr_ref,
    head_ref,
    *rest,
):
    (
        du_ref, dz_ref, dv_ref, dr_ref, cg_ref, cgr_ref, ng_ref, hg_ref,
        dob_scr, dgb_scr, sq_scr, we_scr, st_scr, ds_scr, bcol_scr, trow_scr, colr_scr, rowr_scr, step_scr, act_scr, dn_scr,
    ) = rest[-21:]
    groups = pl.num_programs(0) // 2
    at = pl.program_id(0)
    rows, width = g_ref.shape
    inner = dgb_scr.shape[0] * WIDE

    @pl.when(at == 0)
    def _():
        live = lax.broadcasted_iota(jnp.int32, (rows, 1), 0) < at_ref[1]
        dob_scr[...] = jnp.where(live, g_ref[...].astype(F32), 0.0).astype(BF16)
        sq_scr[...] = jnp.zeros_like(sq_scr)
        we_scr[...] = jnp.zeros_like(we_scr)
        ds_scr[...] = jnp.zeros_like(ds_scr)
        dn_scr[...] = jnp.zeros_like(dn_scr)
        rowr_scr[...] = jnp.zeros_like(rowr_scr)
        pre = cr_ref[0]
        act = pre * sigmoid(pre)
        act_scr[...] = act
        st_scr[...] = lax.dot_general(
            act[:, :STATE], act[:, STATE:], (((1,), (1,)), ((), ())), precision=EXACT, preferred_element_type=F32
        )
        step, rate, sums, shifted = step_terms(vr_ref[0, :, 2 * STATE : 3 * STATE], head_ref)
        step_scr[...] = step
        spread(bcol_scr, shifted, dgb_scr.shape[0])
        trow_scr[...] = sums.T

    @pl.when(at < groups)
    def _():
        dgb = nt_dot(dob_scr[...], wo_ref[...])
        dgb_scr[at] = dgb
        z = z_ref[0]
        w = y_ref[0] * (z * sigmoid(z))
        sq_scr[...] += jnp.sum(w * w, axis=1, keepdims=True)
        we_scr[...] += jnp.sum(w * (dgb * chan_ref[5:6, :]), axis=1, keepdims=True)

    @pl.when(at >= groups)
    def _():
        j = at - groups
        q = lax.rsqrt(sq_scr[...] * (1.0 / inner) + EPS)
        pull = q * q * q * (we_scr[...] * (1.0 / inner))
        dgb = dgb_scr[j]
        z = z_ref[0]
        y = y_ref[0]
        sz = sigmoid(z)
        silu_z = z * sz
        w = y * silu_z
        dw = q * (dgb * chan_ref[5:6, :]) - w * pull
        cg_ref[5:6, :] = jnp.sum(w * q * dgb, axis=0, keepdims=True)
        dy = dw * silu_z
        dz = (dw * y * (sz * (1.0 + z * (1.0 - sz)))).astype(BF16)
        dz_ref[0] = dz
        dn = nt_dot(dz, wz_ref[...])

        c = c_ref[0]
        sc = sigmoid(c)
        x = c * sc
        x_low = x.astype(BF16)
        dy_low = dy.astype(BF16)
        cg_ref[6:7, :] = jnp.sum(dy * x, axis=0, keepdims=True)
        cg_ref[7:8, :] = jnp.zeros((1, WIDE), F32)
        cols = bcol_scr[j]
        head_rows = pl.ds(pl.multiple_of(j * GROUP, GROUP), GROUP)
        rws = trow_scr[head_rows, :]
        lane = lax.broadcasted_iota(jnp.int32, (HALF, HALF), 1)
        causal = lane >= lax.broadcasted_iota(jnp.int32, (HALF, HALF), 0)
        first = lane < HEAD_DIM
        lane_row = lax.broadcasted_iota(jnp.int32, (1, HALF), 1)
        sub = lax.broadcasted_iota(jnp.int32, (GROUP, HALF), 0)
        blocks = rows // HALF
        col_sums = [jnp.zeros((HALF, HALF), F32) for _ in range(blocks)]
        row_sums = [jnp.zeros((GROUP, HALF), F32) for _ in range(blocks)]
        parts = []
        for pair in range(GROUP // 2):
            here = slice(pair * HALF, (pair + 1) * HALF)
            pieces = []
            row_part = [[None] * blocks, [None] * blocks]
            for sb in range(blocks):
                s_here = slice(sb * HALF, (sb + 1) * HALF)
                x_here = x_low[s_here, here]
                split = (
                    jnp.where(first, x_here, jnp.zeros_like(x_here)),
                    jnp.where(first, jnp.zeros_like(x_here), x_here),
                )
                mixes = [[], []]
                lane_sum = [None, None]
                for tb in range(sb, blocks):
                    t_here = slice(tb * HALF, (tb + 1) * HALF)
                    dy_here = dy_low[t_here, here]
                    contact = st_scr[s_here, t_here]
                    touched = None
                    for k in range(2):
                        h = 2 * pair + k
                        gap = rws[h : h + 1, t_here] - cols[s_here, h : h + 1]
                        if sb == tb:
                            gap = jnp.where(causal, gap, NEG)
                        decay = jnp.exp2(gap)
                        mix = decay * contact
                        meet = nt_dot(split[k], dy_here)
                        through = decay * meet
                        pairs = through * contact
                        touched = through if touched is None else touched + through
                        mixes[k].append(mix.astype(BF16))
                        lane_sum[k] = pairs if lane_sum[k] is None else lane_sum[k] + pairs
                        down = jnp.sum(pairs, axis=0, keepdims=True)
                        row_part[k][tb] = down if row_part[k][tb] is None else row_part[k][tb] + down
                    ds_scr[s_here, t_here] += touched
                out = []
                for k in range(2):
                    h = 2 * pair + k
                    mix = jnp.concatenate(mixes[k], axis=1) if len(mixes[k]) > 1 else mixes[k][0]
                    out.append(nn_dot(mix, dy_low[sb * HALF :, here]))
                    total = jnp.sum(lane_sum[k], axis=1, keepdims=True)
                    col_sums[sb] = jnp.where(lane_row == h, total, col_sums[sb])
                pieces.append(jnp.where(first, out[0], out[1]))
            for k in range(2):
                for tb in range(blocks):
                    row_sums[tb] = jnp.where(sub == 2 * pair + k, row_part[k][tb], row_sums[tb])
            parts.append(jnp.concatenate(pieces, axis=0))
        colr_scr[j] = jnp.concatenate(col_sums, axis=0)
        rowr_scr[head_rows, :] = jnp.concatenate(row_sums, axis=1)
        dx = jnp.concatenate(parts, axis=1) + chan_ref[6:7, :] * dy
        dc = dx * (sc * (1.0 + c * (1.0 - sc)))
        dv = conv_back(dc, v_ref[0], chan_ref, cg_ref).astype(BF16)
        dv_ref[0] = dv
        dn_scr[...] += dn + nt_dot(dv, wx_ref[...])

    @pl.when(at == 2 * groups - 1)
    def _():
        act = act_scr[...]
        ds = ds_scr[...].astype(BF16)
        act_low = act.astype(BF16)
        d_b = nn_dot(ds, act_low[:, STATE:])
        d_c = lax.dot_general(ds, act_low[:, :STATE], (((0,), (0,)), ((), ())), preferred_element_type=F32)
        pre = cr_ref[0]
        sp = sigmoid(pre)
        d_pre = jnp.concatenate([d_b, d_c], axis=1) * (sp * (1.0 + pre * (1.0 - sp)))
        d_raw = conv_back(d_pre, vr_ref[0, :, : 2 * STATE], chanr_ref, cgr_ref)
        cgr_ref[5:8, :] = jnp.zeros((3, 2 * STATE), F32)
        col_total = colr_scr[0]
        for g in range(1, colr_scr.shape[0]):
            col_total = col_total + pltpu.roll(colr_scr[g], g * GROUP, 1)
        d_sums = rowr_scr[...].T - col_total
        at_row = lax.broadcasted_iota(jnp.int32, (rows, rows), 0)
        of_row = lax.broadcasted_iota(jnp.int32, (rows, rows), 1)
        upper = (of_row >= at_row).astype(F32)
        d_log = jnp.dot(upper, d_sums, precision=EXACT, preferred_element_type=F32)
        step = step_scr[...]
        rate = -jnp.exp(head_ref[1:2, :])
        d_step = col_total / step + rate * d_log
        raw_step = vr_ref[0, :, 2 * STATE : 3 * STATE] + head_ref[0:1, :]
        lanes = lax.broadcasted_iota(jnp.int32, (rows, HALF), 1)
        used = lanes < inner // HEAD_DIM
        d_raw_step = jnp.where(used, d_step * jax.nn.sigmoid(raw_step), 0.0)
        hg_ref[0:1, :] = jnp.sum(d_raw_step, axis=0, keepdims=True)
        hg_ref[1:2, :] = jnp.sum(jnp.where(used, d_log * step * rate, 0.0), axis=0, keepdims=True)
        hg_ref[2:8, :] = jnp.zeros((6, HALF), F32)
        dr = jnp.concatenate([d_raw, d_raw_step], axis=1).astype(BF16)
        dr_ref[0] = dr
        dn = dn_scr[...] + nt_dot(dr, wr_ref[...])
        u = u_ref[...].astype(F32)
        p = lax.rsqrt(jnp.mean(u * u, axis=1, keepdims=True) + EPS)
        e = dn * norm_ref[...]
        du = g_ref[...].astype(F32) + p * e - u * (p * p * p * jnp.mean(u * e, axis=1, keepdims=True))
        du_ref[...] = du.astype(BF16)
        ng_ref[0:1, :] = jnp.sum(u * p * dn, axis=0, keepdims=True)
        ng_ref[1:8, :] = jnp.zeros((7, width), F32)


def conv_back(dc, values, taps_ref, grad_ref):
    rows = lax.broadcasted_iota(jnp.int32, dc.shape, 0)
    count = dc.shape[0]
    grad_ref[4:5, :] = jnp.sum(dc, axis=0, keepdims=True)
    grad_ref[CONV - 1 : CONV, :] = jnp.sum(dc * values, axis=0, keepdims=True)
    total = taps_ref[CONV - 1 : CONV, :] * dc
    for ahead in range(1, CONV):
        moved = jnp.where(rows < count - ahead, pltpu.roll(dc, count - ahead, 0), 0.0)
        tap = CONV - 1 - ahead
        grad_ref[tap : tap + 1, :] = jnp.sum(moved * values, axis=0, keepdims=True)
        total = total + taps_ref[tap : tap + 1, :] * moved
    return total


def backward_slot(numbers, kept, grads, g, u, w_out, w_in, norm_gain, chan, chan_r, heads, slots):
    rows, width = g.shape
    inner = chan.shape[1]
    groups = inner // WIDE
    tail = w_in.shape[1] - 2 * inner
    z, v, c, y, v_r, c_r = kept
    early = lambda i: jnp.minimum(i, groups - 1)
    late = lambda i: jnp.maximum(i - groups, 0)
    cycle = lambda i: lax.rem(i, groups)
    whole = lambda a, b: pl.BlockSpec((a, b), lambda i, n: (0, 0))
    kept_whole = lambda b: pl.BlockSpec((1, rows, b), lambda i, n: (n[0], 0, 0))
    in_specs = [
        whole(rows, width),
        whole(rows, width),
        pl.BlockSpec((WIDE, width), lambda i, n: (early(i), 0)),
        pl.BlockSpec((width, WIDE), lambda i, n: (0, late(i))),
        pl.BlockSpec((width, WIDE), lambda i, n: (0, groups + late(i))),
        pl.BlockSpec((width, tail), lambda i, n: (0, 2 * inner // tail)),
        pl.BlockSpec((1, rows, WIDE), lambda i, n: (n[0], 0, cycle(i))),
        pl.BlockSpec((1, rows, WIDE), lambda i, n: (n[0], 0, late(i))),
        pl.BlockSpec((1, rows, WIDE), lambda i, n: (n[0], 0, late(i))),
        pl.BlockSpec((1, rows, WIDE), lambda i, n: (n[0], 0, cycle(i))),
        kept_whole(tail),
        kept_whole(2 * STATE),
        whole(1, width),
        pl.BlockSpec((8, WIDE), lambda i, n: (0, cycle(i))),
        whole(8, 2 * STATE),
        whole(8, HALF),
    ]
    args = [g, u, w_out, w_in, w_in, w_in, z, v, c, y, v_r, c_r, norm_gain, chan, chan_r, heads]
    aliases = {}
    if grads is not None:
        for k, arr in enumerate(grads):
            aliases[len(args) + 1] = k + 1
            args.append(arr)
            in_specs.append(pl.BlockSpec(memory_space=pl.ANY))
    out_shape = [
        jax.ShapeDtypeStruct((rows, width), BF16),
        jax.ShapeDtypeStruct((slots, rows, inner), BF16),
        jax.ShapeDtypeStruct((slots, rows, inner), BF16),
        jax.ShapeDtypeStruct((slots, rows, tail), BF16),
        jax.ShapeDtypeStruct((8, inner), F32),
        jax.ShapeDtypeStruct((8, 2 * STATE), F32),
        jax.ShapeDtypeStruct((8, width), F32),
        jax.ShapeDtypeStruct((8, HALF), F32),
    ]
    out_specs = [
        whole(rows, width),
        pl.BlockSpec((1, rows, WIDE), lambda i, n: (n[2], 0, late(i))),
        pl.BlockSpec((1, rows, WIDE), lambda i, n: (n[2], 0, late(i))),
        pl.BlockSpec((1, rows, tail), lambda i, n: (n[2], 0, 0)),
        pl.BlockSpec((8, WIDE), lambda i, n: (0, late(i))),
        whole(8, 2 * STATE),
        whole(8, width),
        whole(8, HALF),
    ]
    return pl.pallas_call(
        backward_kernel,
        grid_spec=pltpu.PrefetchScalarGridSpec(
            num_scalar_prefetch=1,
            grid=(2 * groups,),
            in_specs=in_specs,
            out_specs=out_specs,
            scratch_shapes=[
                pltpu.VMEM((rows, width), BF16),
                pltpu.VMEM((groups, rows, WIDE), F32),
                pltpu.VMEM((rows, 1), F32),
                pltpu.VMEM((rows, 1), F32),
                pltpu.VMEM((rows, rows), F32),
                pltpu.VMEM((rows, rows), F32),
                pltpu.VMEM((groups, rows, HALF), F32),
                pltpu.VMEM((HALF, rows), F32),
                pltpu.VMEM((groups, rows, HALF), F32),
                pltpu.VMEM((HALF, rows), F32),
                pltpu.VMEM((rows, HALF), F32),
                pltpu.VMEM((rows, 2 * STATE), F32),
                pltpu.VMEM((rows, width), F32),
            ],
        ),
        out_shape=out_shape,
        input_output_aliases=aliases,
        compiler_params=pltpu.CompilerParams(vmem_limit_bytes=VMEM),
        name="backward_slot",
    )(numbers, *args)


def pick(values, index, axis):
    return lax.dynamic_index_in_dim(values, index, axis, keepdims=False)


def swap(values, axis, bit):
    return lax.ppermute(values, axis, [(a, a ^ bit) for a in range(lax.axis_size(axis))])


def line_sum(blocks, axis, scale):
    count = lax.axis_size(axis)
    length = count // scale
    here = lax.axis_index(axis) // scale
    up = down = None
    for step in range(1, length):
        send_up = pick(blocks, jnp.clip(length - step + here, 0, length - 1), 0)
        send_down = pick(blocks, jnp.clip(here - (length - step), 0, length - 1), 0)
        if step > 1:
            send_up = (send_up.astype(F32) + up.astype(F32)).astype(BF16)
            send_down = (send_down.astype(F32) + down.astype(F32)).astype(BF16)
        up = lax.ppermute(send_up, axis, [(a, a + scale) for a in range(count - scale) if a // scale <= step - 1])
        down = lax.ppermute(
            send_down, axis, [(a, a - scale) for a in range(scale, count) if a // scale >= length - step]
        )
    own = pick(blocks, here, 0).astype(F32)
    return own if up is None else own + up.astype(F32) + down.astype(F32)


def tn_dot(a, b):
    return lax.dot_general(a, b, (((0,), (0,)), ((), ())), preferred_element_type=F32)


def by_partner(values, axis):
    count = lax.axis_size(axis)
    rows, total = values.shape
    split = values.reshape(rows, count // 4, 4, total // count)
    mine = lax.axis_index(axis) % 4
    return [pick(split, mine ^ delta, 2).reshape(rows, total // 4) for delta in range(4)]


def owned_sum(left, right, axis):
    count = lax.axis_size(axis)
    near = swap(tn_dot(jnp.concatenate([left[1], left[3]], axis=1), right).astype(BF16), axis, 1)
    half = near.shape[0] // 2
    far = swap((tn_dot(left[2], right) + near[half:].astype(F32)).astype(BF16), axis, 2)
    total = (tn_dot(left[0], right) + near[:half].astype(F32) + far.astype(F32)).astype(BF16)
    return line_sum(total.reshape(count // 4, -1, total.shape[1]), axis, 4)


def small_sums(scattered, common, axis):
    count = lax.axis_size(axis)
    place = lax.axis_index(axis)
    common = jnp.pad(common, (0, scattered.shape[1] - common.shape[0]))[None]
    bit = 1
    while bit < count:
        mine = (place // bit) % 2
        split = scattered.reshape(-1, 2, scattered.shape[1])
        sent = jnp.concatenate([pick(split, 1 - mine, 1), common], axis=0)
        came = swap(sent, axis, bit)
        scattered = pick(split, mine, 1) + came[:-1]
        common = common + came[-1:]
        bit *= 2
    return scattered[0], common[0]


def body(
    block_input,
    cotangent,
    lengths,
    in_weight,
    out_weight,
    conv_weight,
    conv_bias,
    norm_gain,
    gate_gain,
    dt_bias,
    a_log,
    skip_d,
):
    axis = "fsdp"
    count = lax.axis_size(axis)
    section = lax.axis_index("section")
    micro, rows, width = block_input.shape
    depth, proj_cols = in_weight.shape[1:]
    inner = gate_gain.shape[1] * count
    channels = conv_bias.shape[1] * count
    heads = dt_bias.shape[1]
    cols = -(-proj_cols // HALF) * HALF
    small = [a.reshape(-1) for a in (conv_weight[0], conv_bias[0], norm_gain[0], gate_gain[0])]
    sizes = [a.shape[0] for a in small]
    small_cols = -(-sum(sizes) // depth)
    packed = jnp.pad(jnp.concatenate(small), (0, small_cols * depth - sum(sizes))).reshape(depth, small_cols)
    packed = jnp.concatenate(
        [in_weight[0], packed, jnp.zeros((depth, cols - proj_cols - small_cols), BF16)], axis=1
    )
    w_in = lax.all_gather(packed, axis, axis=0, tiled=True)
    w_out = lax.all_gather(out_weight[0], axis, axis=0, tiled=True)
    flat = w_in[:, proj_cols : proj_cols + small_cols].reshape(count, depth * small_cols).astype(F32)
    cuts = [0]
    for size in sizes:
        cuts.append(cuts[-1] + size)
    taps = flat[:, cuts[0] : cuts[1]].reshape(count, CONV, -1).transpose(1, 0, 2).reshape(CONV, channels)
    bias = flat[:, cuts[1] : cuts[2]].reshape(1, channels)
    norm = flat[:, cuts[2] : cuts[3]].reshape(1, width)
    gate = flat[:, cuts[3] : cuts[4]].reshape(1, inner)
    skip = jnp.repeat(skip_d[0], HEAD_DIM)[None]
    chan = jnp.concatenate([taps[:, :inner], bias[:, :inner], gate, skip, jnp.zeros((1, inner), F32)], axis=0)
    chan_r = jnp.concatenate([taps[:, inner:], bias[:, inner:], jnp.zeros((3, channels - inner), F32)], axis=0)
    head_rows = jnp.pad(jnp.stack([dt_bias[0], a_log[0]]), ((0, 6), (0, HALF - heads)))
    places = jnp.arange(rows, dtype=jnp.int32)
    live = [(places < lengths[m, 0])[:, None] for m in range(micro)]

    kept = None

    def run_forward(kept, place, u):
        return forward_slot(place, kept, u, w_in, norm, chan, chan_r, head_rows, gate, 2 * micro)

    def finish(place, u, alive):
        branch = nn_dot(kept[1][place], w_out)
        return (u.astype(F32) + jnp.where(alive, branch, 0.0)).astype(BF16)

    for m in range(micro):
        kept = run_forward(kept, m, block_input[m])
    first = [finish(m, block_input[m], live[m]) for m in range(micro)]
    arrived = [lax.ppermute(h, "section", [(0, 1)]) for h in first]
    for m in range(micro):
        kept = run_forward(kept, micro + m, arrived[m])
    second = [finish(micro + m, arrived[m], live[m]) for m in range(micro)]
    outputs = jnp.stack([jnp.where(section == 0, a, b) for a, b in zip(first, second)])
    entered = [jnp.where(section == 0, block_input[m], arrived[m]) for m in range(micro)]

    is_last = section == 1
    returning = jnp.zeros((rows, width), BF16)
    grads = None
    gradients, incomings, small_terms = [], [], []
    for moment in range(micro + 1):
        position = micro - 1 - moment + (1 - section)
        active = (position >= 0) & (position < micro)
        slot = jnp.clip(position, 0, micro - 1)
        own = cotangent[micro - 1 - moment] if moment < micro else jnp.zeros((rows, width), BF16)
        incoming = jnp.where(is_last, own, returning)
        numbers = jnp.stack(
            [section * micro + slot, lengths[slot, 0], jnp.where(active, position, micro)]
        ).astype(jnp.int32)
        before, after = min(micro - 1, micro - moment), max(0, micro - 1 - moment)
        u = jnp.where(is_last, entered[after], entered[before])
        du, *rest = backward_slot(
            numbers, kept[2:], grads, incoming, u, w_out, w_in, norm, chan, chan_r, head_rows, micro + 1
        )
        grads, terms = rest[:3], rest[3:]
        gradients.append(du)
        incomings.append(incoming)
        small_terms.append(terms)
        if moment < micro:
            returning = lax.ppermute(du, "section", [(1, 0)])
    input_grads = jnp.stack(
        [jnp.where(is_last, gradients[micro - 1 - m], gradients[micro - m]) for m in range(micro)]
    )
    branch = [
        jnp.where(live[m], jnp.where(is_last, incomings[micro - 1 - m], incomings[micro - m]), jnp.zeros((), BF16))
        for m in range(micro)
    ]
    all_rows = micro * rows
    mine = lambda a: lax.dynamic_slice_in_dim(a, section * micro, micro, 0).reshape(all_rows, -1)
    left_out = by_partner(mine(kept[1]), axis)
    left_in = by_partner(mine(kept[0]), axis)
    out_grad = owned_sum(left_out, jnp.concatenate(branch, axis=0), axis)
    steady = lambda a: a[:micro].reshape(all_rows, -1)
    grad_z = owned_sum(left_in, steady(grads[0]), axis)
    grad_x = owned_sum(left_in, jnp.concatenate([steady(grads[1]), steady(grads[2])], axis=1), axis)
    in_grad = jnp.concatenate([grad_z, grad_x[:, : proj_cols - inner]], axis=1)

    chan_g, chan_rg, norm_g, head_g = [sum(t[k] for t in small_terms) for k in range(4)]
    taps_g = jnp.concatenate([chan_g[:CONV], chan_rg[:CONV]], axis=1)
    bias_g = jnp.concatenate([chan_g[CONV], chan_rg[CONV]])
    pieces = [
        taps_g.reshape(CONV, count, -1).transpose(1, 0, 2).reshape(count, -1),
        bias_g.reshape(count, -1),
        norm_g[0].reshape(count, -1),
        chan_g[5].reshape(count, -1),
    ]
    skip_g = chan_g[6].reshape(heads, HEAD_DIM).sum(axis=1)
    own_small, head_small = small_sums(
        jnp.concatenate(pieces, axis=1), jnp.concatenate([head_g[0, :heads], head_g[1, :heads], skip_g]), axis
    )
    parts = [own_small[a:b] for a, b in zip(cuts[:-1], cuts[1:])]
    return (
        outputs[None],
        input_grads[None],
        in_grad[None],
        out_grad[None],
        parts[0].reshape(1, CONV, -1),
        parts[1][None],
        parts[2][None],
        parts[3][None],
        head_small[None, :heads],
        head_small[None, heads : 2 * heads],
        head_small[None, 2 * heads : 3 * heads],
    )


def solution(mesh):
    in_specs = (
        P(None, "fsdp", None),
        P(None, "fsdp", None),
        P(None, "fsdp"),
        P("section", "fsdp", None),
        P("section", "fsdp", None),
        P("section", None, "fsdp"),
        P("section", "fsdp"),
        P("section", "fsdp"),
        P("section", "fsdp"),
        P("section", None),
        P("section", None),
        P("section", None),
    )
    out_specs = (
        P("section", None, "fsdp", None),
        P("section", None, "fsdp", None),
        P("section", "fsdp", None),
        P("section", "fsdp", None),
        P("section", None, "fsdp"),
        P("section", "fsdp"),
        P("section", "fsdp"),
        P("section", "fsdp"),
        P("section", None),
        P("section", None),
        P("section", None),
    )
    return jax.shard_map(body, mesh=mesh, in_specs=in_specs, out_specs=out_specs, check_vma=False)
```

```python
import functools

import jax
import jax.numpy as jnp
from jax import lax
from jax.experimental import pallas as pl
from jax.experimental.pallas import tpu as pltpu
from jax.sharding import PartitionSpec as P

HEAD_DIM = 64
STATE = 128
CONV = 4
EPS = 1e-05
LOG2E = 1.4426950408889634
HALF = 128
WIDE = 512
GROUP = WIDE // HEAD_DIM
TINY = 1e-30
NEG = -1e30
VMEM = 56 * 1024 * 1024
F32 = jnp.float32
BF16 = jnp.bfloat16
EXACT = lax.Precision.HIGHEST


def nt_dot(a, b):
    return lax.dot_general(a, b, (((1,), (1,)), ((), ())), preferred_element_type=F32)


def nn_dot(a, b):
    return jnp.dot(a, b, preferred_element_type=F32)


def sigmoid(v):
    return 0.5 * jnp.tanh(0.5 * v) + 0.5


def conv_rows(values, taps, bias):
    rows = lax.broadcasted_iota(jnp.int32, values.shape, 0)
    total = bias + taps[CONV - 1 : CONV, :] * values
    for back in range(1, CONV):
        moved = jnp.where(rows >= back, pltpu.roll(values, back, 0), 0.0)
        total = total + taps[CONV - 1 - back : CONV - back, :] * moved
    return total


def softplus(v):
    return jnp.maximum(v, 0.0) + jnp.log1p(jnp.exp(-jnp.abs(v)))


def step_terms(step_raw, head_ref):
    rows = step_raw.shape[0]
    step = jnp.maximum(softplus(step_raw + head_ref[0:1, :]), TINY)
    rate = -jnp.exp(head_ref[1:2, :])
    at = lax.broadcasted_iota(jnp.int32, (rows, rows), 0)
    of = lax.broadcasted_iota(jnp.int32, (rows, rows), 1)
    lower = (at >= of).astype(F32)
    sums = jnp.dot(lower, step * rate, precision=EXACT, preferred_element_type=F32) * LOG2E
    return step, rate, sums, sums - jnp.log2(step)


def spread(target, values, groups):
    for g in range(groups):
        target[g] = pltpu.roll(values, (HALF - g * GROUP) % HALF, 1) if g else values


def fold(block):
    return block[:, 0].reshape(-1, block.shape[-1])


def forward_kernel(
    at_ref, u_ref, ublk_ref, wo_ref, wz_ref, wx_ref, wb_ref, wc_ref, wt_ref, norm_ref, chan_ref, chanr_ref, head_ref, gate_ref, *rest
):
    (nb_ref, gb_ref, z_ref, v_ref, c_ref, y_ref, vr_ref, cr_ref, h_ref, w_scr, sq_scr, s_scr, col_scr, row_scr) = rest[-14:]
    step_at = pl.program_id(0)
    groups = w_scr.shape[0]
    rows = u_ref.shape[0]

    @pl.when(step_at == 0)
    def _():
        u = u_ref[...].astype(F32)
        scale = lax.rsqrt(jnp.mean(u * u, axis=1, keepdims=True) + EPS)
        nb_ref[0] = (u * scale * norm_ref[...]).astype(BF16)
        nb = nb_ref[0]
        raw = jnp.concatenate([nn_dot(nb, fold(wb_ref[...])), nn_dot(nb, fold(wc_ref[...]))], axis=1)
        steps = nn_dot(nb, fold(wt_ref[...]))
        vr_ref[0, :, : 2 * STATE] = raw
        vr_ref[0, :, 2 * STATE :] = steps
        pre = conv_rows(raw, chanr_ref[0:4, :], chanr_ref[4:5, :])
        cr_ref[0] = pre
        act = pre * sigmoid(pre)
        s_scr[...] = lax.dot_general(
            act[:, STATE:], act[:, :STATE], (((1,), (1,)), ((), ())), precision=EXACT, preferred_element_type=F32
        )
        _, _, sums, shifted = step_terms(steps, head_ref)
        spread(col_scr, sums, groups)
        row_scr[...] = shifted.T
        sq_scr[...] = jnp.zeros_like(sq_scr)

    @pl.when(step_at < groups)
    def _():
        nb = nb_ref[0]
        z = nn_dot(nb, fold(wz_ref[...]))
        z_ref[0] = z
        v = nn_dot(nb, fold(wx_ref[...]))
        v_ref[0] = v
        c = conv_rows(v, chan_ref[0:4, :], chan_ref[4:5, :])
        c_ref[0] = c
        x = c * sigmoid(c)
        x_low = x.astype(BF16)
        cols = col_scr[step_at]
        rws = row_scr[pl.ds(pl.multiple_of(step_at * GROUP, GROUP), GROUP), :]
        lane = lax.broadcasted_iota(jnp.int32, (HALF, HALF), 1)
        causal = lax.broadcasted_iota(jnp.int32, (HALF, HALF), 0) >= lane
        first = lane < HEAD_DIM
        parts = []
        for pair in range(GROUP // 2):
            here = slice(pair * HALF, (pair + 1) * HALF)
            pieces = []
            for tb in range(rows // HALF):
                t_here = slice(tb * HALF, (tb + 1) * HALF)
                both = []
                for h in (2 * pair, 2 * pair + 1):
                    col = cols[t_here, h : h + 1]
                    mix = []
                    for sb in range(tb + 1):
                        s_here = slice(sb * HALF, (sb + 1) * HALF)
                        gap = col - rws[h : h + 1, s_here]
                        if sb == tb:
                            gap = jnp.where(causal, gap, NEG)
                        mix.append((jnp.exp2(gap) * s_scr[t_here, s_here]).astype(BF16))
                    mix = jnp.concatenate(mix, axis=1) if len(mix) > 1 else mix[0]
                    both.append(nn_dot(mix, x_low[: (tb + 1) * HALF, here]))
                pieces.append(jnp.where(first, both[0], both[1]))
            parts.append(jnp.concatenate(pieces, axis=0))
        y = jnp.concatenate(parts, axis=1) + chan_ref[6:7, :] * x
        y_ref[0] = y
        w = y * (z * sigmoid(z))
        w_scr[step_at] = w
        sq_scr[...] += jnp.sum(w * w, axis=1, keepdims=True)

    @pl.when(step_at == groups - 1)
    def _():
        scale = lax.rsqrt(sq_scr[...] * (1.0 / (groups * WIDE)) + EPS)
        for g in range(groups):
            here = slice(g * WIDE, (g + 1) * WIDE)
            gb_ref[0, :, here] = (w_scr[g] * scale * gate_ref[:, here]).astype(BF16)

    @pl.when(step_at >= groups)
    def _():
        live = lax.broadcasted_iota(jnp.int32, (rows, 1), 0) < at_ref[0]
        branch = jnp.where(live, nn_dot(gb_ref[0], wo_ref[...]), 0.0)
        h_ref[...] = (ublk_ref[...].astype(F32) + branch).astype(BF16)


def in_specs_of(view, groups, late):
    parts, _, depth, _ = view.shape
    width = parts * depth
    start = width // WIDE
    small = (width + groups * WIDE) // HALF
    tall = lambda half, cols, at: pl.BlockSpec((parts, 1, depth, cols), lambda i, n: (0, half, 0, at(i)))
    return [
        tall(0, WIDE, lambda i: start + late(i)),
        tall(1, WIDE, lambda i: start + late(i)),
        tall(0, HALF, lambda i: small),
        tall(1, HALF, lambda i: small),
        tall(0, HALF, lambda i: small + 1),
    ]


def forward_slot(place, length, kept, u, w_all, view, norm_gain, chan, chan_r, heads, gate_gain, slots):
    rows, width = u.shape
    inner = chan.shape[1]
    groups = inner // WIDE
    shapes = [
        ((rows, width), BF16),
        ((rows, inner), BF16),
        ((rows, inner), F32),
        ((rows, inner), F32),
        ((rows, inner), F32),
        ((rows, inner), F32),
        ((rows, 3 * STATE), F32),
        ((rows, 2 * STATE), F32),
    ]
    early = lambda i: jnp.minimum(i, groups - 1)
    late = lambda i: jnp.maximum(i - groups, 0)
    wide_out = lambda: pl.BlockSpec((1, rows, WIDE), lambda i, n: (place, 0, early(i)))
    whole = lambda a, b: pl.BlockSpec((a, b), lambda i, n: (0, 0))
    whole_out = lambda b: pl.BlockSpec((1, rows, b), lambda i, n: (place, 0, 0))
    in_specs = [
        whole(rows, width),
        pl.BlockSpec((rows, WIDE), lambda i, n: (0, late(i))),
        pl.BlockSpec((inner, WIDE), lambda i, n: (0, late(i))),
        *in_specs_of(view, groups, early),
        whole(1, width),
        pl.BlockSpec((8, WIDE), lambda i, n: (0, early(i))),
        whole(8, 2 * STATE),
        whole(8, HALF),
        whole(1, inner),
    ]
    args = [u, u, w_all] + [view] * 5 + [norm_gain, chan, chan_r, heads, gate_gain]
    aliases = {}
    if kept is not None:
        for k, arr in enumerate(kept):
            aliases[len(args) + 1] = k
            args.append(arr)
            in_specs.append(pl.BlockSpec(memory_space=pl.ANY))
    out_specs = [whole_out(width), whole_out(inner)] + [wide_out() for _ in range(4)]
    out_specs += [whole_out(3 * STATE), whole_out(2 * STATE), pl.BlockSpec((rows, WIDE), lambda i, n: (0, late(i)))]
    out_shape = [jax.ShapeDtypeStruct((slots,) + s, d) for s, d in shapes]
    *kept, h = pl.pallas_call(
        forward_kernel,
        grid_spec=pltpu.PrefetchScalarGridSpec(
            num_scalar_prefetch=1,
            grid=(groups + width // WIDE,),
            in_specs=in_specs,
            out_specs=out_specs,
            scratch_shapes=[
                pltpu.VMEM((groups, rows, WIDE), F32),
                pltpu.VMEM((rows, 1), F32),
                pltpu.VMEM((rows, rows), F32),
                pltpu.VMEM((groups, rows, HALF), F32),
                pltpu.VMEM((HALF, rows), F32),
            ],
        ),
        out_shape=out_shape + [jax.ShapeDtypeStruct((rows, width), BF16)],
        input_output_aliases=aliases,
        compiler_params=pltpu.CompilerParams(vmem_limit_bytes=VMEM),
        cost_estimate=pl.CostEstimate(flops=22 * 10**9, bytes_accessed=60 * 10**6, transcendentals=0),
        name="forward_slot",
    )(length, *args)
    return kept, h


def backward_kernel(
    at_ref,
    g_ref,
    u_ref,
    wo_ref,
    wz_ref,
    wx_ref,
    wb_ref,
    wc_ref,
    wt_ref,
    z_ref,
    v_ref,
    c_ref,
    y_ref,
    vr_ref,
    cr_ref,
    norm_ref,
    chan_ref,
    chanr_ref,
    head_ref,
    past_ref,
    *rest,
):
    (
        du_ref, dz_ref, dv_ref, sum_ref,
        dob_scr, dgb_scr, sq_scr, we_scr, st_scr, ds_scr, bcol_scr, trow_scr, colr_scr, rowr_scr, step_scr, act_scr, dn_scr,
    ) = rest[-17:]
    groups = pl.num_programs(0) // 2
    at = pl.program_id(0)
    rows, width = g_ref.shape
    inner = dgb_scr.shape[0] * WIDE

    @pl.when(at == 0)
    def _():
        live = lax.broadcasted_iota(jnp.int32, (rows, 1), 0) < at_ref[1]
        dob_scr[...] = jnp.where(live, g_ref[...].astype(F32), 0.0).astype(BF16)
        sq_scr[...] = jnp.zeros_like(sq_scr)
        we_scr[...] = jnp.zeros_like(we_scr)
        ds_scr[...] = jnp.zeros_like(ds_scr)
        dn_scr[...] = jnp.zeros_like(dn_scr)
        rowr_scr[...] = jnp.zeros_like(rowr_scr)
        pre = cr_ref[0]
        act = pre * sigmoid(pre)
        act_scr[...] = act
        st_scr[...] = lax.dot_general(
            act[:, :STATE], act[:, STATE:], (((1,), (1,)), ((), ())), precision=EXACT, preferred_element_type=F32
        )
        step, rate, sums, shifted = step_terms(vr_ref[0, :, 2 * STATE : 3 * STATE], head_ref)
        step_scr[...] = step
        spread(bcol_scr, shifted, dgb_scr.shape[0])
        trow_scr[...] = sums.T

    @pl.when(at < groups)
    def _():
        dgb = nt_dot(dob_scr[...], wo_ref[...])
        dgb_scr[at] = dgb
        z = z_ref[0]
        w = y_ref[0] * (z * sigmoid(z))
        sq_scr[...] += jnp.sum(w * w, axis=1, keepdims=True)
        we_scr[...] += jnp.sum(w * (dgb * chan_ref[5:6, :]), axis=1, keepdims=True)

    @pl.when(at >= groups)
    def _():
        j = at - groups
        q = lax.rsqrt(sq_scr[...] * (1.0 / inner) + EPS)
        pull = q * q * q * (we_scr[...] * (1.0 / inner))
        dgb = dgb_scr[j]
        z = z_ref[0]
        y = y_ref[0]
        sz = sigmoid(z)
        silu_z = z * sz
        w = y * silu_z
        dw = q * (dgb * chan_ref[5:6, :]) - w * pull
        wide = pl.ds(pl.multiple_of(j * WIDE, WIDE), WIDE)
        sum_ref[5:6, wide] = past_ref[5:6, wide] + jnp.sum(w * q * dgb, axis=0, keepdims=True)
        dy = dw * silu_z
        dz = (dw * y * (sz * (1.0 + z * (1.0 - sz)))).astype(BF16)
        dz_ref[0] = dz
        dn = nt_dot(dz, fold(wz_ref[...]))

        c = c_ref[0]
        sc = sigmoid(c)
        x = c * sc
        x_low = x.astype(BF16)
        dy_low = dy.astype(BF16)
        sum_ref[6:7, wide] = past_ref[6:7, wide] + jnp.sum(dy * x, axis=0, keepdims=True)
        cols = bcol_scr[j]
        head_rows = pl.ds(pl.multiple_of(j * GROUP, GROUP), GROUP)
        rws = trow_scr[head_rows, :]
        lane = lax.broadcasted_iota(jnp.int32, (HALF, HALF), 1)
        causal = lane >= lax.broadcasted_iota(jnp.int32, (HALF, HALF), 0)
        first = lane < HEAD_DIM
        lane_row = lax.broadcasted_iota(jnp.int32, (1, HALF), 1)
        sub = lax.broadcasted_iota(jnp.int32, (GROUP, HALF), 0)
        blocks = rows // HALF
        col_sums = [jnp.zeros((HALF, HALF), F32) for _ in range(blocks)]
        row_sums = [jnp.zeros((GROUP, HALF), F32) for _ in range(blocks)]
        parts = []
        for pair in range(GROUP // 2):
            here = slice(pair * HALF, (pair + 1) * HALF)
            pieces = []
            row_part = [[None] * blocks, [None] * blocks]
            for sb in range(blocks):
                s_here = slice(sb * HALF, (sb + 1) * HALF)
                x_here = x_low[s_here, here]
                split = (
                    jnp.where(first, x_here, jnp.zeros_like(x_here)),
                    jnp.where(first, jnp.zeros_like(x_here), x_here),
                )
                mixes = [[], []]
                lane_sum = [None, None]
                for tb in range(sb, blocks):
                    t_here = slice(tb * HALF, (tb + 1) * HALF)
                    dy_here = dy_low[t_here, here]
                    contact = st_scr[s_here, t_here]
                    touched = None
                    for k in range(2):
                        h = 2 * pair + k
                        gap = rws[h : h + 1, t_here] - cols[s_here, h : h + 1]
                        if sb == tb:
                            gap = jnp.where(causal, gap, NEG)
                        decay = jnp.exp2(gap)
                        mix = decay * contact
                        meet = nt_dot(split[k], dy_here)
                        through = decay * meet
                        pairs = through * contact
                        touched = through if touched is None else touched + through
                        mixes[k].append(mix.astype(BF16))
                        lane_sum[k] = pairs if lane_sum[k] is None else lane_sum[k] + pairs
                        down = jnp.sum(pairs, axis=0, keepdims=True)
                        row_part[k][tb] = down if row_part[k][tb] is None else row_part[k][tb] + down
                    ds_scr[s_here, t_here] += touched
                out = []
                for k in range(2):
                    h = 2 * pair + k
                    mix = jnp.concatenate(mixes[k], axis=1) if len(mixes[k]) > 1 else mixes[k][0]
                    out.append(nn_dot(mix, dy_low[sb * HALF :, here]))
                    total = jnp.sum(lane_sum[k], axis=1, keepdims=True)
                    col_sums[sb] = jnp.where(lane_row == h, total, col_sums[sb])
                pieces.append(jnp.where(first, out[0], out[1]))
            for k in range(2):
                for tb in range(blocks):
                    row_sums[tb] = jnp.where(sub == 2 * pair + k, row_part[k][tb], row_sums[tb])
            parts.append(jnp.concatenate(pieces, axis=0))
        colr_scr[j] = jnp.concatenate(col_sums, axis=0)
        rowr_scr[head_rows, :] = jnp.concatenate(row_sums, axis=1)
        dx = jnp.concatenate(parts, axis=1) + chan_ref[6:7, :] * dy
        dc = dx * (sc * (1.0 + c * (1.0 - sc)))
        dv = conv_back(dc, v_ref[0], chan_ref, past_ref, sum_ref, wide).astype(BF16)
        dv_ref[0, :, wide] = dv
        dn_scr[...] += dn + nt_dot(dv, fold(wx_ref[...]))

    @pl.when(at == 2 * groups - 1)
    def _():
        act = act_scr[...]
        ds = ds_scr[...].astype(BF16)
        act_low = act.astype(BF16)
        d_b = nn_dot(ds, act_low[:, STATE:])
        d_c = lax.dot_general(ds, act_low[:, :STATE], (((0,), (0,)), ((), ())), preferred_element_type=F32)
        pre = cr_ref[0]
        sp = sigmoid(pre)
        d_pre = jnp.concatenate([d_b, d_c], axis=1) * (sp * (1.0 + pre * (1.0 - sp)))
        narrow = slice(inner, inner + 2 * STATE)
        d_raw = conv_back(d_pre, vr_ref[0, :, : 2 * STATE], chanr_ref, past_ref, sum_ref, narrow)
        sum_ref[5:7, narrow] = jnp.zeros((2, 2 * STATE), F32)
        col_total = colr_scr[0]
        for g in range(1, colr_scr.shape[0]):
            col_total = col_total + pltpu.roll(colr_scr[g], g * GROUP, 1)
        d_sums = rowr_scr[...].T - col_total
        at_row = lax.broadcasted_iota(jnp.int32, (rows, rows), 0)
        of_row = lax.broadcasted_iota(jnp.int32, (rows, rows), 1)
        upper = (of_row >= at_row).astype(F32)
        d_log = jnp.dot(upper, d_sums, precision=EXACT, preferred_element_type=F32)
        step = step_scr[...]
        rate = -jnp.exp(head_ref[1:2, :])
        d_step = col_total / step + rate * d_log
        raw_step = vr_ref[0, :, 2 * STATE : 3 * STATE] + head_ref[0:1, :]
        lanes = lax.broadcasted_iota(jnp.int32, (rows, HALF), 1)
        used = lanes < inner // HEAD_DIM
        d_raw_step = jnp.where(used, d_step * jax.nn.sigmoid(raw_step), 0.0)
        last = past_ref[7:8, :]
        sum_ref[7:8, width : width + HALF] = last[:, width : width + HALF] + jnp.sum(d_raw_step, axis=0, keepdims=True)
        sum_ref[7:8, width + HALF : width + 2 * HALF] = last[:, width + HALF : width + 2 * HALF] + jnp.sum(
            jnp.where(used, d_log * step * rate, 0.0), axis=0, keepdims=True
        )
        sum_ref[7:8, width + 2 * HALF :] = jnp.zeros((1, inner - width), F32)
        dr = jnp.concatenate([d_raw, d_raw_step], axis=1).astype(BF16)
        dv_ref[0, :, inner:] = dr
        dn = dn_scr[...] + nt_dot(dr[:, :STATE], fold(wb_ref[...]))
        dn = dn + nt_dot(dr[:, STATE : 2 * STATE], fold(wc_ref[...])) + nt_dot(dr[:, 2 * STATE :], fold(wt_ref[...]))
        u = u_ref[...].astype(F32)
        p = lax.rsqrt(jnp.mean(u * u, axis=1, keepdims=True) + EPS)
        e = dn * norm_ref[...]
        du = g_ref[...].astype(F32) + p * e - u * (p * p * p * jnp.mean(u * e, axis=1, keepdims=True))
        du_ref[...] = du.astype(BF16)
        sum_ref[7:8, :width] = last[:, :width] + jnp.sum(u * p * dn, axis=0, keepdims=True)


def conv_back(dc, values, taps_ref, past_ref, sum_ref, here):
    rows = lax.broadcasted_iota(jnp.int32, dc.shape, 0)
    count = dc.shape[0]
    sum_ref[4:5, here] = past_ref[4:5, here] + jnp.sum(dc, axis=0, keepdims=True)
    total = 0.0
    for ahead in range(CONV):
        moved = jnp.where(rows < count - ahead, pltpu.roll(dc, count - ahead, 0), 0.0) if ahead else dc
        tap = CONV - 1 - ahead
        sum_ref[tap : tap + 1, here] = past_ref[tap : tap + 1, here] + jnp.sum(moved * values, axis=0, keepdims=True)
        total = total + taps_ref[tap : tap + 1, :] * moved
    return total


def backward_slot(numbers, kept, grads, past, g, u, w_all, view, norm_gain, chan, chan_r, heads, slots):
    rows, width = g.shape
    inner = chan.shape[1]
    groups = inner // WIDE
    tail = 3 * STATE
    z, v, c, y, v_r, c_r = kept
    early = lambda i: jnp.minimum(i, groups - 1)
    late = lambda i: jnp.maximum(i - groups, 0)
    cycle = lambda i: lax.rem(i, groups)
    whole = lambda a, b: pl.BlockSpec((a, b), lambda i, n: (0, 0))
    kept_whole = lambda b: pl.BlockSpec((1, rows, b), lambda i, n: (n[0], 0, 0))
    in_specs = [
        whole(rows, width),
        whole(rows, width),
        pl.BlockSpec((WIDE, width), lambda i, n: (early(i), 0)),
        *in_specs_of(view, groups, late),
        pl.BlockSpec((1, rows, WIDE), lambda i, n: (n[0], 0, cycle(i))),
        pl.BlockSpec((1, rows, WIDE), lambda i, n: (n[0], 0, late(i))),
        pl.BlockSpec((1, rows, WIDE), lambda i, n: (n[0], 0, late(i))),
        pl.BlockSpec((1, rows, WIDE), lambda i, n: (n[0], 0, cycle(i))),
        kept_whole(tail),
        kept_whole(2 * STATE),
        whole(1, width),
        pl.BlockSpec((8, WIDE), lambda i, n: (0, cycle(i))),
        whole(8, 2 * STATE),
        whole(8, HALF),
        whole(8, inner + 2 * STATE),
    ]
    args = [g, u, w_all] + [view] * 5 + [z, v, c, y, v_r, c_r, norm_gain, chan, chan_r, heads, past]
    aliases = {}
    if grads is not None:
        for k, arr in enumerate(grads):
            aliases[len(args) + 1] = k + 1
            args.append(arr)
            in_specs.append(pl.BlockSpec(memory_space=pl.ANY))
    out_shape = [
        jax.ShapeDtypeStruct((rows, width), BF16),
        jax.ShapeDtypeStruct((slots, rows, inner), BF16),
        jax.ShapeDtypeStruct((slots, rows, inner + tail), BF16),
        jax.ShapeDtypeStruct((8, inner + 2 * STATE), F32),
    ]
    out_specs = [
        whole(rows, width),
        pl.BlockSpec((1, rows, WIDE), lambda i, n: (n[2], 0, late(i))),
        pl.BlockSpec((1, rows, inner + tail), lambda i, n: (n[2], 0, 0)),
        whole(8, inner + 2 * STATE),
    ]
    return pl.pallas_call(
        backward_kernel,
        grid_spec=pltpu.PrefetchScalarGridSpec(
            num_scalar_prefetch=1,
            grid=(2 * groups,),
            in_specs=in_specs,
            out_specs=out_specs,
            scratch_shapes=[
                pltpu.VMEM((rows, width), BF16),
                pltpu.VMEM((groups, rows, WIDE), F32),
                pltpu.VMEM((rows, 1), F32),
                pltpu.VMEM((rows, 1), F32),
                pltpu.VMEM((rows, rows), F32),
                pltpu.VMEM((rows, rows), F32),
                pltpu.VMEM((groups, rows, HALF), F32),
                pltpu.VMEM((HALF, rows), F32),
                pltpu.VMEM((groups, rows, HALF), F32),
                pltpu.VMEM((HALF, rows), F32),
                pltpu.VMEM((rows, HALF), F32),
                pltpu.VMEM((rows, 2 * STATE), F32),
                pltpu.VMEM((rows, width), F32),
            ],
        ),
        out_shape=out_shape,
        input_output_aliases=aliases,
        compiler_params=pltpu.CompilerParams(vmem_limit_bytes=VMEM),
        cost_estimate=pl.CostEstimate(flops=10**9, bytes_accessed=10**6, transcendentals=0),
        name="backward_slot",
    )(numbers, *args)


def pack_kernel(inner, in_ref, out_ref, packed_ref):
    depth, width = in_ref.shape[0], out_ref.shape[1]
    mid, end = 2 * inner + 2 * STATE, in_ref.shape[1]
    packed_ref[:, :width] = out_ref[...]
    tail = width + inner
    for half in range(2):
        rows = slice(half * depth, (half + 1) * depth)
        packed_ref[rows, width:tail] = in_ref[:, half * inner : (half + 1) * inner]
        packed_ref[rows, tail : tail + STATE] = in_ref[:, mid - 2 * STATE + half * STATE : mid - STATE + half * STATE]
        packed_ref[rows, tail + STATE :] = jnp.zeros((depth, STATE), BF16)
    packed_ref[:depth, tail + STATE : tail + STATE + end - mid] = in_ref[:, mid:]


def pack(in_shard, out_shard, inner):
    depth, width = in_shard.shape[0], out_shard.shape[1]
    return pl.pallas_call(
        functools.partial(pack_kernel, inner),
        out_shape=jax.ShapeDtypeStruct((2 * depth, width + inner + 2 * STATE), BF16),
        name="pack",
    )(in_shard, out_shard)


def order_kernel(at_ref, a_ref, own_ref, other_ref, turn_scr):
    turn_scr[...] = a_ref[0].astype(F32).T.reshape(turn_scr.shape)
    for part in range(2):
        for line in range(own_ref.shape[2]):
            own_ref[part, 0, line] = turn_scr[4 * line + at_ref[1 + 2 * part]].astype(BF16)
            other_ref[part, 0, line] = turn_scr[4 * line + at_ref[2 + 2 * part]].astype(BF16)


def by_owner(numbers, values, micro, count):
    _, rows, total = values.shape
    depth = total // count
    line = count // 4
    out = pl.BlockSpec((2, 1, line, depth, rows), lambda i, n: (0, i, 0, 0, 0))
    made = jax.ShapeDtypeStruct((2, micro, line, depth, rows), BF16)
    own, other = pl.pallas_call(
        order_kernel,
        grid_spec=pltpu.PrefetchScalarGridSpec(
            num_scalar_prefetch=1,
            grid=(micro,),
            in_specs=[pl.BlockSpec((1, rows, total), lambda i, n: (n[0] + i, 0, 0))],
            out_specs=[out, out],
            scratch_shapes=[pltpu.VMEM((count, depth, rows), F32)],
        ),
        out_shape=[made, made],
        compiler_params=pltpu.CompilerParams(vmem_limit_bytes=VMEM),
        cost_estimate=pl.CostEstimate(flops=3 * 10**9, bytes_accessed=2 * 10**6, transcendentals=0),
        name="by_owner",
    )(numbers, values)
    flat = (2, micro, line * depth, rows)
    return own.reshape(flat), other.reshape(flat)


def outer_kernel(own_ref, sib_ref, right_ref, first_ref, later_ref, keep_ref, send_ref):
    micro = own_ref.shape[1]
    for part, out_ref in ((0, keep_ref), (1, send_ref)):
        total = None
        for m in range(micro):
            term = nn_dot(own_ref[part, m], right_ref[m])
            term = term + nn_dot(sib_ref[part, m], first_ref[...] if m == 0 else later_ref[m - 1])
            total = term if total is None else total + term
        out_ref[...] = total.astype(BF16)


def outer_sum(own, sib, right, first, later, start, stop, block):
    _, micro, high, rows = own.shape
    low, steps = start // block, (stop - start) // block
    full = pl.BlockSpec(own.shape, lambda i: (0, 0, 0, 0))
    out = pl.BlockSpec((high, block), lambda i: (0, i))
    made = jax.ShapeDtypeStruct((high, stop - start), BF16)
    return pl.pallas_call(
        outer_kernel,
        grid=(steps,),
        in_specs=[
            full,
            full,
            pl.BlockSpec((micro, rows, block), lambda i: (0, 0, low + i)),
            pl.BlockSpec((rows, block), lambda i: (0, low + i)),
            pl.BlockSpec((micro - 1, rows, block), lambda i: (0, 0, low + i)),
        ],
        out_specs=[out, out],
        out_shape=[made, made],
        compiler_params=pltpu.CompilerParams(vmem_limit_bytes=VMEM),
        cost_estimate=pl.CostEstimate(flops=10**9, bytes_accessed=10**6, transcendentals=0),
        name="outer_sum",
    )(own, sib, right, first, later)


def pick(values, index, axis):
    return lax.dynamic_index_in_dim(values, index, axis, keepdims=False)


def swap(values, axis, bit):
    return lax.ppermute(values, axis, [(a, a ^ bit) for a in range(lax.axis_size(axis))])


def all_rows_of(row, axis):
    count = lax.axis_size(axis)
    place = lax.axis_index(axis)
    table = jnp.where(jnp.arange(count, dtype=jnp.int32)[:, None] == place, row[None], jnp.zeros((), row.dtype))
    bit = 1
    while bit < count:
        table = table + swap(table, axis, bit)
        bit *= 2
    return table


def owned_sums(chunks, axis):
    count = lax.axis_size(axis)
    length = count // 4
    results, token = [], None
    for keep, far, eager in chunks:
        if token is not None:
            far, _ = lax.optimization_barrier((far, token))
        terms = [a.reshape(length, -1, a.shape[1]) for a in (keep, far)]
        bit = 1
        while bit < length:
            mine = (lax.axis_index(axis) // (4 * bit)) % 2
            half = lambda a, which: pick(a.reshape((-1, 2) + a.shape[1:]), which, 1)
            sent = sum(half(a, 1 - mine).astype(F32) for a in terms).astype(BF16)
            came = swap(sent, axis, 4 * bit)
            terms = [half(a, mine) for a in terms] + [came]
            if bit == 1 or not eager:
                token = sent
            bit *= 2
        results.append(sum(a[0].astype(F32) for a in terms))
    return results


def all_sum(values, axis):
    bit = 1
    while bit < lax.axis_size(axis):
        values = values + swap(values, axis, bit)
        bit *= 2
    return values


def body(
    block_input,
    cotangent,
    lengths,
    in_weight,
    out_weight,
    conv_weight,
    conv_bias,
    norm_gain,
    gate_gain,
    dt_bias,
    a_log,
    skip_d,
):
    axis = "fsdp"
    count = lax.axis_size(axis)
    section = lax.axis_index("section")
    micro, rows, width = block_input.shape
    depth, proj_cols = in_weight.shape[1:]
    inner = gate_gain.shape[1] * count
    channels = conv_bias.shape[1] * count
    heads = dt_bias.shape[1]
    small = [a.reshape(-1) for a in (conv_weight[0], conv_bias[0], norm_gain[0], gate_gain[0])]
    sizes = [a.shape[0] for a in small]
    w_all = lax.all_gather(pack(in_weight[0], out_weight[0], inner), axis, axis=0, tiled=True)
    view = w_all.reshape(count, 2, depth, -1)
    if depth % 16:
        view = view.transpose(1, 0, 2, 3).reshape(1, 2, width, -1)
    flat = all_rows_of(jnp.concatenate(small), axis).astype(F32)
    cuts = [0]
    for size in sizes:
        cuts.append(cuts[-1] + size)
    taps = flat[:, cuts[0] : cuts[1]].reshape(count, CONV, -1).transpose(1, 0, 2).reshape(CONV, channels)
    bias = flat[:, cuts[1] : cuts[2]].reshape(1, channels)
    norm = flat[:, cuts[2] : cuts[3]].reshape(1, width)
    gate = flat[:, cuts[3] : cuts[4]].reshape(1, inner)
    skip = jnp.repeat(skip_d[0], HEAD_DIM)[None]
    chan = jnp.concatenate([taps[:, :inner], bias[:, :inner], gate, skip, jnp.zeros((1, inner), F32)], axis=0)
    chan_r = jnp.concatenate([taps[:, inner:], bias[:, inner:], jnp.zeros((3, channels - inner), F32)], axis=0)
    head_rows = jnp.pad(jnp.stack([dt_bias[0], a_log[0]]), ((0, 6), (0, HALF - heads)))
    places = jnp.arange(rows, dtype=jnp.int32)
    live = [(places < lengths[m, 0])[:, None] for m in range(micro)]

    kept = None

    def run_forward(kept, place, m, u):
        return forward_slot(
            place, lengths[m], kept, u, w_all, view, norm, chan, chan_r, head_rows, gate, 2 * micro
        )

    first, second = [], []
    for m in range(micro):
        kept, h = run_forward(kept, m, m, block_input[m])
        first.append(h)
    arrived = [lax.ppermute(h, "section", [(0, 1)]) for h in first]
    for m in range(micro):
        kept, h = run_forward(kept, micro + m, m, arrived[m])
        second.append(h)
    outputs = jnp.stack([jnp.where(section == 0, a, b) for a, b in zip(first, second)])
    arrived, second = lax.optimization_barrier((arrived, second))
    entered = [jnp.where(section == 0, block_input[m], arrived[m]) for m in range(micro)]

    is_last = section == 1
    returning = jnp.zeros((rows, width), BF16)
    grads = None
    gradients, branch = [], [None] * micro
    sums = jnp.zeros((8, inner + 2 * STATE), F32)
    mine = (lax.axis_index(axis) % 4).astype(jnp.int32)
    owners = jnp.stack([section * micro, mine, mine ^ 1, mine ^ 2, mine ^ 3]).astype(jnp.int32)
    for moment in range(micro + 1):
        position = micro - 1 - moment + (1 - section)
        active = (position >= 0) & (position < micro)
        slot = jnp.clip(position, 0, micro - 1)
        own = cotangent[micro - 1 - moment] if moment < micro else jnp.zeros((rows, width), BF16)
        incoming = jnp.where(is_last, own, returning)
        if moment > 0:
            m = micro - moment
            branch[m] = jnp.where(live[m], jnp.where(is_last, cotangent[m], returning), jnp.zeros((), BF16))
        if moment == micro:
            branch_sib = swap(branch[0], axis, 1)
            out_pairs = []
            for a, b in ((0, width - WIDE), (width - WIDE, width)):
                out_pairs.append(outer_sum(out_own, out_sib, jnp.stack(branch), branch_sib, branch_later, a, b, WIDE))
                branch_sib, out_pairs = lax.optimization_barrier((branch_sib, out_pairs))
            incoming, out_pairs = lax.optimization_barrier((incoming, out_pairs))
            out_fars = [swap(send, axis, 2) for _, send in out_pairs]
        numbers = jnp.stack(
            [section * micro + slot, lengths[slot, 0], jnp.where(active, position, micro)]
        ).astype(jnp.int32)
        before, after = min(micro - 1, micro - moment), max(0, micro - 1 - moment)
        u = jnp.where(is_last, entered[after], entered[before])
        du, *grads, sums = backward_slot(
            numbers, kept[2:], grads, sums, incoming, u, w_all, view, norm, chan, chan_r, head_rows, micro + 1
        )
        gradients.append(du)
        if moment < micro:
            returning = lax.ppermute(du, "section", [(1, 0)])
        if moment == micro - 1:
            nb, gb, _ = lax.optimization_barrier((kept[0], kept[1], du))
            out_own, out_other = by_owner(owners, gb, micro, count)
            in_own, in_other = by_owner(owners, nb, micro, count)
            ready = (out_other, in_other, jnp.stack(branch[1:]), grads[0][1:micro], grads[1][1:micro])
            returning, ready, out_own, in_own = lax.optimization_barrier((returning, ready, out_own, in_own))
            out_sib, in_sib, branch_later, z_later, v_later = (swap(a, axis, 1) for a in ready)
    input_grads = jnp.stack(
        [jnp.where(is_last, gradients[micro - 1 - m], gradients[micro - m]) for m in range(micro)]
    )
    firsts, out_fars[0] = lax.optimization_barrier(([a[0] for a in grads], out_fars[0]))
    z_first, v_first = (swap(a, axis, 1) for a in firsts)
    cut, end = 5 * 384, inner + 3 * STATE
    keeps, sends = zip(
        outer_sum(in_own, in_sib, grads[0], z_first, z_later, 0, inner, WIDE),
        outer_sum(in_own, in_sib, grads[1], v_first, v_later, 0, cut, 640),
        outer_sum(in_own, in_sib, grads[1], v_first, v_later, cut, end, 384),
    )
    sums, _ = lax.optimization_barrier((sums, sends[-1]))
    fars = out_fars + [swap(a, axis, 2) for a in sends]
    keeps = [keep for keep, _ in out_pairs] + list(keeps)
    parts = owned_sums(list(zip(keeps, fars, [False, False, True, True, True])), axis)
    out_grad, in_parts = jnp.concatenate(parts[:2], axis=1), parts[2:]
    in_grad = jnp.concatenate(in_parts, axis=1)[:, :proj_cols]

    sums = all_sum(sums, axis)
    place = lax.axis_index(axis)
    cut_out = lambda row, size: lax.dynamic_slice(sums, (row, place * size), (1, size))
    taps_g = lax.dynamic_slice(sums, (0, place * (channels // count)), (CONV, channels // count))
    skip_g = sums[6, :inner].reshape(heads, HEAD_DIM).sum(axis=1)
    return (
        outputs[None],
        input_grads[None],
        in_grad[None],
        out_grad[None],
        taps_g[None],
        cut_out(4, channels // count),
        cut_out(7, width // count),
        cut_out(5, inner // count),
        sums[7:8, width : width + heads],
        sums[7:8, width + HALF : width + HALF + heads],
        skip_g[None],
    )


def solution(mesh):
    in_specs = (
        P(None, "fsdp", None),
        P(None, "fsdp", None),
        P(None, "fsdp"),
        P("section", "fsdp", None),
        P("section", "fsdp", None),
        P("section", None, "fsdp"),
        P("section", "fsdp"),
        P("section", "fsdp"),
        P("section", "fsdp"),
        P("section", None),
        P("section", None),
        P("section", None),
    )
    out_specs = (
        P("section", None, "fsdp", None),
        P("section", None, "fsdp", None),
        P("section", "fsdp", None),
        P("section", "fsdp", None),
        P("section", None, "fsdp"),
        P("section", "fsdp"),
        P("section", "fsdp"),
        P("section", "fsdp"),
        P("section", None),
        P("section", None),
        P("section", None),
    )
    return jax.shard_map(body, mesh=mesh, in_specs=in_specs, out_specs=out_specs, check_vma=False)
```

```python
import functools

import jax
import jax.numpy as jnp
from jax import lax
from jax.experimental import pallas as pl
from jax.experimental.pallas import tpu as pltpu
from jax.sharding import PartitionSpec as P

HEAD_DIM = 64
STATE = 128
CONV = 4
EPS = 1e-05
LOG2E = 1.4426950408889634
HALF = 128
WIDE = 512
GROUP = WIDE // HEAD_DIM
TINY = 1e-30
NEG = -1e30
VMEM = 60 * 1024 * 1024
F32 = jnp.float32
BF16 = jnp.bfloat16
EXACT = lax.Precision.HIGHEST


def nt_dot(a, b):
    return lax.dot_general(a, b, (((1,), (1,)), ((), ())), preferred_element_type=F32)


def nn_dot(a, b):
    return jnp.dot(a, b, preferred_element_type=F32)


def sigmoid(v):
    return 0.5 * jnp.tanh(0.5 * v) + 0.5


def conv_rows(values, taps, bias):
    rows = lax.broadcasted_iota(jnp.int32, values.shape, 0)
    total = bias + taps[CONV - 1 : CONV, :] * values
    for back in range(1, CONV):
        moved = jnp.where(rows >= back, pltpu.roll(values, back, 0), 0.0)
        total = total + taps[CONV - 1 - back : CONV - back, :] * moved
    return total


def softplus(v):
    return jnp.maximum(v, 0.0) + jnp.log1p(jnp.exp(-jnp.abs(v)))


def step_terms(step_raw, head_ref):
    rows = step_raw.shape[0]
    step = jnp.maximum(softplus(step_raw + head_ref[0:1, :]), TINY)
    rate = -jnp.exp(head_ref[1:2, :])
    at = lax.broadcasted_iota(jnp.int32, (rows, rows), 0)
    of = lax.broadcasted_iota(jnp.int32, (rows, rows), 1)
    lower = (at >= of).astype(F32)
    sums = jnp.dot(lower, step * rate, precision=EXACT, preferred_element_type=F32) * LOG2E
    return step, rate, sums, sums - jnp.log2(step)


def spread(target, values, groups):
    for g in range(groups):
        target[g] = pltpu.roll(values, (HALF - g * GROUP) % HALF, 1) if g else values


def fold(block):
    return block.reshape(-1, block.shape[-1])


def lanes(index):
    return pl.ds(pl.multiple_of(index * WIDE, WIDE), WIDE)


def in_copies(view_ref, wz_scr, wx_scr, wr_scr, sem, base):
    parts, _, depth, _ = view_ref.shape
    width, groups = parts * depth, wz_scr.shape[0]
    tail = width + groups * WIDE

    def of_group(j):
        here = pl.ds(pl.multiple_of(width + j * WIDE, WIDE), WIDE)
        return [
            pltpu.make_async_copy(view_ref.at[:, 0, :, here], wz_scr.at[j], sem.at[base + j]),
            pltpu.make_async_copy(view_ref.at[:, 1, :, here], wx_scr.at[j], sem.at[base + groups + j]),
        ]

    def of_rest():
        return [
            pltpu.make_async_copy(view_ref.at[:, half, :, pl.ds(at, HALF)], wr_scr.at[k], sem.at[base + 2 * groups + k])
            for k, (half, at) in enumerate(((0, tail), (1, tail), (0, tail + HALF)))
        ]

    return of_group, of_rest


def start_all(copies):
    for copy in copies:
        copy.start()


def wait_all(copies):
    for copy in copies:
        copy.wait()


def forward_kernel(place, at_ref, u_hbm, w_hbm, view_hbm, norm_ref, chan_ref, chanr_ref, head_ref, gate_ref, *rest):
    (
        nb_hbm, gb_hbm, z_hbm, v_hbm, y_hbm, vr_hbm, cr_hbm, h_hbm,
        u_scr, wz_scr, wx_scr, wr_scr, wo_scr, nb_scr, gb_scr, z_scr, v_scr, y_scr, vr_scr, cr_scr, h_scr,
        w_scr, sq_scr, s_scr, col_scr, row_scr, sem, out_sem,
    ) = rest[-28:]
    groups, rows, _ = w_scr.shape
    of_group, of_rest = in_copies(view_hbm, wz_scr, wx_scr, wr_scr, sem, 1)
    spare = 2 * groups + 4
    u_copy = pltpu.make_async_copy(u_hbm, u_scr, sem.at[0])

    def of_out(k):
        return pltpu.make_async_copy(w_hbm.at[:, lanes(k)], wo_scr.at[k], sem.at[spare + k])

    def kept_copies(j):
        return [
            pltpu.make_async_copy(scr.at[j], hbm.at[place, :, lanes(j)], out_sem.at[k * groups + j])
            for k, (scr, hbm) in enumerate(((z_scr, z_hbm), (v_scr, v_hbm), (y_scr, y_hbm)))
        ]

    last = 3 * groups
    whole_copies = [
        pltpu.make_async_copy(scr, hbm.at[place], out_sem.at[last + k])
        for k, (scr, hbm) in enumerate(((nb_scr, nb_hbm), (gb_scr, gb_hbm), (vr_scr, vr_hbm), (cr_scr, cr_hbm)))
    ]
    h_copy = pltpu.make_async_copy(h_scr, h_hbm, out_sem.at[last + 4])

    @pl.when(at_ref[1] == 1)
    def _():
        u_copy.start()
        start_all(of_rest())
        for j in range(groups):
            start_all(of_group(j))
        for k in range(wo_scr.shape[0]):
            of_out(k).start()

        u_copy.wait()
        u = u_scr[...].astype(F32)
        scale = lax.rsqrt(jnp.mean(u * u, axis=1, keepdims=True) + EPS)
        nb_scr[...] = (u * scale * norm_ref[...]).astype(BF16)
        nb = nb_scr[...]
        wait_all(of_rest())
        raw = jnp.concatenate([nn_dot(nb, fold(wr_scr[0])), nn_dot(nb, fold(wr_scr[1]))], axis=1)
        steps = nn_dot(nb, fold(wr_scr[2]))
        vr_scr[:, : 2 * STATE] = raw
        vr_scr[:, 2 * STATE :] = steps
        pre = conv_rows(raw, chanr_ref[0:4, :], chanr_ref[4:5, :])
        cr_scr[...] = pre
        act = pre * sigmoid(pre)
        s_scr[...] = lax.dot_general(
            act[:, STATE:], act[:, :STATE], (((1,), (1,)), ((), ())), precision=EXACT, preferred_element_type=F32
        )
        _, _, sums, shifted = step_terms(steps, head_ref)
        spread(col_scr, sums, groups)
        row_scr[...] = shifted.T
        sq_scr[...] = jnp.zeros_like(sq_scr)

        def group(j, carry):
            wait_all(of_group(j))
            nb = nb_scr[...]
            z = nn_dot(nb, fold(wz_scr[j]))
            z_scr[j] = z
            v = nn_dot(nb, fold(wx_scr[j]))
            v_scr[j] = v
            taps = chan_ref[:, lanes(j)]
            c = conv_rows(v, taps[0:4, :], taps[4:5, :])
            x = c * sigmoid(c)
            x_low = x.astype(BF16)
            cols = col_scr[j]
            rws = row_scr[pl.ds(pl.multiple_of(j * GROUP, GROUP), GROUP), :]
            lane = lax.broadcasted_iota(jnp.int32, (HALF, HALF), 1)
            causal = lax.broadcasted_iota(jnp.int32, (HALF, HALF), 0) >= lane
            first = lane < HEAD_DIM
            parts = []
            for pair in range(GROUP // 2):
                here = slice(pair * HALF, (pair + 1) * HALF)
                pieces = []
                for tb in range(rows // HALF):
                    t_here = slice(tb * HALF, (tb + 1) * HALF)
                    both = []
                    for h in (2 * pair, 2 * pair + 1):
                        col = cols[t_here, h : h + 1]
                        mix = []
                        for sb in range(tb + 1):
                            s_here = slice(sb * HALF, (sb + 1) * HALF)
                            gap = col - rws[h : h + 1, s_here]
                            if sb == tb:
                                gap = jnp.where(causal, gap, NEG)
                            mix.append((jnp.exp2(gap) * s_scr[t_here, s_here]).astype(BF16))
                        mix = jnp.concatenate(mix, axis=1) if len(mix) > 1 else mix[0]
                        both.append(nn_dot(mix, x_low[: (tb + 1) * HALF, here]))
                    pieces.append(jnp.where(first, both[0], both[1]))
                parts.append(jnp.concatenate(pieces, axis=0))
            y = jnp.concatenate(parts, axis=1) + taps[6:7, :] * x
            y_scr[j] = y
            w = y * (z * sigmoid(z))
            w_scr[j] = w
            sq_scr[...] += jnp.sum(w * w, axis=1, keepdims=True)
            start_all(kept_copies(j))
            return carry

        lax.fori_loop(0, groups, group, 0)
        scale = lax.rsqrt(sq_scr[...] * (1.0 / (groups * WIDE)) + EPS)
        for g in range(groups):
            here = slice(g * WIDE, (g + 1) * WIDE)
            gb_scr[:, here] = (w_scr[g] * scale * gate_ref[:, here]).astype(BF16)
        start_all(whole_copies)
        live = lax.broadcasted_iota(jnp.int32, (rows, 1), 0) < at_ref[0]
        for k in range(wo_scr.shape[0]):
            here = slice(k * WIDE, (k + 1) * WIDE)
            of_out(k).wait()
            branch = jnp.where(live, nn_dot(gb_scr[...], wo_scr[k]), 0.0)
            h_scr[:, here] = (u_scr[:, here].astype(F32) + branch).astype(BF16)
        h_copy.start()
        for j in range(groups):
            wait_all(kept_copies(j))
        wait_all(whole_copies)
        h_copy.wait()


def forward_slot(place, numbers, kept, u, w_all, view, norm_gain, chan, chan_r, heads, gate_gain, slots):
    rows, width = u.shape
    inner = chan.shape[1]
    groups = inner // WIDE
    parts, _, depth, _ = view.shape
    shapes = [((rows, width), BF16), ((rows, inner), BF16)] + [((rows, inner), F32)] * 3
    shapes += [((rows, 3 * STATE), F32), ((rows, 2 * STATE), F32)]
    far = pl.BlockSpec(memory_space=pl.ANY)
    near = pl.BlockSpec(memory_space=pltpu.VMEM)
    args = [numbers, u, w_all, view, norm_gain, chan, chan_r, heads, gate_gain]
    in_specs = [pl.BlockSpec(memory_space=pltpu.SMEM), far, far, far] + [near] * 5
    aliases = {}
    if kept is not None:
        for k, arr in enumerate(kept):
            aliases[len(args)] = k
            args.append(arr)
            in_specs.append(far)
    out_shape = [jax.ShapeDtypeStruct((slots,) + s, d) for s, d in shapes]
    tall = pltpu.VMEM((groups, parts, depth, WIDE), BF16)
    wide = pltpu.VMEM((groups, rows, WIDE), F32)
    *kept, h = pl.pallas_call(
        functools.partial(forward_kernel, place),
        in_specs=in_specs,
        out_specs=[far] * 8,
        out_shape=out_shape + [jax.ShapeDtypeStruct((rows, width), BF16)],
        scratch_shapes=[
            pltpu.VMEM((rows, width), BF16),
            tall,
            tall,
            pltpu.VMEM((3, parts, depth, HALF), BF16),
            pltpu.VMEM((width // WIDE, inner, WIDE), BF16),
            pltpu.VMEM((rows, width), BF16),
            pltpu.VMEM((rows, inner), BF16),
            wide,
            wide,
            wide,
            pltpu.VMEM((rows, 3 * STATE), F32),
            pltpu.VMEM((rows, 2 * STATE), F32),
            pltpu.VMEM((rows, width), BF16),
            wide,
            pltpu.VMEM((rows, 1), F32),
            pltpu.VMEM((rows, rows), F32),
            pltpu.VMEM((groups, rows, HALF), F32),
            pltpu.VMEM((HALF, rows), F32),
            pltpu.SemaphoreType.DMA((2 * groups + 4 + width // WIDE,)),
            pltpu.SemaphoreType.DMA((3 * groups + 5,)),
        ],
        input_output_aliases=aliases,
        compiler_params=pltpu.CompilerParams(vmem_limit_bytes=VMEM),
        cost_estimate=pl.CostEstimate(flops=22 * 10**9, bytes_accessed=60 * 10**6, transcendentals=0),
        name="forward_slot",
    )(*args)
    return kept, h


def backward_kernel(
    place, at_ref, g_hbm, u_hbm, w_hbm, view_hbm, z_hbm, v_hbm, y_hbm, vr_hbm, cr_hbm,
    norm_ref, chan_ref, chanr_ref, head_ref, past_ref, *rest
):
    (
        du_hbm, dz_hbm, dv_hbm, sum_ref,
        g_scr, u_scr, wo_scr, wz_scr, wx_scr, wr_scr, z_scr, v_scr, y_scr, vr_scr, cr_scr, dz_scr, dv_scr,
        dob_scr, dgb_scr, sq_scr, we_scr, st_scr, ds_scr, bcol_scr, trow_scr, colr_scr, rowr_scr, step_scr, act_scr, dn_scr,
        sem, out_sem,
    ) = rest[-32:]
    groups, rows, _ = dgb_scr.shape
    width = g_scr.shape[1]
    inner = groups * WIDE
    of_group, of_rest = in_copies(view_hbm, wz_scr, wx_scr, wr_scr, sem, 4)
    base = 2 * groups + 7
    g_copy = pltpu.make_async_copy(g_hbm, g_scr, sem.at[0])
    u_copy = pltpu.make_async_copy(u_hbm, u_scr, sem.at[1])
    vr_copy = pltpu.make_async_copy(vr_hbm.at[place], vr_scr, sem.at[2])
    cr_copy = pltpu.make_async_copy(cr_hbm.at[place], cr_scr, sem.at[3])

    def early(j):
        tall = pl.ds(pl.multiple_of(j * WIDE, WIDE), WIDE)
        return [
            pltpu.make_async_copy(w_hbm.at[tall, pl.ds(0, width)], wo_scr.at[j], sem.at[base + j]),
            pltpu.make_async_copy(z_hbm.at[place, :, lanes(j)], z_scr.at[j], sem.at[base + groups + j]),
            pltpu.make_async_copy(y_hbm.at[place, :, lanes(j)], y_scr.at[j], sem.at[base + 2 * groups + j]),
        ]

    def late(j):
        return of_group(j) + [
            pltpu.make_async_copy(v_hbm.at[place, :, lanes(j)], v_scr.at[j], sem.at[base + 3 * groups + j]),
        ]

    def dz_copy(j):
        return pltpu.make_async_copy(dz_scr.at[j], dz_hbm.at[:, lanes(j)], out_sem.at[j])

    dv_copy = pltpu.make_async_copy(dv_scr, dv_hbm, out_sem.at[groups])
    du_copy = pltpu.make_async_copy(dob_scr, du_hbm, out_sem.at[groups + 1])

    @pl.when(at_ref[1] != 1)
    def _():
        sum_ref[...] = past_ref[...]

    @pl.when(at_ref[1] == 1)
    def _():
        start_all([g_copy, vr_copy, cr_copy])
        for j in range(groups):
            start_all(early(j))
        for j in range(groups):
            start_all(late(j))
        start_all(of_rest() + [u_copy])

        sq_scr[...] = jnp.zeros_like(sq_scr)
        we_scr[...] = jnp.zeros_like(we_scr)
        ds_scr[...] = jnp.zeros_like(ds_scr)
        dn_scr[...] = jnp.zeros_like(dn_scr)
        rowr_scr[...] = jnp.zeros_like(rowr_scr)
        g_copy.wait()
        live = lax.broadcasted_iota(jnp.int32, (rows, 1), 0) < at_ref[0]
        dob_scr[...] = jnp.where(live, g_scr[...].astype(F32), 0.0).astype(BF16)
        cr_copy.wait()
        pre = cr_scr[...]
        act = pre * sigmoid(pre)
        act_scr[...] = act
        st_scr[...] = lax.dot_general(
            act[:, :STATE], act[:, STATE:], (((1,), (1,)), ((), ())), precision=EXACT, preferred_element_type=F32
        )
        vr_copy.wait()
        step, rate, sums, shifted = step_terms(vr_scr[:, 2 * STATE : 3 * STATE], head_ref)
        step_scr[...] = step
        spread(bcol_scr, shifted, groups)
        trow_scr[...] = sums.T

        def first_pass(j, carry):
            wait_all(early(j))
            dgb = nt_dot(dob_scr[...], wo_scr[j])
            dgb_scr[j] = dgb
            z = z_scr[j]
            w = y_scr[j] * (z * sigmoid(z))
            sq_scr[...] += jnp.sum(w * w, axis=1, keepdims=True)
            we_scr[...] += jnp.sum(w * (dgb * chan_ref[5:6, lanes(j)]), axis=1, keepdims=True)
            return carry

        lax.fori_loop(0, groups, first_pass, 0)

        def second_pass(j, carry):
            wait_all(late(j))
            wide = lanes(j)
            taps = chan_ref[:, wide]
            q = lax.rsqrt(sq_scr[...] * (1.0 / inner) + EPS)
            pull = q * q * q * (we_scr[...] * (1.0 / inner))
            dgb = dgb_scr[j]
            z = z_scr[j]
            y = y_scr[j]
            sz = sigmoid(z)
            silu_z = z * sz
            w = y * silu_z
            dw = q * (dgb * taps[5:6, :]) - w * pull
            sum_ref[5:6, wide] = past_ref[5:6, wide] + jnp.sum(w * q * dgb, axis=0, keepdims=True)
            dy = dw * silu_z
            dz = (dw * y * (sz * (1.0 + z * (1.0 - sz)))).astype(BF16)
            dz_scr[j] = dz
            dz_copy(j).start()
            dn = nt_dot(dz, fold(wz_scr[j]))

            c = conv_rows(v_scr[j], taps[0:4, :], taps[4:5, :])
            sc = sigmoid(c)
            x = c * sc
            x_low = x.astype(BF16)
            dy_low = dy.astype(BF16)
            sum_ref[6:7, wide] = past_ref[6:7, wide] + jnp.sum(dy * x, axis=0, keepdims=True)
            cols = bcol_scr[j]
            head_rows = pl.ds(pl.multiple_of(j * GROUP, GROUP), GROUP)
            rws = trow_scr[head_rows, :]
            lane = lax.broadcasted_iota(jnp.int32, (HALF, HALF), 1)
            causal = lane >= lax.broadcasted_iota(jnp.int32, (HALF, HALF), 0)
            first = lane < HEAD_DIM
            lane_row = lax.broadcasted_iota(jnp.int32, (1, HALF), 1)
            sub = lax.broadcasted_iota(jnp.int32, (GROUP, HALF), 0)
            blocks = rows // HALF
            col_sums = [jnp.zeros((HALF, HALF), F32) for _ in range(blocks)]
            row_sums = [jnp.zeros((GROUP, HALF), F32) for _ in range(blocks)]
            parts = []
            for pair in range(GROUP // 2):
                here = slice(pair * HALF, (pair + 1) * HALF)
                pieces = []
                row_part = [[None] * blocks, [None] * blocks]
                for sb in range(blocks):
                    s_here = slice(sb * HALF, (sb + 1) * HALF)
                    x_here = x_low[s_here, here]
                    split = (
                        jnp.where(first, x_here, jnp.zeros_like(x_here)),
                        jnp.where(first, jnp.zeros_like(x_here), x_here),
                    )
                    mixes = [[], []]
                    lane_sum = [None, None]
                    for tb in range(sb, blocks):
                        t_here = slice(tb * HALF, (tb + 1) * HALF)
                        dy_here = dy_low[t_here, here]
                        contact = st_scr[s_here, t_here]
                        touched = None
                        for k in range(2):
                            h = 2 * pair + k
                            gap = rws[h : h + 1, t_here] - cols[s_here, h : h + 1]
                            if sb == tb:
                                gap = jnp.where(causal, gap, NEG)
                            decay = jnp.exp2(gap)
                            mix = decay * contact
                            meet = nt_dot(split[k], dy_here)
                            through = decay * meet
                            pairs = through * contact
                            touched = through if touched is None else touched + through
                            mixes[k].append(mix.astype(BF16))
                            lane_sum[k] = pairs if lane_sum[k] is None else lane_sum[k] + pairs
                            down = jnp.sum(pairs, axis=0, keepdims=True)
                            row_part[k][tb] = down if row_part[k][tb] is None else row_part[k][tb] + down
                        ds_scr[s_here, t_here] += touched
                    out = []
                    for k in range(2):
                        h = 2 * pair + k
                        mix = jnp.concatenate(mixes[k], axis=1) if len(mixes[k]) > 1 else mixes[k][0]
                        out.append(nn_dot(mix, dy_low[sb * HALF :, here]))
                        total = jnp.sum(lane_sum[k], axis=1, keepdims=True)
                        col_sums[sb] = jnp.where(lane_row == h, total, col_sums[sb])
                    pieces.append(jnp.where(first, out[0], out[1]))
                for k in range(2):
                    for tb in range(blocks):
                        row_sums[tb] = jnp.where(sub == 2 * pair + k, row_part[k][tb], row_sums[tb])
                parts.append(jnp.concatenate(pieces, axis=0))
            colr_scr[j] = jnp.concatenate(col_sums, axis=0)
            rowr_scr[head_rows, :] = jnp.concatenate(row_sums, axis=1)
            dx = jnp.concatenate(parts, axis=1) + taps[6:7, :] * dy
            dc = dx * (sc * (1.0 + c * (1.0 - sc)))
            dv = conv_back(dc, v_scr[j], taps, past_ref, sum_ref, wide).astype(BF16)
            dv_scr[:, wide] = dv
            dn_scr[...] += dn + nt_dot(dv, fold(wx_scr[j]))
            return carry

        lax.fori_loop(0, groups, second_pass, 0)
        act = act_scr[...]
        ds = ds_scr[...].astype(BF16)
        act_low = act.astype(BF16)
        d_b = nn_dot(ds, act_low[:, STATE:])
        d_c = lax.dot_general(ds, act_low[:, :STATE], (((0,), (0,)), ((), ())), preferred_element_type=F32)
        pre = cr_scr[...]
        sp = sigmoid(pre)
        d_pre = jnp.concatenate([d_b, d_c], axis=1) * (sp * (1.0 + pre * (1.0 - sp)))
        narrow = slice(inner, inner + 2 * STATE)
        d_raw = conv_back(d_pre, vr_scr[:, : 2 * STATE], chanr_ref[...], past_ref, sum_ref, narrow)
        sum_ref[5:7, narrow] = jnp.zeros((2, 2 * STATE), F32)
        col_total = colr_scr[0]
        for g in range(1, groups):
            col_total = col_total + pltpu.roll(colr_scr[g], g * GROUP, 1)
        d_sums = rowr_scr[...].T - col_total
        at_row = lax.broadcasted_iota(jnp.int32, (rows, rows), 0)
        of_row = lax.broadcasted_iota(jnp.int32, (rows, rows), 1)
        upper = (of_row >= at_row).astype(F32)
        d_log = jnp.dot(upper, d_sums, precision=EXACT, preferred_element_type=F32)
        step = step_scr[...]
        rate = -jnp.exp(head_ref[1:2, :])
        d_step = col_total / step + rate * d_log
        raw_step = vr_scr[:, 2 * STATE : 3 * STATE] + head_ref[0:1, :]
        used = lax.broadcasted_iota(jnp.int32, (rows, HALF), 1) < inner // HEAD_DIM
        d_raw_step = jnp.where(used, d_step * jax.nn.sigmoid(raw_step), 0.0)
        last = past_ref[7:8, :]
        sum_ref[7:8, width : width + HALF] = last[:, width : width + HALF] + jnp.sum(d_raw_step, axis=0, keepdims=True)
        sum_ref[7:8, width + HALF : width + 2 * HALF] = last[:, width + HALF : width + 2 * HALF] + jnp.sum(
            jnp.where(used, d_log * step * rate, 0.0), axis=0, keepdims=True
        )
        sum_ref[7:8, width + 2 * HALF :] = jnp.zeros((1, inner - width), F32)
        dr = jnp.concatenate([d_raw, d_raw_step], axis=1).astype(BF16)
        dv_scr[:, inner:] = dr
        dv_copy.start()
        wait_all(of_rest())
        dn = dn_scr[...]
        for k in range(3):
            dn = dn + nt_dot(dr[:, k * STATE : (k + 1) * STATE], fold(wr_scr[k]))
        u_copy.wait()
        u = u_scr[...].astype(F32)
        p = lax.rsqrt(jnp.mean(u * u, axis=1, keepdims=True) + EPS)
        e = dn * norm_ref[...]
        du = g_scr[...].astype(F32) + p * e - u * (p * p * p * jnp.mean(u * e, axis=1, keepdims=True))
        dob_scr[...] = du.astype(BF16)
        du_copy.start()
        sum_ref[7:8, :width] = last[:, :width] + jnp.sum(u * p * dn, axis=0, keepdims=True)
        for j in range(groups):
            dz_copy(j).wait()
        dv_copy.wait()
        du_copy.wait()


def conv_back(dc, values, taps, past_ref, sum_ref, here):
    rows = lax.broadcasted_iota(jnp.int32, dc.shape, 0)
    count = dc.shape[0]
    sum_ref[4:5, here] = past_ref[4:5, here] + jnp.sum(dc, axis=0, keepdims=True)
    total = 0.0
    for ahead in range(CONV):
        moved = jnp.where(rows < count - ahead, pltpu.roll(dc, count - ahead, 0), 0.0) if ahead else dc
        tap = CONV - 1 - ahead
        sum_ref[tap : tap + 1, here] = past_ref[tap : tap + 1, here] + jnp.sum(moved * values, axis=0, keepdims=True)
        total = total + taps[tap : tap + 1, :] * moved
    return total


def backward_slot(place, numbers, kept, grads, past, g, u, w_all, view, norm_gain, chan, chan_r, heads):
    rows, width = g.shape
    inner = chan.shape[1]
    groups = inner // WIDE
    parts, _, depth, _ = view.shape
    far = pl.BlockSpec(memory_space=pl.ANY)
    near = pl.BlockSpec(memory_space=pltpu.VMEM)
    args = [numbers, g, u, w_all, view, *kept, norm_gain, chan, chan_r, heads, past]
    in_specs = [pl.BlockSpec(memory_space=pltpu.SMEM)] + [far] * 9 + [near] * 5
    aliases = {}
    if grads is not None:
        for k, arr in enumerate(grads):
            aliases[len(args)] = k + 1
            args.append(arr)
            in_specs.append(far)
    tall = pltpu.VMEM((groups, parts, depth, WIDE), BF16)
    wide = pltpu.VMEM((groups, rows, WIDE), F32)
    slot = pltpu.VMEM((rows, width), BF16)
    return pl.pallas_call(
        functools.partial(backward_kernel, place),
        in_specs=in_specs,
        out_specs=[far, far, far, near],
        out_shape=[
            jax.ShapeDtypeStruct((rows, width), BF16),
            jax.ShapeDtypeStruct((rows, inner), BF16),
            jax.ShapeDtypeStruct((rows, inner + 3 * STATE), BF16),
            jax.ShapeDtypeStruct((8, inner + 2 * STATE), F32),
        ],
        scratch_shapes=[
            slot,
            slot,
            pltpu.VMEM((groups, WIDE, width), BF16),
            tall,
            tall,
            pltpu.VMEM((3, parts, depth, HALF), BF16),
            wide,
            wide,
            wide,
            pltpu.VMEM((rows, 3 * STATE), F32),
            pltpu.VMEM((rows, 2 * STATE), F32),
            pltpu.VMEM((groups, rows, WIDE), BF16),
            pltpu.VMEM((rows, inner + 3 * STATE), BF16),
            slot,
            wide,
            pltpu.VMEM((rows, 1), F32),
            pltpu.VMEM((rows, 1), F32),
            pltpu.VMEM((rows, rows), F32),
            pltpu.VMEM((rows, rows), F32),
            pltpu.VMEM((groups, rows, HALF), F32),
            pltpu.VMEM((HALF, rows), F32),
            pltpu.VMEM((groups, rows, HALF), F32),
            pltpu.VMEM((HALF, rows), F32),
            pltpu.VMEM((rows, HALF), F32),
            pltpu.VMEM((rows, 2 * STATE), F32),
            pltpu.VMEM((rows, width), F32),
            pltpu.SemaphoreType.DMA((6 * groups + 7,)),
            pltpu.SemaphoreType.DMA((groups + 2,)),
        ],
        input_output_aliases=aliases,
        compiler_params=pltpu.CompilerParams(vmem_limit_bytes=VMEM),
        cost_estimate=pl.CostEstimate(flops=10**9, bytes_accessed=10**6, transcendentals=0),
        name="backward_slot",
    )(*args)


def pack_kernel(inner, in_ref, out_ref, packed_ref):
    depth, width = in_ref.shape[0], out_ref.shape[1]
    mid, end = 2 * inner + 2 * STATE, in_ref.shape[1]
    packed_ref[:, :width] = out_ref[...]
    tail = width + inner
    for half in range(2):
        rows = slice(half * depth, (half + 1) * depth)
        packed_ref[rows, width:tail] = in_ref[:, half * inner : (half + 1) * inner]
        packed_ref[rows, tail : tail + STATE] = in_ref[:, mid - 2 * STATE + half * STATE : mid - STATE + half * STATE]
        packed_ref[rows, tail + STATE :] = jnp.zeros((depth, STATE), BF16)
    packed_ref[:depth, tail + STATE : tail + STATE + end - mid] = in_ref[:, mid:]


def pack(in_shard, out_shard, inner):
    depth, width = in_shard.shape[0], out_shard.shape[1]
    return pl.pallas_call(
        functools.partial(pack_kernel, inner),
        out_shape=jax.ShapeDtypeStruct((2 * depth, width + inner + 2 * STATE), BF16),
        name="pack",
    )(in_shard, out_shard)


def order_kernel(at_ref, a_ref, own_ref, other_ref, turn_scr):
    turn_scr[...] = a_ref[0].astype(F32).T.reshape(turn_scr.shape)
    for part in range(2):
        for line in range(own_ref.shape[2]):
            own_ref[part, 0, line] = turn_scr[4 * line + at_ref[1 + 2 * part]].astype(BF16)
            other_ref[part, 0, line] = turn_scr[4 * line + at_ref[2 + 2 * part]].astype(BF16)


def by_owner(numbers, values, micro, count):
    _, rows, total = values.shape
    depth = total // count
    line = count // 4
    out = pl.BlockSpec((2, 1, line, depth, rows), lambda i, n: (0, i, 0, 0, 0))
    made = jax.ShapeDtypeStruct((2, micro, line, depth, rows), BF16)
    own, other = pl.pallas_call(
        order_kernel,
        grid_spec=pltpu.PrefetchScalarGridSpec(
            num_scalar_prefetch=1,
            grid=(micro,),
            in_specs=[pl.BlockSpec((1, rows, total), lambda i, n: (n[0] + i, 0, 0))],
            out_specs=[out, out],
            scratch_shapes=[pltpu.VMEM((count, depth, rows), F32)],
        ),
        out_shape=[made, made],
        compiler_params=pltpu.CompilerParams(vmem_limit_bytes=VMEM),
        cost_estimate=pl.CostEstimate(flops=3 * 10**9, bytes_accessed=2 * 10**6, transcendentals=0),
        name="by_owner",
    )(numbers, values)
    flat = (2, micro, line * depth, rows)
    return own.reshape(flat), other.reshape(flat)


def outer_kernel(own_ref, sib_ref, *rest):
    rights, outs = rest[:-2], rest[-2:]
    micro = own_ref.shape[1]
    right = jnp.concatenate([ref[...] for ref in rights], axis=0)
    for part, out_ref in enumerate(outs):
        left = jnp.concatenate([ref[part, m] for ref in (own_ref, sib_ref) for m in range(micro)], axis=1)
        out_ref[...] = nn_dot(left, right).astype(BF16)


def outer_sum(own, sib, rights, start, stop, block):
    _, micro, high, rows = own.shape
    low, steps = start // block, (stop - start) // block
    full = pl.BlockSpec(own.shape, lambda i: (0, 0, 0, 0))
    out = pl.BlockSpec((high, block), lambda i: (0, i))
    made = jax.ShapeDtypeStruct((high, stop - start), BF16)
    return pl.pallas_call(
        outer_kernel,
        grid=(steps,),
        in_specs=[full, full] + [pl.BlockSpec((rows, block), lambda i: (0, low + i)) for _ in rights],
        out_specs=[out, out],
        out_shape=[made, made],
        compiler_params=pltpu.CompilerParams(vmem_limit_bytes=VMEM),
        cost_estimate=pl.CostEstimate(flops=10**9, bytes_accessed=10**6, transcendentals=0),
        name="outer_sum",
    )(own, sib, *rights)


def pick(values, index, axis):
    return lax.dynamic_index_in_dim(values, index, axis, keepdims=False)


def swap(values, axis, bit):
    return lax.ppermute(values, axis, [(a, a ^ bit) for a in range(lax.axis_size(axis))])


def all_rows_of(row, axis):
    count = lax.axis_size(axis)
    place = lax.axis_index(axis)
    table = jnp.where(jnp.arange(count, dtype=jnp.int32)[:, None] == place, row[None], jnp.zeros((), row.dtype))
    bit = 1
    while bit < count:
        table = table + swap(table, axis, bit)
        bit *= 2
    return table


def owned_sums(chunks, axis, rider):
    count = lax.axis_size(axis)
    length = count // 4
    results, token = [], None
    rider_far = swap(rider, axis, 2)
    for k, (keep, far) in enumerate(chunks):
        rides = k == len(chunks) - 1
        if token is not None:
            far, _ = lax.optimization_barrier((far, token))
        if rides:
            far, rider_far = lax.optimization_barrier((far, rider_far))
            rider = rider + rider_far
        terms = [a.reshape(length, -1, a.shape[1]) for a in (keep, far)]
        bit = 1
        while bit < length:
            mine = (lax.axis_index(axis) // (4 * bit)) % 2
            half = lambda a, which: pick(a.reshape((-1, 2) + a.shape[1:]), which, 1)
            sent = sum(half(a, 1 - mine).astype(F32) for a in terms).astype(BF16)
            if rides:
                sent, rider = lax.optimization_barrier((sent, rider))
            came = swap(sent, axis, 4 * bit)
            if rides:
                rider = rider + swap(rider, axis, 4 * bit)
            terms = [half(a, mine) for a in terms] + [came]
            token = came if k == 0 else sent
            bit *= 2
        results.append(sum(a[0].astype(F32) for a in terms))
    return results, rider


def body(
    block_input,
    cotangent,
    lengths,
    in_weight,
    out_weight,
    conv_weight,
    conv_bias,
    norm_gain,
    gate_gain,
    dt_bias,
    a_log,
    skip_d,
):
    axis = "fsdp"
    count = lax.axis_size(axis)
    section = lax.axis_index("section")
    micro, rows, width = block_input.shape
    depth, proj_cols = in_weight.shape[1:]
    inner = gate_gain.shape[1] * count
    channels = conv_bias.shape[1] * count
    heads = dt_bias.shape[1]
    small = [a.reshape(-1) for a in (conv_weight[0], conv_bias[0], norm_gain[0], gate_gain[0])]
    sizes = [a.shape[0] for a in small]
    w_all = lax.all_gather(pack(in_weight[0], out_weight[0], inner), axis, axis=0, tiled=True)
    view = w_all.reshape(count, 2, depth, -1)
    if depth % 16:
        view = view.transpose(1, 0, 2, 3).reshape(1, 2, width, -1)
    flat = all_rows_of(jnp.concatenate(small), axis).astype(F32)
    cuts = [0]
    for size in sizes:
        cuts.append(cuts[-1] + size)
    taps = flat[:, cuts[0] : cuts[1]].reshape(count, CONV, -1).transpose(1, 0, 2).reshape(CONV, channels)
    bias = flat[:, cuts[1] : cuts[2]].reshape(1, channels)
    norm = flat[:, cuts[2] : cuts[3]].reshape(1, width)
    gate = flat[:, cuts[3] : cuts[4]].reshape(1, inner)
    skip = jnp.repeat(skip_d[0], HEAD_DIM)[None]
    chan = jnp.concatenate([taps[:, :inner], bias[:, :inner], gate, skip, jnp.zeros((1, inner), F32)], axis=0)
    chan_r = jnp.concatenate([taps[:, inner:], bias[:, inner:], jnp.zeros((3, channels - inner), F32)], axis=0)
    head_rows = jnp.pad(jnp.stack([dt_bias[0], a_log[0]]), ((0, 6), (0, HALF - heads)))
    places = jnp.arange(rows, dtype=jnp.int32)
    live = [(places < lengths[m, 0])[:, None] for m in range(micro)]

    def numbers(m, stage):
        return jnp.stack([lengths[m, 0], (section == stage).astype(jnp.int32)])

    kept = None
    first, second = [], []
    for m in range(micro):
        kept, h = forward_slot(
            m, numbers(m, 0), kept, block_input[m], w_all, view, norm, chan, chan_r, head_rows, gate, 2 * micro
        )
        first.append(h)
    arrived = [lax.ppermute(h, "section", [(0, 1)]) for h in first]
    for m in range(micro):
        kept, h = forward_slot(
            micro + m, numbers(m, 1), kept, arrived[m], w_all, view, norm, chan, chan_r, head_rows, gate, 2 * micro
        )
        second.append(h)
    outputs = jnp.stack([jnp.where(section == 0, a, b) for a, b in zip(first, second)])

    def run_backward(place, m, stage, grads, sums, g, u):
        return backward_slot(
            place, numbers(m, stage), kept[2:], grads, sums, g, u, w_all, view, norm, chan, chan_r, head_rows
        )

    is_last = section == 1
    sums = jnp.zeros((8, inner + 2 * STATE), F32)
    grads, late_grads, early_grads, returned = [None] * micro, [None] * micro, [None] * micro, [None] * micro
    for m in reversed(range(micro)):
        late_grads[m], *grads[m], sums = run_backward(micro + m, m, 1, None, sums, cotangent[m], arrived[m])
        returned[m] = lax.ppermute(late_grads[m], "section", [(1, 0)])

    mine = (lax.axis_index(axis) % 4).astype(jnp.int32)
    owners = jnp.stack([section * micro, mine, mine ^ 1, mine ^ 2, mine ^ 3]).astype(jnp.int32)
    nb, gb, _ = lax.optimization_barrier((kept[0], kept[1], late_grads[0]))
    out_own, out_other = by_owner(owners, gb, micro, count)
    in_own, in_other = by_owner(owners, nb, micro, count)
    out_sib, in_sib = swap(out_other, axis, 1), swap(in_other, axis, 1)
    returned[-1], out_own, in_own = lax.optimization_barrier((returned[-1], out_own, in_own))

    branch, branch_sib, z_sib, v_sib = [None] * micro, [None] * micro, [None] * micro, [None] * micro

    def take_branch(m):
        branch[m] = jnp.where(live[m], jnp.where(is_last, cotangent[m], returned[m]), jnp.zeros((), BF16))
        branch_sib[m] = swap(branch[m], axis, 1)

    for m in reversed(range(1, micro)):
        take_branch(m)
        early_grads[m], *grads[m], sums = run_backward(m, m, 0, grads[m], sums, returned[m], block_input[m])
        z_sib[m], v_sib[m] = (swap(a, axis, 1) for a in grads[m])
    returned[0], early_grads[-1] = lax.optimization_barrier((returned[0], early_grads[-1]))
    take_branch(0)
    out_keep, out_send = outer_sum(out_own, out_sib, branch + branch_sib, 0, width, WIDE)
    returned[0], out_send = lax.optimization_barrier((returned[0], out_send))
    out_far = swap(out_send, axis, 2)
    early_grads[0], *grads[0], sums = run_backward(0, 0, 0, grads[0], sums, returned[0], block_input[0])
    z_sib[0], v_sib[0] = (swap(a, axis, 1) for a in grads[0])
    input_grads = jnp.stack([jnp.where(is_last, a, b) for a, b in zip(late_grads, early_grads)])

    z_rows = [a for a, _ in grads] + z_sib
    v_rows = [a for _, a in grads] + v_sib
    cut, end = 5 * 384, inner + 3 * STATE
    pairs = [
        outer_sum(in_own, in_sib, z_rows, 0, inner, 2 * WIDE),
        outer_sum(in_own, in_sib, v_rows, 0, cut, 640),
        outer_sum(in_own, in_sib, v_rows, cut, end, 384),
    ]
    pairs[0], out_far = lax.optimization_barrier((pairs[0], out_far))
    sums, _ = lax.optimization_barrier((sums, pairs[-1][1]))
    sums = sums + swap(sums, axis, 1)
    chunks = [(out_keep, out_far)] + [(keep, swap(send, axis, 2)) for keep, send in pairs]
    parts, sums = owned_sums(chunks, axis, sums)
    out_grad, in_grad = parts[0], jnp.concatenate(parts[1:], axis=1)[:, :proj_cols]

    place = lax.axis_index(axis)
    cut_out = lambda row, size: lax.dynamic_slice(sums, (row, place * size), (1, size))
    taps_g = lax.dynamic_slice(sums, (0, place * (channels // count)), (CONV, channels // count))
    skip_g = sums[6, :inner].reshape(heads, HEAD_DIM).sum(axis=1)
    return (
        outputs[None],
        input_grads[None],
        in_grad[None],
        out_grad[None],
        taps_g[None],
        cut_out(4, channels // count),
        cut_out(7, width // count),
        cut_out(5, inner // count),
        sums[7:8, width : width + heads],
        sums[7:8, width + HALF : width + HALF + heads],
        skip_g[None],
    )


def solution(mesh):
    in_specs = (
        P(None, "fsdp", None),
        P(None, "fsdp", None),
        P(None, "fsdp"),
        P("section", "fsdp", None),
        P("section", "fsdp", None),
        P("section", None, "fsdp"),
        P("section", "fsdp"),
        P("section", "fsdp"),
        P("section", "fsdp"),
        P("section", None),
        P("section", None),
        P("section", None),
    )
    out_specs = (
        P("section", None, "fsdp", None),
        P("section", None, "fsdp", None),
        P("section", "fsdp", None),
        P("section", "fsdp", None),
        P("section", None, "fsdp"),
        P("section", "fsdp"),
        P("section", "fsdp"),
        P("section", "fsdp"),
        P("section", None),
        P("section", None),
        P("section", None),
    )
    return jax.shard_map(body, mesh=mesh, in_specs=in_specs, out_specs=out_specs, check_vma=False)
```

```python
import functools

import jax
import jax.numpy as jnp
from jax import lax
from jax.experimental import pallas as pl
from jax.experimental.pallas import tpu as pltpu
from jax.sharding import PartitionSpec as P

HEAD_DIM = 64
STATE = 128
CONV = 4
EPS = 1e-05
LOG2E = 1.4426950408889634
HALF = 128
WIDE = 512
GROUP = WIDE // HEAD_DIM
TINY = 1e-30
SUB = 8
CHUNK = 64
NEG = -1e30
VMEM = 60 * 1024 * 1024
F32 = jnp.float32
BF16 = jnp.bfloat16
EXACT = lax.Precision.HIGHEST


def nt_dot(a, b):
    return lax.dot_general(a, b, (((1,), (1,)), ((), ())), preferred_element_type=F32)


def nn_dot(a, b):
    return jnp.dot(a, b, preferred_element_type=F32)


def sigmoid(v):
    return 0.5 * jnp.tanh(0.5 * v) + 0.5


def down(values, steps):
    count = values.shape[0]
    moved = pltpu.roll(values, steps % count, 0)
    rows = lax.broadcasted_iota(jnp.int32, (SUB, values.shape[1]), 0)
    if steps > 0:
        return jnp.concatenate([jnp.where(rows >= steps, moved[:SUB], 0.0), moved[SUB:]], axis=0)
    return jnp.concatenate([moved[:-SUB], jnp.where(rows < SUB + steps, moved[-SUB:], 0.0)], axis=0)


def conv_rows(values, taps, bias):
    total = bias + taps[CONV - 1 : CONV, :] * values
    for back in range(1, CONV):
        total = total + taps[CONV - 1 - back : CONV - back, :] * down(values, back)
    return total


def fewer(block):
    total = block[:SUB]
    for at in range(SUB, block.shape[0], SUB):
        total = total + block[at : at + SUB]
    return total


def piece_of(scr, j, piece, pieces):
    _, parts, depth, _ = scr.shape
    if parts % pieces == 0:
        return fold(scr[j, piece * (parts // pieces) : (piece + 1) * (parts // pieces)])
    size = parts * depth // pieces
    return fold(scr[j])[piece * size : (piece + 1) * size]


def softplus(v):
    return jnp.maximum(v, 0.0) + jnp.log1p(jnp.exp(-jnp.abs(v)))


def step_terms(step_raw, head_ref):
    rows = step_raw.shape[0]
    step = jnp.maximum(softplus(step_raw + head_ref[0:1, :]), TINY)
    rate = -jnp.exp(head_ref[1:2, :])
    at = lax.broadcasted_iota(jnp.int32, (rows, rows), 0)
    of = lax.broadcasted_iota(jnp.int32, (rows, rows), 1)
    lower = (at >= of).astype(F32)
    sums = jnp.dot(lower, step * rate, precision=EXACT, preferred_element_type=F32) * LOG2E
    return step, rate, sums, sums - jnp.log2(step)


def spread(target, values, groups):
    for g in range(groups):
        target[g] = pltpu.roll(values, (HALF - g * GROUP) % HALF, 1) if g else values


def fold(block):
    return block.reshape(-1, block.shape[-1])


def lanes(index):
    return pl.ds(pl.multiple_of(index * WIDE, WIDE), WIDE)


def in_copies(view_ref, wz_scr, wx_scr, wr_scr, sem, base):
    parts, _, depth, _ = view_ref.shape
    width, groups = parts * depth, wz_scr.shape[0]
    tail = width + groups * WIDE

    def of_group(j):
        here = pl.ds(pl.multiple_of(width + j * WIDE, WIDE), WIDE)
        return [
            pltpu.make_async_copy(view_ref.at[:, 0, :, here], wz_scr.at[j], sem.at[base + j]),
            pltpu.make_async_copy(view_ref.at[:, 1, :, here], wx_scr.at[j], sem.at[base + groups + j]),
        ]

    def of_rest():
        return [
            pltpu.make_async_copy(view_ref.at[:, half, :, pl.ds(at, HALF)], wr_scr.at[k], sem.at[base + 2 * groups + k])
            for k, (half, at) in enumerate(((0, tail), (1, tail), (0, tail + HALF)))
        ]

    return of_group, of_rest


def start_all(copies):
    for copy in copies:
        copy.start()


def wait_all(copies):
    for copy in copies:
        copy.wait()


def forward_kernel(place, at_ref, u_hbm, w_hbm, view_hbm, norm_ref, chan_ref, chanr_ref, head_ref, gate_ref, *rest):
    (
        nb_hbm, gb_hbm, z_hbm, v_hbm, y_hbm, vr_hbm, cr_hbm, h_hbm,
        u_scr, wz_scr, wx_scr, wr_scr, wo_scr, nb_scr, gb_scr, z_scr, v_scr, y_scr, vr_scr, cr_scr, h_scr,
        w_scr, sq_scr, s_scr, col_scr, row_scr, sem, out_sem,
    ) = rest[-28:]
    groups, rows, _ = w_scr.shape
    of_group, of_rest = in_copies(view_hbm, wz_scr, wx_scr, wr_scr, sem, 1)
    spare = 2 * groups + 4
    u_copy = pltpu.make_async_copy(u_hbm, u_scr, sem.at[0])

    def of_out(k):
        return pltpu.make_async_copy(w_hbm.at[:, lanes(k)], wo_scr.at[k], sem.at[spare + k])

    def kept_copies(j):
        return [
            pltpu.make_async_copy(scr.at[j], hbm.at[place, :, lanes(j)], out_sem.at[k * groups + j])
            for k, (scr, hbm) in enumerate(((z_scr, z_hbm), (v_scr, v_hbm), (y_scr, y_hbm)))
        ]

    last = 3 * groups
    whole_copies = [
        pltpu.make_async_copy(scr, hbm.at[place], out_sem.at[last + k])
        for k, (scr, hbm) in enumerate(((nb_scr, nb_hbm), (gb_scr, gb_hbm), (vr_scr, vr_hbm), (cr_scr, cr_hbm)))
    ]
    h_copy = pltpu.make_async_copy(h_scr, h_hbm, out_sem.at[last + 4])

    @pl.when(at_ref[1] == 1)
    def _():
        u_copy.start()
        start_all(of_rest())
        for j in range(groups):
            start_all(of_group(j))
        for k in range(wo_scr.shape[0]):
            of_out(k).start()

        u_copy.wait()
        u = u_scr[...].astype(F32)
        scale = lax.rsqrt(jnp.mean(u * u, axis=1, keepdims=True) + EPS)
        nb_scr[...] = (u * scale * norm_ref[...]).astype(BF16)
        nb = nb_scr[...]
        wait_all(of_rest())
        raw = jnp.concatenate([nn_dot(nb, fold(wr_scr[0])), nn_dot(nb, fold(wr_scr[1]))], axis=1)
        steps = nn_dot(nb, fold(wr_scr[2]))
        vr_scr[:, : 2 * STATE] = raw
        vr_scr[:, 2 * STATE :] = steps
        pre = conv_rows(raw, chanr_ref[0:4, :], chanr_ref[4:5, :])
        cr_scr[...] = pre
        act = pre * sigmoid(pre)
        s_scr[...] = lax.dot_general(
            act[:, STATE:], act[:, :STATE], (((1,), (1,)), ((), ())), precision=EXACT, preferred_element_type=F32
        )
        _, _, sums, shifted = step_terms(steps, head_ref)
        spread(col_scr, sums, groups)
        row_scr[...] = shifted.T
        sq_scr[...] = jnp.zeros_like(sq_scr)

        def group(j, carry):
            wait_all(of_group(j))
            nb = nb_scr[...]
            z = nn_dot(nb, fold(wz_scr[j]))
            z_scr[j] = z
            v = nn_dot(nb, fold(wx_scr[j]))
            v_scr[j] = v
            taps = chan_ref[:, lanes(j)]
            c = conv_rows(v, taps[0:4, :], taps[4:5, :])
            x = c * sigmoid(c)
            x_low = x.astype(BF16)
            cols = col_scr[j]
            rws = row_scr[pl.ds(pl.multiple_of(j * GROUP, GROUP), GROUP), :]
            lane = lax.broadcasted_iota(jnp.int32, (HALF, HALF), 1)
            causal = lax.broadcasted_iota(jnp.int32, (HALF, HALF), 0) >= lane
            first = lane < HEAD_DIM
            parts = []
            for pair in range(GROUP // 2):
                here = slice(pair * HALF, (pair + 1) * HALF)
                pieces = []
                for tb in range(rows // HALF):
                    t_here = slice(tb * HALF, (tb + 1) * HALF)
                    both = []
                    for h in (2 * pair, 2 * pair + 1):
                        col = cols[t_here, h : h + 1]
                        mix = []
                        for sb in range(tb + 1):
                            s_here = slice(sb * HALF, (sb + 1) * HALF)
                            gap = col - rws[h : h + 1, s_here]
                            if sb == tb:
                                gap = jnp.where(causal, gap, NEG)
                            mix.append((jnp.exp2(gap) * s_scr[t_here, s_here]).astype(BF16))
                        mix = jnp.concatenate(mix, axis=1) if len(mix) > 1 else mix[0]
                        both.append(nn_dot(mix, x_low[: (tb + 1) * HALF, here]))
                    pieces.append(jnp.where(first, both[0], both[1]))
                parts.append(jnp.concatenate(pieces, axis=0))
            y = jnp.concatenate(parts, axis=1) + taps[6:7, :] * x
            y_scr[j] = y
            w = y * (z * sigmoid(z))
            w_scr[j] = w
            sq_scr[...] += jnp.sum(w * w, axis=1, keepdims=True)
            start_all(kept_copies(j))
            return carry

        lax.fori_loop(0, groups, group, 0)
        scale = lax.rsqrt(sq_scr[...] * (1.0 / (groups * WIDE)) + EPS)
        vr_scr[:, 3 * STATE - 1 :] = scale
        for g in range(groups):
            here = slice(g * WIDE, (g + 1) * WIDE)
            gb_scr[:, here] = (w_scr[g] * scale * gate_ref[:, here]).astype(BF16)
        start_all(whole_copies)
        live = lax.broadcasted_iota(jnp.int32, (rows, 1), 0) < at_ref[0]
        for k in range(wo_scr.shape[0]):
            here = slice(k * WIDE, (k + 1) * WIDE)
            of_out(k).wait()
            branch = jnp.where(live, nn_dot(gb_scr[...], wo_scr[k]), 0.0)
            h_scr[:, here] = (u_scr[:, here].astype(F32) + branch).astype(BF16)
        h_copy.start()
        for j in range(groups):
            wait_all(kept_copies(j))
        wait_all(whole_copies)
        h_copy.wait()


def forward_slot(place, numbers, kept, u, w_all, view, norm_gain, chan, chan_r, heads, gate_gain, slots):
    rows, width = u.shape
    inner = chan.shape[1]
    groups = inner // WIDE
    parts, _, depth, _ = view.shape
    shapes = [((rows, width), BF16), ((rows, inner), BF16)] + [((rows, inner), F32)] * 3
    shapes += [((rows, 3 * STATE), F32), ((rows, 2 * STATE), F32)]
    far = pl.BlockSpec(memory_space=pl.ANY)
    near = pl.BlockSpec(memory_space=pltpu.VMEM)
    args = [numbers, u, w_all, view, norm_gain, chan, chan_r, heads, gate_gain]
    in_specs = [pl.BlockSpec(memory_space=pltpu.SMEM), far, far, far] + [near] * 5
    aliases = {}
    if kept is not None:
        for k, arr in enumerate(kept):
            aliases[len(args)] = k
            args.append(arr)
            in_specs.append(far)
    out_shape = [jax.ShapeDtypeStruct((slots,) + s, d) for s, d in shapes]
    tall = pltpu.VMEM((groups, parts, depth, WIDE), BF16)
    wide = pltpu.VMEM((groups, rows, WIDE), F32)
    *kept, h = pl.pallas_call(
        functools.partial(forward_kernel, place),
        in_specs=in_specs,
        out_specs=[far] * 8,
        out_shape=out_shape + [jax.ShapeDtypeStruct((rows, width), BF16)],
        scratch_shapes=[
            pltpu.VMEM((rows, width), BF16),
            tall,
            tall,
            pltpu.VMEM((3, parts, depth, HALF), BF16),
            pltpu.VMEM((width // WIDE, inner, WIDE), BF16),
            pltpu.VMEM((rows, width), BF16),
            pltpu.VMEM((rows, inner), BF16),
            wide,
            wide,
            wide,
            pltpu.VMEM((rows, 3 * STATE), F32),
            pltpu.VMEM((rows, 2 * STATE), F32),
            pltpu.VMEM((rows, width), BF16),
            wide,
            pltpu.VMEM((rows, 1), F32),
            pltpu.VMEM((rows, rows), F32),
            pltpu.VMEM((groups, rows, HALF), F32),
            pltpu.VMEM((HALF, rows), F32),
            pltpu.SemaphoreType.DMA((2 * groups + 4 + width // WIDE,)),
            pltpu.SemaphoreType.DMA((3 * groups + 5,)),
        ],
        input_output_aliases=aliases,
        compiler_params=pltpu.CompilerParams(vmem_limit_bytes=VMEM),
        cost_estimate=pl.CostEstimate(flops=22 * 10**9, bytes_accessed=60 * 10**6, transcendentals=0),
        name="forward_slot",
    )(*args)
    return kept, h


def backward_kernel(
    place, at_ref, g_hbm, u_hbm, w_hbm, view_hbm, gb_hbm, z_hbm, v_hbm, y_hbm, vr_hbm, cr_hbm,
    norm_ref, chan_ref, chanr_ref, head_ref, past_ref, *rest
):
    (
        du_hbm, dz_hbm, dv_hbm, sum_ref,
        g_scr, u_scr, wo_scr, wz_scr, wx_scr, wr_scr, gb_scr, z_scr, v_scr, y_scr, vr_scr, cr_scr, dz_scr, dv_scr,
        dob_scr, dgb_scr, dzp_scr, dvp_scr, c_scr, dy_scr, slope_scr, xl_scr, dyl_scr, q_scr, pull_scr, we_scr, st_scr, ds_scr, bcol_scr, trow_scr, colr_scr, rowr_scr, step_scr, act_scr, dn_scr,
        sem, out_sem,
    ) = rest[-41:]
    groups, rows, _ = dgb_scr.shape
    width = g_scr.shape[1]
    inner = groups * WIDE
    of_group, of_rest = in_copies(view_hbm, wz_scr, wx_scr, wr_scr, sem, 4)
    base = 2 * groups + 7
    g_copy = pltpu.make_async_copy(g_hbm, g_scr, sem.at[0])
    u_copy = pltpu.make_async_copy(u_hbm, u_scr, sem.at[1])
    vr_copy = pltpu.make_async_copy(vr_hbm.at[place], vr_scr, sem.at[2])
    cr_copy = pltpu.make_async_copy(cr_hbm.at[place], cr_scr, sem.at[3])

    def early(j):
        tall = pl.ds(pl.multiple_of(j * WIDE, WIDE), WIDE)
        return [
            pltpu.make_async_copy(w_hbm.at[tall, pl.ds(0, width)], wo_scr.at[j], sem.at[base + j]),
            pltpu.make_async_copy(gb_hbm.at[place, :, lanes(j)], gb_scr.at[j], sem.at[base + 4 * groups + j]),
        ]

    def late(j):
        return of_group(j) + [
            pltpu.make_async_copy(z_hbm.at[place, :, lanes(j)], z_scr.at[j], sem.at[base + groups + j]),
            pltpu.make_async_copy(y_hbm.at[place, :, lanes(j)], y_scr.at[j], sem.at[base + 2 * groups + j]),
            pltpu.make_async_copy(v_hbm.at[place, :, lanes(j)], v_scr.at[j], sem.at[base + 3 * groups + j]),
        ]

    def dz_copy(j):
        return pltpu.make_async_copy(dz_scr.at[j], dz_hbm.at[:, lanes(j)], out_sem.at[j])

    dv_copy = pltpu.make_async_copy(dv_scr, dv_hbm, out_sem.at[groups])
    du_copy = pltpu.make_async_copy(dob_scr, du_hbm, out_sem.at[groups + 1])

    @pl.when(at_ref[1] != 1)
    def _():
        sum_ref[...] = past_ref[...]

    @pl.when(at_ref[1] == 1)
    def _():
        start_all([g_copy, vr_copy, cr_copy])
        for j in range(groups):
            start_all(early(j))
        for j in range(groups):
            start_all(late(j))
        start_all(of_rest() + [u_copy])

        we_scr[...] = jnp.zeros_like(we_scr)
        ds_scr[...] = jnp.zeros_like(ds_scr)
        dn_scr[...] = jnp.zeros_like(dn_scr)
        rowr_scr[...] = jnp.zeros_like(rowr_scr)
        g_copy.wait()
        live = lax.broadcasted_iota(jnp.int32, (rows, 1), 0) < at_ref[0]
        dob_scr[...] = jnp.where(live, g_scr[...].astype(F32), 0.0).astype(BF16)
        cr_copy.wait()
        pre = cr_scr[...]
        act = pre * sigmoid(pre)
        act_scr[...] = act
        st_scr[...] = lax.dot_general(
            act[:, :STATE], act[:, STATE:], (((1,), (1,)), ((), ())), precision=EXACT, preferred_element_type=F32
        )
        vr_copy.wait()
        step, rate, sums, shifted = step_terms(vr_scr[:, 2 * STATE : 3 * STATE], head_ref)
        step_scr[...] = step
        spread(bcol_scr, shifted, groups)
        trow_scr[...] = sums.T

        def first_pass(j, carry):
            wait_all(early(j))
            for half in range(2):
                wide = slice(half * 2 * HALF, (half + 1) * 2 * HALF)
                dgb = nt_dot(dob_scr[...], wo_scr[j, wide, :])
                dgb_scr[j, :, wide] = dgb
                for at in range(0, rows, CHUNK):
                    at = slice(at, at + CHUNK)
                    product = dgb[at] * gb_scr[j, at, wide].astype(F32)
                    we_scr[at, :] += product[:, :HALF] + product[:, HALF:]
            return carry

        lax.fori_loop(0, groups, first_pass, 0)

        def second_pass(j, carry):
            wait_all(late(j))
            taps = chan_ref[:, lanes(j)]
            past = past_ref[:, lanes(j)]
            before = jnp.maximum(j - 1, 0)
            cols = bcol_scr[j]
            head_rows = pl.ds(pl.multiple_of(j * GROUP, GROUP), GROUP)
            rws = trow_scr[head_rows, :]
            lane = lax.broadcasted_iota(jnp.int32, (HALF, HALF), 1)
            causal = lane >= lax.broadcasted_iota(jnp.int32, (HALF, HALF), 0)
            first = lane < HEAD_DIM
            lane_row = lax.broadcasted_iota(jnp.int32, (1, HALF), 1)
            sub = lax.broadcasted_iota(jnp.int32, (GROUP, HALF), 0)
            blocks = rows // HALF
            pairs = GROUP // 2
            col_sums = [jnp.zeros((HALF, HALF), F32) for _ in range(blocks)]
            row_sums = [jnp.zeros((GROUP, HALF), F32) for _ in range(blocks)]
            for pair in range(pairs):
                here = slice(pair * HALF, (pair + 1) * HALF)
                col = pl.ds(pl.multiple_of(j * WIDE + pair * HALF, HALF), HALF)
                share = slice(pair * (width // pairs), (pair + 1) * (width // pairs))
                dn_scr[:, share] += nt_dot(dzp_scr[...], piece_of(wz_scr, before, pair, pairs)) + nt_dot(
                    dvp_scr[...], piece_of(wx_scr, before, pair, pairs)
                )
                c_scr[...] = conv_rows(v_scr[j, :, here], taps[0:4, here], taps[4:5, here])
                gate_sum = jnp.zeros((SUB, HALF), F32)
                skip_sum = jnp.zeros((SUB, HALF), F32)
                for at in range(0, rows, CHUNK):
                    at = slice(at, at + CHUNK)
                    q = q_scr[at, :]
                    dgb = dgb_scr[j, at, here]
                    z = z_scr[j, at, here]
                    y = y_scr[j, at, here]
                    sz = sigmoid(z)
                    silu_z = z * sz
                    w = y * silu_z
                    scaled = q * dgb
                    dw = scaled * taps[5:6, here] - w * pull_scr[at, :]
                    gate_sum = gate_sum + fewer(w * scaled)
                    dy = dw * silu_z
                    dy_scr[at, :] = dy
                    dyl_scr[at, :] = dy.astype(BF16)
                    dz_scr[j, at, here] = (dw * y * (sz + silu_z * (1.0 - sz))).astype(BF16)
                    c = c_scr[at, :]
                    sc = sigmoid(c)
                    x = c * sc
                    xl_scr[at, :] = x.astype(BF16)
                    slope_scr[at, :] = sc + x * (1.0 - sc)
                    skip_sum = skip_sum + fewer(dy * x)
                sum_ref[5:6, col] = past[5:6, here] + jnp.sum(gate_sum, axis=0, keepdims=True)
                sum_ref[6:7, col] = past[6:7, here] + jnp.sum(skip_sum, axis=0, keepdims=True)

                pieces = []
                row_part = [[None] * blocks, [None] * blocks]
                for sb in range(blocks):
                    s_here = slice(sb * HALF, (sb + 1) * HALF)
                    x_here = xl_scr[s_here, :]
                    none = jnp.zeros_like(x_here)
                    split = jnp.concatenate([jnp.where(first, x_here, none), jnp.where(first, none, x_here)], axis=0)
                    meets = nt_dot(split, dyl_scr[sb * HALF :, :])
                    mixes = [[], []]
                    lane_sum = [None, None]
                    for tb in range(sb, blocks):
                        t_here = slice(tb * HALF, (tb + 1) * HALF)
                        contact = st_scr[s_here, t_here]
                        touched = None
                        for k in range(2):
                            h = 2 * pair + k
                            gap = rws[h : h + 1, t_here] - cols[s_here, h : h + 1]
                            if sb == tb:
                                gap = jnp.where(causal, gap, NEG)
                            decay = jnp.exp2(gap)
                            meet = meets[k * HALF : (k + 1) * HALF, (tb - sb) * HALF : (tb - sb + 1) * HALF]
                            through = decay * meet
                            both = through * contact
                            touched = through if touched is None else touched + through
                            mixes[k].append((decay * contact).astype(BF16))
                            lane_sum[k] = both if lane_sum[k] is None else lane_sum[k] + both
                            falling = fewer(both)
                            row_part[k][tb] = falling if row_part[k][tb] is None else row_part[k][tb] + falling
                        ds_scr[s_here, t_here] += touched
                    mix = jnp.concatenate([jnp.concatenate(m, axis=1) if len(m) > 1 else m[0] for m in mixes], axis=0)
                    out = nn_dot(mix, dyl_scr[sb * HALF :, :])
                    for k in range(2):
                        total = jnp.sum(lane_sum[k], axis=1, keepdims=True)
                        col_sums[sb] = jnp.where(lane_row == 2 * pair + k, total, col_sums[sb])
                    pieces.append(jnp.where(first, out[:HALF], out[HALF:]))
                for k in range(2):
                    for tb in range(blocks):
                        total = jnp.sum(row_part[k][tb], axis=0, keepdims=True)
                        row_sums[tb] = jnp.where(sub == 2 * pair + k, total, row_sums[tb])
                dx = jnp.concatenate(pieces, axis=0)
                dc = (dx + taps[6:7, here] * dy_scr[...]) * slope_scr[...]
                dv, tap_sums = conv_back(dc, v_scr[j, :, here], taps[:, here])
                dv_scr[:, col] = dv.astype(BF16)
                for row, one in enumerate(tap_sums):
                    sum_ref[row : row + 1, col] = past[row : row + 1, here] + one
            colr_scr[j] = jnp.concatenate(col_sums, axis=0)
            rowr_scr[head_rows, :] = jnp.concatenate(row_sums, axis=1)
            dzp_scr[...] = dz_scr[j]
            dvp_scr[...] = dv_scr[:, lanes(j)]
            dz_copy(j).start()
            return carry

        for at in range(0, rows, CHUNK):
            at = slice(at, at + CHUNK)
            q = vr_scr[at, 3 * STATE - 1 :]
            pull = q * q * (jnp.sum(we_scr[at, :], axis=1, keepdims=True) * (1.0 / inner))
            q_scr[at, :] = jnp.broadcast_to(q, (CHUNK, HALF))
            pull_scr[at, :] = jnp.broadcast_to(pull, (CHUNK, HALF))
        dzp_scr[...] = jnp.zeros_like(dzp_scr)
        dvp_scr[...] = jnp.zeros_like(dvp_scr)
        lax.fori_loop(0, groups, second_pass, 0)
        dn_scr[...] += nt_dot(dzp_scr[...], fold(wz_scr[groups - 1])) + nt_dot(dvp_scr[...], fold(wx_scr[groups - 1]))
        act = act_scr[...]
        ds = ds_scr[...].astype(BF16)
        act_low = act.astype(BF16)
        d_b = nn_dot(ds, act_low[:, STATE:])
        d_c = lax.dot_general(ds, act_low[:, :STATE], (((0,), (0,)), ((), ())), preferred_element_type=F32)
        pre = cr_scr[...]
        sp = sigmoid(pre)
        d_pre = jnp.concatenate([d_b, d_c], axis=1) * (sp * (1.0 + pre * (1.0 - sp)))
        narrow = slice(inner, inner + 2 * STATE)
        d_raw, tap_sums = conv_back(d_pre, vr_scr[:, : 2 * STATE], chanr_ref[...])
        for row, one in enumerate(tap_sums):
            sum_ref[row : row + 1, narrow] = past_ref[row : row + 1, narrow] + one
        sum_ref[5:7, narrow] = jnp.zeros((2, 2 * STATE), F32)
        col_total = colr_scr[0]
        for g in range(1, groups):
            col_total = col_total + pltpu.roll(colr_scr[g], g * GROUP, 1)
        d_sums = rowr_scr[...].T - col_total
        at_row = lax.broadcasted_iota(jnp.int32, (rows, rows), 0)
        of_row = lax.broadcasted_iota(jnp.int32, (rows, rows), 1)
        upper = (of_row >= at_row).astype(F32)
        d_log = jnp.dot(upper, d_sums, precision=EXACT, preferred_element_type=F32)
        step = step_scr[...]
        rate = -jnp.exp(head_ref[1:2, :])
        d_step = col_total / step + rate * d_log
        raw_step = vr_scr[:, 2 * STATE : 3 * STATE] + head_ref[0:1, :]
        used = lax.broadcasted_iota(jnp.int32, (rows, HALF), 1) < inner // HEAD_DIM
        d_raw_step = jnp.where(used, d_step * jax.nn.sigmoid(raw_step), 0.0)
        last = past_ref[7:8, :]
        sum_ref[7:8, width : width + HALF] = last[:, width : width + HALF] + jnp.sum(d_raw_step, axis=0, keepdims=True)
        sum_ref[7:8, width + HALF : width + 2 * HALF] = last[:, width + HALF : width + 2 * HALF] + jnp.sum(
            jnp.where(used, d_log * step * rate, 0.0), axis=0, keepdims=True
        )
        sum_ref[7:8, width + 2 * HALF :] = jnp.zeros((1, inner - width), F32)
        dr = jnp.concatenate([d_raw, d_raw_step], axis=1).astype(BF16)
        dv_scr[:, inner:] = dr
        dv_copy.start()
        wait_all(of_rest())
        for k in range(3):
            dn_scr[...] += nt_dot(dr[:, k * STATE : (k + 1) * STATE], fold(wr_scr[k]))
        u_copy.wait()
        norm_sum = jnp.zeros((SUB, width), F32)
        for at in range(0, rows, 16):
            at = slice(at, at + 16)
            u = u_scr[at, :].astype(F32)
            dn = dn_scr[at, :]
            p = lax.rsqrt(jnp.mean(u * u, axis=1, keepdims=True) + EPS)
            e = dn * norm_ref[...]
            du = g_scr[at, :].astype(F32) + p * e - u * (p * p * p * jnp.mean(u * e, axis=1, keepdims=True))
            dob_scr[at, :] = du.astype(BF16)
            norm_sum = norm_sum + fewer(u * p * dn)
        du_copy.start()
        sum_ref[7:8, :width] = last[:, :width] + jnp.sum(norm_sum, axis=0, keepdims=True)
        for j in range(groups):
            dz_copy(j).wait()
        dv_copy.wait()
        du_copy.wait()


def conv_back(dc, values, taps):
    total, sums = 0.0, [None] * CONV
    for ahead in range(CONV):
        moved = down(dc, -ahead) if ahead else dc
        tap = CONV - 1 - ahead
        total = total + taps[tap : tap + 1, :] * moved
        sums[tap] = jnp.sum(fewer(moved * values), axis=0, keepdims=True)
    return total, sums + [jnp.sum(fewer(dc), axis=0, keepdims=True)]


def backward_slot(place, numbers, kept, grads, past, g, u, w_all, view, norm_gain, chan, chan_r, heads):
    rows, width = g.shape
    inner = chan.shape[1]
    groups = inner // WIDE
    parts, _, depth, _ = view.shape
    far = pl.BlockSpec(memory_space=pl.ANY)
    near = pl.BlockSpec(memory_space=pltpu.VMEM)
    args = [numbers, g, u, w_all, view, *kept, norm_gain, chan, chan_r, heads, past]
    in_specs = [pl.BlockSpec(memory_space=pltpu.SMEM)] + [far] * 10 + [near] * 5
    aliases = {}
    if grads is not None:
        for k, arr in enumerate(grads):
            aliases[len(args)] = k + 1
            args.append(arr)
            in_specs.append(far)
    tall = pltpu.VMEM((groups, parts, depth, WIDE), BF16)
    wide = pltpu.VMEM((groups, rows, WIDE), F32)
    slot = pltpu.VMEM((rows, width), BF16)
    return pl.pallas_call(
        functools.partial(backward_kernel, place),
        in_specs=in_specs,
        out_specs=[far, far, far, near],
        out_shape=[
            jax.ShapeDtypeStruct((rows, width), BF16),
            jax.ShapeDtypeStruct((rows, inner), BF16),
            jax.ShapeDtypeStruct((rows, inner + 3 * STATE), BF16),
            jax.ShapeDtypeStruct((8, inner + 2 * STATE), F32),
        ],
        scratch_shapes=[
            slot,
            slot,
            pltpu.VMEM((groups, WIDE, width), BF16),
            tall,
            tall,
            pltpu.VMEM((3, parts, depth, HALF), BF16),
            pltpu.VMEM((groups, rows, WIDE), BF16),
            wide,
            wide,
            wide,
            pltpu.VMEM((rows, 3 * STATE), F32),
            pltpu.VMEM((rows, 2 * STATE), F32),
            pltpu.VMEM((groups, rows, WIDE), BF16),
            pltpu.VMEM((rows, inner + 3 * STATE), BF16),
            slot,
            wide,
            pltpu.VMEM((rows, WIDE), BF16),
            pltpu.VMEM((rows, WIDE), BF16),
            pltpu.VMEM((rows, HALF), F32),
            pltpu.VMEM((rows, HALF), F32),
            pltpu.VMEM((rows, HALF), F32),
            pltpu.VMEM((rows, HALF), BF16),
            pltpu.VMEM((rows, HALF), BF16),
            pltpu.VMEM((rows, HALF), F32),
            pltpu.VMEM((rows, HALF), F32),
            pltpu.VMEM((rows, HALF), F32),
            pltpu.VMEM((rows, rows), F32),
            pltpu.VMEM((rows, rows), F32),
            pltpu.VMEM((groups, rows, HALF), F32),
            pltpu.VMEM((HALF, rows), F32),
            pltpu.VMEM((groups, rows, HALF), F32),
            pltpu.VMEM((HALF, rows), F32),
            pltpu.VMEM((rows, HALF), F32),
            pltpu.VMEM((rows, 2 * STATE), F32),
            pltpu.VMEM((rows, width), F32),
            pltpu.SemaphoreType.DMA((7 * groups + 7,)),
            pltpu.SemaphoreType.DMA((groups + 2,)),
        ],
        input_output_aliases=aliases,
        compiler_params=pltpu.CompilerParams(vmem_limit_bytes=VMEM),
        cost_estimate=pl.CostEstimate(flops=10**9, bytes_accessed=10**6, transcendentals=0),
        name="backward_slot",
    )(*args)


def pack_kernel(inner, in_ref, out_ref, packed_ref):
    depth, width = in_ref.shape[0], out_ref.shape[1]
    mid, end = 2 * inner + 2 * STATE, in_ref.shape[1]
    packed_ref[:, :width] = out_ref[...]
    tail = width + inner
    for half in range(2):
        rows = slice(half * depth, (half + 1) * depth)
        packed_ref[rows, width:tail] = in_ref[:, half * inner : (half + 1) * inner]
        packed_ref[rows, tail : tail + STATE] = in_ref[:, mid - 2 * STATE + half * STATE : mid - STATE + half * STATE]
        packed_ref[rows, tail + STATE :] = jnp.zeros((depth, STATE), BF16)
    packed_ref[:depth, tail + STATE : tail + STATE + end - mid] = in_ref[:, mid:]


def pack(in_shard, out_shard, inner):
    depth, width = in_shard.shape[0], out_shard.shape[1]
    return pl.pallas_call(
        functools.partial(pack_kernel, inner),
        out_shape=jax.ShapeDtypeStruct((2 * depth, width + inner + 2 * STATE), BF16),
        name="pack",
    )(in_shard, out_shard)


def order_kernel(at_ref, a_ref, own_ref, other_ref, turn_scr):
    turn_scr[...] = a_ref[0].astype(F32).T.reshape(turn_scr.shape)
    for part in range(2):
        for line in range(own_ref.shape[2]):
            own_ref[part, 0, line] = turn_scr[4 * line + at_ref[1 + 2 * part]].astype(BF16)
            other_ref[part, 0, line] = turn_scr[4 * line + at_ref[2 + 2 * part]].astype(BF16)


def by_owner(numbers, values, micro, count):
    _, rows, total = values.shape
    depth = total // count
    line = count // 4
    out = pl.BlockSpec((2, 1, line, depth, rows), lambda i, n: (0, i, 0, 0, 0))
    made = jax.ShapeDtypeStruct((2, micro, line, depth, rows), BF16)
    own, other = pl.pallas_call(
        order_kernel,
        grid_spec=pltpu.PrefetchScalarGridSpec(
            num_scalar_prefetch=1,
            grid=(micro,),
            in_specs=[pl.BlockSpec((1, rows, total), lambda i, n: (n[0] + i, 0, 0))],
            out_specs=[out, out],
            scratch_shapes=[pltpu.VMEM((count, depth, rows), F32)],
        ),
        out_shape=[made, made],
        compiler_params=pltpu.CompilerParams(vmem_limit_bytes=VMEM),
        cost_estimate=pl.CostEstimate(flops=3 * 10**9, bytes_accessed=2 * 10**6, transcendentals=0),
        name="by_owner",
    )(numbers, values)
    flat = (2, micro, line * depth, rows)
    return own.reshape(flat), other.reshape(flat)


def outer_kernel(own_ref, sib_ref, *rest):
    rights, outs = rest[:-2], rest[-2:]
    micro = own_ref.shape[1]
    right = jnp.concatenate([ref[...] for ref in rights], axis=0)
    for part, out_ref in enumerate(outs):
        left = jnp.concatenate([ref[part, m] for ref in (own_ref, sib_ref) for m in range(micro)], axis=1)
        out_ref[...] = nn_dot(left, right).astype(BF16)


def outer_sum(own, sib, rights, start, stop, block):
    _, micro, high, rows = own.shape
    low, steps = start // block, (stop - start) // block
    full = pl.BlockSpec(own.shape, lambda i: (0, 0, 0, 0))
    out = pl.BlockSpec((high, block), lambda i: (0, i))
    made = jax.ShapeDtypeStruct((high, stop - start), BF16)
    return pl.pallas_call(
        outer_kernel,
        grid=(steps,),
        in_specs=[full, full] + [pl.BlockSpec((rows, block), lambda i: (0, low + i)) for _ in rights],
        out_specs=[out, out],
        out_shape=[made, made],
        compiler_params=pltpu.CompilerParams(vmem_limit_bytes=VMEM),
        cost_estimate=pl.CostEstimate(flops=10**9, bytes_accessed=10**6, transcendentals=0),
        name="outer_sum",
    )(own, sib, *rights)


def pick(values, index, axis):
    return lax.dynamic_index_in_dim(values, index, axis, keepdims=False)


def swap(values, axis, bit):
    return lax.ppermute(values, axis, [(a, a ^ bit) for a in range(lax.axis_size(axis))])


def all_rows_of(row, axis):
    count = lax.axis_size(axis)
    place = lax.axis_index(axis)
    table = jnp.where(jnp.arange(count, dtype=jnp.int32)[:, None] == place, row[None], jnp.zeros((), row.dtype))
    bit = 1
    while bit < count:
        table = table + swap(table, axis, bit)
        bit *= 2
    return table


def owned_sums(chunks, axis, rider, ahead):
    count = lax.axis_size(axis)
    length = count // 4
    results, token = [], None
    rider_far = swap(rider, axis, 2)
    for k, (keep, far) in enumerate(chunks):
        rides = k == len(chunks) - 1
        if token is not None:
            far, _ = lax.optimization_barrier((far, token))
        if rides:
            far, rider_far = lax.optimization_barrier((far, rider_far))
            rider = rider + rider_far
        if k == 0:
            far, _ = lax.optimization_barrier((far, ahead[0]))
        terms = [a.reshape(length, -1, a.shape[1]) for a in (keep, far)]
        bit = 1
        while bit < length:
            mine = (lax.axis_index(axis) // (4 * bit)) % 2
            half = lambda a, which: pick(a.reshape((-1, 2) + a.shape[1:]), which, 1)
            sent = sum(half(a, 1 - mine).astype(F32) for a in terms).astype(BF16)
            if rides:
                sent, rider = lax.optimization_barrier((sent, rider))
            if k == 0 and bit > 1:
                sent, _ = lax.optimization_barrier((sent, ahead[1:]))
            came = swap(sent, axis, 4 * bit)
            if rides:
                rider = rider + swap(rider, axis, 4 * bit)
            terms = [half(a, mine) for a in terms] + [came]
            token = came if k == 0 else sent
            bit *= 2
        results.append(sum(a[0].astype(F32) for a in terms))
    return results, rider


def body(
    block_input,
    cotangent,
    lengths,
    in_weight,
    out_weight,
    conv_weight,
    conv_bias,
    norm_gain,
    gate_gain,
    dt_bias,
    a_log,
    skip_d,
):
    axis = "fsdp"
    count = lax.axis_size(axis)
    section = lax.axis_index("section")
    micro, rows, width = block_input.shape
    depth, proj_cols = in_weight.shape[1:]
    inner = gate_gain.shape[1] * count
    channels = conv_bias.shape[1] * count
    heads = dt_bias.shape[1]
    small = [a.reshape(-1) for a in (conv_weight[0], conv_bias[0], norm_gain[0], gate_gain[0])]
    sizes = [a.shape[0] for a in small]
    w_all = lax.all_gather(pack(in_weight[0], out_weight[0], inner), axis, axis=0, tiled=True)
    view = w_all.reshape(count, 2, depth, -1)
    if depth % 16:
        view = view.transpose(1, 0, 2, 3).reshape(1, 2, width, -1)
    flat = all_rows_of(jnp.concatenate(small), axis).astype(F32)
    cuts = [0]
    for size in sizes:
        cuts.append(cuts[-1] + size)
    taps = flat[:, cuts[0] : cuts[1]].reshape(count, CONV, -1).transpose(1, 0, 2).reshape(CONV, channels)
    bias = flat[:, cuts[1] : cuts[2]].reshape(1, channels)
    norm = flat[:, cuts[2] : cuts[3]].reshape(1, width)
    gate = flat[:, cuts[3] : cuts[4]].reshape(1, inner)
    skip = jnp.repeat(skip_d[0], HEAD_DIM)[None]
    chan = jnp.concatenate([taps[:, :inner], bias[:, :inner], gate, skip, jnp.zeros((1, inner), F32)], axis=0)
    chan_r = jnp.concatenate([taps[:, inner:], bias[:, inner:], jnp.zeros((3, channels - inner), F32)], axis=0)
    head_rows = jnp.pad(jnp.stack([dt_bias[0], a_log[0]]), ((0, 6), (0, HALF - heads)))
    places = jnp.arange(rows, dtype=jnp.int32)
    live = [(places < lengths[m, 0])[:, None] for m in range(micro)]

    def numbers(m, stage):
        return jnp.stack([lengths[m, 0], (section == stage).astype(jnp.int32)])

    kept = None
    first, second = [], []
    for m in range(micro):
        kept, h = forward_slot(
            m, numbers(m, 0), kept, block_input[m], w_all, view, norm, chan, chan_r, head_rows, gate, 2 * micro
        )
        first.append(h)
    arrived = [lax.ppermute(h, "section", [(0, 1)]) for h in first]
    for m in range(micro):
        kept, h = forward_slot(
            micro + m, numbers(m, 1), kept, arrived[m], w_all, view, norm, chan, chan_r, head_rows, gate, 2 * micro
        )
        second.append(h)
    outputs = jnp.stack([jnp.where(section == 0, a, b) for a, b in zip(first, second)])

    def run_backward(place, m, stage, grads, sums, g, u):
        return backward_slot(
            place, numbers(m, stage), kept[1:], grads, sums, g, u, w_all, view, norm, chan, chan_r, head_rows
        )

    is_last = section == 1
    sums = jnp.zeros((8, inner + 2 * STATE), F32)
    grads, late_grads, early_grads, returned = [None] * micro, [None] * micro, [None] * micro, [None] * micro
    for m in reversed(range(micro)):
        late_grads[m], *grads[m], sums = run_backward(micro + m, m, 1, None, sums, cotangent[m], arrived[m])
        returned[m] = lax.ppermute(late_grads[m], "section", [(1, 0)])

    mine = (lax.axis_index(axis) % 4).astype(jnp.int32)
    owners = jnp.stack([section * micro, mine, mine ^ 1, mine ^ 2, mine ^ 3]).astype(jnp.int32)
    nb, gb, _ = lax.optimization_barrier((kept[0], kept[1], late_grads[0]))
    out_own, out_other = by_owner(owners, gb, micro, count)
    in_own, in_other = by_owner(owners, nb, micro, count)
    out_sib, in_sib = swap(out_other, axis, 1), swap(in_other, axis, 1)
    returned[-1], out_own, in_own = lax.optimization_barrier((returned[-1], out_own, in_own))

    branch, branch_sib, z_sib, v_sib = [None] * micro, [None] * micro, [None] * micro, [None] * micro

    def take_branch(m):
        branch[m] = jnp.where(live[m], jnp.where(is_last, cotangent[m], returned[m]), jnp.zeros((), BF16))
        branch_sib[m] = swap(branch[m], axis, 1)

    for m in reversed(range(1, micro)):
        take_branch(m)
        early_grads[m], *grads[m], sums = run_backward(m, m, 0, grads[m], sums, returned[m], block_input[m])
        z_sib[m], v_sib[m] = (swap(a, axis, 1) for a in grads[m])
    returned[0], early_grads[-1] = lax.optimization_barrier((returned[0], early_grads[-1]))
    take_branch(0)
    out_keep, out_send = outer_sum(out_own, out_sib, branch + branch_sib, 0, width, WIDE)
    returned[0], out_send = lax.optimization_barrier((returned[0], out_send))
    out_far = swap(out_send, axis, 2)
    early_grads[0], *grads[0], sums = run_backward(0, 0, 0, grads[0], sums, returned[0], block_input[0])
    z_sib[0], v_sib[0] = (swap(a, axis, 1) for a in grads[0])
    input_grads = jnp.stack([jnp.where(is_last, a, b) for a, b in zip(late_grads, early_grads)])

    z_rows = [a for a, _ in grads] + z_sib
    v_rows = [a for _, a in grads] + v_sib
    cut, block, end = 5 * 384, 384, inner + 3 * STATE
    pairs = [
        outer_sum(in_own, in_sib, z_rows, 0, inner, 2 * WIDE),
        outer_sum(in_own, in_sib, v_rows, 0, cut, 640),
    ]
    pairs += [outer_sum(in_own, in_sib, v_rows, a, a + 2 * block, block) for a in range(cut, end, 2 * block)]
    pairs[0], out_far = lax.optimization_barrier((pairs[0], out_far))
    sums, _ = lax.optimization_barrier((sums, pairs[-1][1]))
    sums = sums + swap(sums, axis, 1)
    chunks = [(out_keep, out_far)] + [(keep, swap(send, axis, 2)) for keep, send in pairs]
    parts, sums = owned_sums(chunks, axis, sums, [send for _, send in pairs[1:]])
    out_grad, in_grad = parts[0], jnp.concatenate(parts[1:], axis=1)[:, :proj_cols]

    place = lax.axis_index(axis)
    cut_out = lambda row, size: lax.dynamic_slice(sums, (row, place * size), (1, size))
    taps_g = lax.dynamic_slice(sums, (0, place * (channels // count)), (CONV, channels // count))
    skip_g = sums[6, :inner].reshape(heads, HEAD_DIM).sum(axis=1)
    return (
        outputs[None],
        input_grads[None],
        in_grad[None],
        out_grad[None],
        taps_g[None],
        cut_out(4, channels // count),
        cut_out(7, width // count),
        cut_out(5, inner // count),
        sums[7:8, width : width + heads],
        sums[7:8, width + HALF : width + HALF + heads],
        skip_g[None],
    )


def solution(mesh):
    in_specs = (
        P(None, "fsdp", None),
        P(None, "fsdp", None),
        P(None, "fsdp"),
        P("section", "fsdp", None),
        P("section", "fsdp", None),
        P("section", None, "fsdp"),
        P("section", "fsdp"),
        P("section", "fsdp"),
        P("section", "fsdp"),
        P("section", None),
        P("section", None),
        P("section", None),
    )
    out_specs = (
        P("section", None, "fsdp", None),
        P("section", None, "fsdp", None),
        P("section", "fsdp", None),
        P("section", "fsdp", None),
        P("section", None, "fsdp"),
        P("section", "fsdp"),
        P("section", "fsdp"),
        P("section", "fsdp"),
        P("section", None),
        P("section", None),
        P("section", None),
    )
    return jax.shard_map(body, mesh=mesh, in_specs=in_specs, out_specs=out_specs, check_vma=False)
```

```python
import functools

import jax
import jax.numpy as jnp
from jax import lax
from jax.experimental import pallas as pl
from jax.experimental.pallas import tpu as pltpu
from jax.sharding import PartitionSpec as P

HEAD_DIM = 64
STATE = 128
CONV = 4
EPS = 1e-05
LOG2E = 1.4426950408889634
HALF = 128
WIDE = 512
GROUP = WIDE // HEAD_DIM
TINY = 1e-30
SUB = 8
CHUNK = 64
NEG = -1e30
VMEM = 60 * 1024 * 1024
F32 = jnp.float32
BF16 = jnp.bfloat16
EXACT = lax.Precision.HIGHEST


def nt_dot(a, b):
    return lax.dot_general(a, b, (((1,), (1,)), ((), ())), preferred_element_type=F32)


def nn_dot(a, b):
    return jnp.dot(a, b, preferred_element_type=F32)


def sigmoid(v):
    return 0.5 * jnp.tanh(0.5 * v) + 0.5


def down(values, steps):
    count = values.shape[0]
    moved = pltpu.roll(values, steps % count, 0)
    rows = lax.broadcasted_iota(jnp.int32, (SUB, values.shape[1]), 0)
    if steps > 0:
        return jnp.concatenate([jnp.where(rows >= steps, moved[:SUB], 0.0), moved[SUB:]], axis=0)
    return jnp.concatenate([moved[:-SUB], jnp.where(rows < SUB + steps, moved[-SUB:], 0.0)], axis=0)


def conv_rows(values, taps, bias):
    total = bias + taps[CONV - 1 : CONV, :] * values
    for back in range(1, CONV):
        total = total + taps[CONV - 1 - back : CONV - back, :] * down(values, back)
    return total


def fewer(block):
    total = block[:SUB]
    for at in range(SUB, block.shape[0], SUB):
        total = total + block[at : at + SUB]
    return total


def piece_of(scr, j, piece, pieces):
    _, parts, depth, _ = scr.shape
    if parts % pieces == 0:
        return fold(scr[j, piece * (parts // pieces) : (piece + 1) * (parts // pieces)])
    size = parts * depth // pieces
    return fold(scr[j])[piece * size : (piece + 1) * size]


def softplus(v):
    return jnp.maximum(v, 0.0) + jnp.log1p(jnp.exp(-jnp.abs(v)))


def step_terms(step_raw, head_ref):
    rows = step_raw.shape[0]
    step = jnp.maximum(softplus(step_raw + head_ref[0:1, :]), TINY)
    rate = -jnp.exp(head_ref[1:2, :])
    at = lax.broadcasted_iota(jnp.int32, (rows, rows), 0)
    of = lax.broadcasted_iota(jnp.int32, (rows, rows), 1)
    lower = (at >= of).astype(F32)
    sums = jnp.dot(lower, step * rate, precision=EXACT, preferred_element_type=F32) * LOG2E
    return step, rate, sums, sums - jnp.log2(step)


def spread(target, values, groups):
    for g in range(groups):
        target[g] = pltpu.roll(values, (HALF - g * GROUP) % HALF, 1) if g else values


def fold(block):
    return block.reshape(-1, block.shape[-1])


def lanes(index):
    return pl.ds(pl.multiple_of(index * WIDE, WIDE), WIDE)


def in_copies(view_ref, wz_scr, wx_scr, wr_scr, sem, base):
    parts, _, depth, _ = view_ref.shape
    width, groups = parts * depth, wz_scr.shape[0]
    tail = width + groups * WIDE

    def of_group(j):
        here = pl.ds(pl.multiple_of(width + j * WIDE, WIDE), WIDE)
        return [
            pltpu.make_async_copy(view_ref.at[:, 0, :, here], wz_scr.at[j], sem.at[base + j]),
            pltpu.make_async_copy(view_ref.at[:, 1, :, here], wx_scr.at[j], sem.at[base + groups + j]),
        ]

    def of_rest():
        return [
            pltpu.make_async_copy(view_ref.at[:, half, :, pl.ds(at, HALF)], wr_scr.at[k], sem.at[base + 2 * groups + k])
            for k, (half, at) in enumerate(((0, tail), (1, tail), (0, tail + HALF)))
        ]

    return of_group, of_rest


def start_all(copies):
    for copy in copies:
        copy.start()


def wait_all(copies):
    for copy in copies:
        copy.wait()


def forward_kernel(place, at_ref, u_hbm, w_hbm, view_hbm, norm_ref, chan_ref, chanr_ref, head_ref, gate_ref, *rest):
    (
        nb_hbm, gb_hbm, z_hbm, v_hbm, y_hbm, vr_hbm, cr_hbm, h_hbm,
        u_scr, wz_scr, wx_scr, wr_scr, wo_scr, nb_scr, gb_scr, z_scr, v_scr, y_scr, vr_scr, cr_scr, h_scr,
        w_scr, sq_scr, s_scr, col_scr, row_scr, sem, out_sem,
    ) = rest[-28:]
    groups, rows, _ = w_scr.shape
    of_group, of_rest = in_copies(view_hbm, wz_scr, wx_scr, wr_scr, sem, 1)
    spare = 2 * groups + 4
    u_copy = pltpu.make_async_copy(u_hbm, u_scr, sem.at[0])

    def of_out(k):
        return pltpu.make_async_copy(w_hbm.at[:, lanes(k)], wo_scr.at[k], sem.at[spare + k])

    def kept_copies(j):
        return [
            pltpu.make_async_copy(scr.at[j], hbm.at[place, :, lanes(j)], out_sem.at[k * groups + j])
            for k, (scr, hbm) in enumerate(((z_scr, z_hbm), (v_scr, v_hbm), (y_scr, y_hbm)))
        ]

    last = 3 * groups
    whole_copies = [
        pltpu.make_async_copy(scr, hbm.at[place], out_sem.at[last + k])
        for k, (scr, hbm) in enumerate(((nb_scr, nb_hbm), (gb_scr, gb_hbm), (vr_scr, vr_hbm), (cr_scr, cr_hbm)))
    ]
    h_copy = pltpu.make_async_copy(h_scr, h_hbm, out_sem.at[last + 4])

    @pl.when(at_ref[1] == 1)
    def _():
        u_copy.start()
        start_all(of_rest())
        for j in range(groups):
            start_all(of_group(j))
        for k in range(wo_scr.shape[0]):
            of_out(k).start()

        u_copy.wait()
        u = u_scr[...].astype(F32)
        scale = lax.rsqrt(jnp.mean(u * u, axis=1, keepdims=True) + EPS)
        nb_scr[...] = (u * scale * norm_ref[...]).astype(BF16)
        nb = nb_scr[...]
        wait_all(of_rest())
        raw = jnp.concatenate([nn_dot(nb, fold(wr_scr[0])), nn_dot(nb, fold(wr_scr[1]))], axis=1)
        steps = nn_dot(nb, fold(wr_scr[2]))
        vr_scr[:, : 2 * STATE] = raw
        vr_scr[:, 2 * STATE :] = steps
        pre = conv_rows(raw, chanr_ref[0:4, :], chanr_ref[4:5, :])
        cr_scr[...] = pre
        act = pre * sigmoid(pre)
        s_scr[...] = lax.dot_general(
            act[:, STATE:], act[:, :STATE], (((1,), (1,)), ((), ())), precision=EXACT, preferred_element_type=F32
        )
        _, _, sums, shifted = step_terms(steps, head_ref)
        spread(col_scr, sums, groups)
        row_scr[...] = shifted.T
        sq_scr[...] = jnp.zeros_like(sq_scr)

        def group(j, carry):
            wait_all(of_group(j))
            nb = nb_scr[...]
            z = nn_dot(nb, fold(wz_scr[j]))
            z_scr[j] = z
            v = nn_dot(nb, fold(wx_scr[j]))
            v_scr[j] = v
            taps = chan_ref[:, lanes(j)]
            c = conv_rows(v, taps[0:4, :], taps[4:5, :])
            x = c * sigmoid(c)
            x_low = x.astype(BF16)
            cols = col_scr[j]
            rws = row_scr[pl.ds(pl.multiple_of(j * GROUP, GROUP), GROUP), :]
            lane = lax.broadcasted_iota(jnp.int32, (HALF, HALF), 1)
            causal = lax.broadcasted_iota(jnp.int32, (HALF, HALF), 0) >= lane
            first = lane < HEAD_DIM
            parts = []
            for pair in range(GROUP // 2):
                here = slice(pair * HALF, (pair + 1) * HALF)
                pieces = []
                for tb in range(rows // HALF):
                    t_here = slice(tb * HALF, (tb + 1) * HALF)
                    both = []
                    for h in (2 * pair, 2 * pair + 1):
                        col = cols[t_here, h : h + 1]
                        mix = []
                        for sb in range(tb + 1):
                            s_here = slice(sb * HALF, (sb + 1) * HALF)
                            gap = col - rws[h : h + 1, s_here]
                            if sb == tb:
                                gap = jnp.where(causal, gap, NEG)
                            mix.append((jnp.exp2(gap) * s_scr[t_here, s_here]).astype(BF16))
                        mix = jnp.concatenate(mix, axis=1) if len(mix) > 1 else mix[0]
                        both.append(nn_dot(mix, x_low[: (tb + 1) * HALF, here]))
                    pieces.append(jnp.where(first, both[0], both[1]))
                parts.append(jnp.concatenate(pieces, axis=0))
            y = jnp.concatenate(parts, axis=1) + taps[6:7, :] * x
            y_scr[j] = y
            w = y * (z * sigmoid(z))
            w_scr[j] = w
            sq_scr[...] += jnp.sum(w * w, axis=1, keepdims=True)
            start_all(kept_copies(j))
            return carry

        lax.fori_loop(0, groups, group, 0)
        scale = lax.rsqrt(sq_scr[...] * (1.0 / (groups * WIDE)) + EPS)
        vr_scr[:, 3 * STATE - 1 :] = scale
        for g in range(groups):
            here = slice(g * WIDE, (g + 1) * WIDE)
            gb_scr[:, here] = (w_scr[g] * scale * gate_ref[:, here]).astype(BF16)
        start_all(whole_copies)
        live = lax.broadcasted_iota(jnp.int32, (rows, 1), 0) < at_ref[0]
        for k in range(wo_scr.shape[0]):
            here = slice(k * WIDE, (k + 1) * WIDE)
            of_out(k).wait()
            branch = jnp.where(live, nn_dot(gb_scr[...], wo_scr[k]), 0.0)
            h_scr[:, here] = (u_scr[:, here].astype(F32) + branch).astype(BF16)
        h_copy.start()
        for j in range(groups):
            wait_all(kept_copies(j))
        wait_all(whole_copies)
        h_copy.wait()


def forward_slot(place, numbers, kept, u, w_all, view, norm_gain, chan, chan_r, heads, gate_gain, slots):
    rows, width = u.shape
    inner = chan.shape[1]
    groups = inner // WIDE
    parts, _, depth, _ = view.shape
    shapes = [((rows, width), BF16), ((rows, inner), BF16)] + [((rows, inner), F32)] * 3
    shapes += [((rows, 3 * STATE), F32), ((rows, 2 * STATE), F32)]
    far = pl.BlockSpec(memory_space=pl.ANY)
    near = pl.BlockSpec(memory_space=pltpu.VMEM)
    args = [numbers, u, w_all, view, norm_gain, chan, chan_r, heads, gate_gain]
    in_specs = [pl.BlockSpec(memory_space=pltpu.SMEM), far, far, far] + [near] * 5
    aliases = {}
    if kept is not None:
        for k, arr in enumerate(kept):
            aliases[len(args)] = k
            args.append(arr)
            in_specs.append(far)
    out_shape = [jax.ShapeDtypeStruct((slots,) + s, d) for s, d in shapes]
    tall = pltpu.VMEM((groups, parts, depth, WIDE), BF16)
    wide = pltpu.VMEM((groups, rows, WIDE), F32)
    *kept, h = pl.pallas_call(
        functools.partial(forward_kernel, place),
        in_specs=in_specs,
        out_specs=[far] * 8,
        out_shape=out_shape + [jax.ShapeDtypeStruct((rows, width), BF16)],
        scratch_shapes=[
            pltpu.VMEM((rows, width), BF16),
            tall,
            tall,
            pltpu.VMEM((3, parts, depth, HALF), BF16),
            pltpu.VMEM((width // WIDE, inner, WIDE), BF16),
            pltpu.VMEM((rows, width), BF16),
            pltpu.VMEM((rows, inner), BF16),
            wide,
            wide,
            wide,
            pltpu.VMEM((rows, 3 * STATE), F32),
            pltpu.VMEM((rows, 2 * STATE), F32),
            pltpu.VMEM((rows, width), BF16),
            wide,
            pltpu.VMEM((rows, 1), F32),
            pltpu.VMEM((rows, rows), F32),
            pltpu.VMEM((groups, rows, HALF), F32),
            pltpu.VMEM((HALF, rows), F32),
            pltpu.SemaphoreType.DMA((2 * groups + 4 + width // WIDE,)),
            pltpu.SemaphoreType.DMA((3 * groups + 5,)),
        ],
        input_output_aliases=aliases,
        compiler_params=pltpu.CompilerParams(vmem_limit_bytes=VMEM),
        cost_estimate=pl.CostEstimate(flops=22 * 10**9, bytes_accessed=60 * 10**6, transcendentals=0),
        name="forward_slot",
    )(*args)
    return kept, h


def backward_kernel(
    place, at_ref, g_hbm, u_hbm, w_hbm, view_hbm, gb_hbm, z_hbm, v_hbm, y_hbm, vr_hbm, cr_hbm,
    norm_ref, chan_ref, chanr_ref, head_ref, past_ref, *rest
):
    (
        du_hbm, dz_hbm, dv_hbm, sum_ref,
        g_scr, u_scr, wo_scr, wz_scr, wx_scr, wr_scr, gb_scr, z_scr, v_scr, y_scr, vr_scr, cr_scr, dz_scr, dv_scr,
        dob_scr, dgb_scr, dzp_scr, dvp_scr, c_scr, dy_scr, slope_scr, xl_scr, dyl_scr, q_scr, pull_scr, we_scr, st_scr, ds_scr, bcol_scr, trow_scr, colr_scr, rowr_scr, step_scr, act_scr, dn_scr,
        sem, out_sem,
    ) = rest[-41:]
    groups, rows, _ = dgb_scr.shape
    width = g_scr.shape[1]
    inner = groups * WIDE
    of_group, of_rest = in_copies(view_hbm, wz_scr, wx_scr, wr_scr, sem, 4)
    base = 2 * groups + 7
    g_copy = pltpu.make_async_copy(g_hbm, g_scr, sem.at[0])
    u_copy = pltpu.make_async_copy(u_hbm, u_scr, sem.at[1])
    vr_copy = pltpu.make_async_copy(vr_hbm.at[place], vr_scr, sem.at[2])
    cr_copy = pltpu.make_async_copy(cr_hbm.at[place], cr_scr, sem.at[3])

    def early(j):
        tall = pl.ds(pl.multiple_of(j * WIDE, WIDE), WIDE)
        return [
            pltpu.make_async_copy(w_hbm.at[tall, pl.ds(0, width)], wo_scr.at[j], sem.at[base + j]),
            pltpu.make_async_copy(gb_hbm.at[place, :, lanes(j)], gb_scr.at[j], sem.at[base + 4 * groups + j]),
        ]

    def late(j):
        return of_group(j) + [
            pltpu.make_async_copy(z_hbm.at[place, :, lanes(j)], z_scr.at[j], sem.at[base + groups + j]),
            pltpu.make_async_copy(y_hbm.at[place, :, lanes(j)], y_scr.at[j], sem.at[base + 2 * groups + j]),
            pltpu.make_async_copy(v_hbm.at[place, :, lanes(j)], v_scr.at[j], sem.at[base + 3 * groups + j]),
        ]

    def dz_copy(j):
        return pltpu.make_async_copy(dz_scr.at[j], dz_hbm.at[:, lanes(j)], out_sem.at[j])

    dv_copy = pltpu.make_async_copy(dv_scr, dv_hbm, out_sem.at[groups])
    du_copy = pltpu.make_async_copy(dob_scr, du_hbm, out_sem.at[groups + 1])

    @pl.when(at_ref[1] != 1)
    def _():
        sum_ref[...] = past_ref[...]

    @pl.when(at_ref[1] == 1)
    def _():
        start_all([g_copy, vr_copy, cr_copy])
        for j in range(groups):
            start_all(early(j))
        for j in range(groups):
            start_all(late(j))
        start_all(of_rest() + [u_copy])

        we_scr[...] = jnp.zeros_like(we_scr)
        ds_scr[...] = jnp.zeros_like(ds_scr)
        dn_scr[...] = jnp.zeros_like(dn_scr)
        rowr_scr[...] = jnp.zeros_like(rowr_scr)
        g_copy.wait()
        live = lax.broadcasted_iota(jnp.int32, (rows, 1), 0) < at_ref[0]
        dob_scr[...] = jnp.where(live, g_scr[...].astype(F32), 0.0).astype(BF16)
        cr_copy.wait()
        pre = cr_scr[...]
        act = pre * sigmoid(pre)
        act_scr[...] = act
        st_scr[...] = lax.dot_general(
            act[:, :STATE], act[:, STATE:], (((1,), (1,)), ((), ())), precision=EXACT, preferred_element_type=F32
        )
        vr_copy.wait()
        step, rate, sums, shifted = step_terms(vr_scr[:, 2 * STATE : 3 * STATE], head_ref)
        step_scr[...] = step
        spread(bcol_scr, shifted, groups)
        trow_scr[...] = sums.T

        def first_pass(j, carry):
            wait_all(early(j))
            for half in range(2):
                wide = slice(half * 2 * HALF, (half + 1) * 2 * HALF)
                dgb = nt_dot(dob_scr[...], wo_scr[j, wide, :])
                dgb_scr[j, :, wide] = dgb
                for at in range(0, rows, CHUNK):
                    at = slice(at, at + CHUNK)
                    product = dgb[at] * gb_scr[j, at, wide].astype(F32)
                    we_scr[at, :] += product[:, :HALF] + product[:, HALF:]
            return carry

        lax.fori_loop(0, groups, first_pass, 0)

        def second_pass(j, carry):
            wait_all(late(j))
            taps = chan_ref[:, lanes(j)]
            past = past_ref[:, lanes(j)]
            before = jnp.maximum(j - 1, 0)
            cols = bcol_scr[j]
            head_rows = pl.ds(pl.multiple_of(j * GROUP, GROUP), GROUP)
            rws = trow_scr[head_rows, :]
            lane = lax.broadcasted_iota(jnp.int32, (HALF, HALF), 1)
            causal = lane >= lax.broadcasted_iota(jnp.int32, (HALF, HALF), 0)
            first = lane < HEAD_DIM
            lane_row = lax.broadcasted_iota(jnp.int32, (1, HALF), 1)
            sub = lax.broadcasted_iota(jnp.int32, (GROUP, HALF), 0)
            blocks = rows // HALF
            pairs = GROUP // 2
            col_sums = [jnp.zeros((HALF, HALF), F32) for _ in range(blocks)]
            row_sums = [jnp.zeros((GROUP, HALF), F32) for _ in range(blocks)]
            for pair in range(pairs):
                here = slice(pair * HALF, (pair + 1) * HALF)
                col = pl.ds(pl.multiple_of(j * WIDE + pair * HALF, HALF), HALF)
                share = slice(pair * (width // pairs), (pair + 1) * (width // pairs))
                dn_scr[:, share] += nt_dot(dzp_scr[...], piece_of(wz_scr, before, pair, pairs)) + nt_dot(
                    dvp_scr[...], piece_of(wx_scr, before, pair, pairs)
                )
                c_scr[...] = conv_rows(v_scr[j, :, here], taps[0:4, here], taps[4:5, here])
                gate_sum = jnp.zeros((SUB, HALF), F32)
                skip_sum = jnp.zeros((SUB, HALF), F32)
                for at in range(0, rows, CHUNK):
                    at = slice(at, at + CHUNK)
                    q = q_scr[at, :]
                    dgb = dgb_scr[j, at, here]
                    z = z_scr[j, at, here]
                    y = y_scr[j, at, here]
                    sz = sigmoid(z)
                    silu_z = z * sz
                    w = y * silu_z
                    scaled = q * dgb
                    dw = scaled * taps[5:6, here] - w * pull_scr[at, :]
                    gate_sum = gate_sum + fewer(w * scaled)
                    dy = dw * silu_z
                    dy_scr[at, :] = dy
                    dyl_scr[at, :] = dy.astype(BF16)
                    dz_scr[j, at, here] = (dw * y * (sz + silu_z * (1.0 - sz))).astype(BF16)
                    c = c_scr[at, :]
                    sc = sigmoid(c)
                    x = c * sc
                    xl_scr[at, :] = x.astype(BF16)
                    slope_scr[at, :] = sc + x * (1.0 - sc)
                    skip_sum = skip_sum + fewer(dy * x)
                sum_ref[5:6, col] = past[5:6, here] + jnp.sum(gate_sum, axis=0, keepdims=True)
                sum_ref[6:7, col] = past[6:7, here] + jnp.sum(skip_sum, axis=0, keepdims=True)

                pieces = []
                row_part = [[None] * blocks, [None] * blocks]
                for sb in range(blocks):
                    s_here = slice(sb * HALF, (sb + 1) * HALF)
                    x_here = xl_scr[s_here, :]
                    none = jnp.zeros_like(x_here)
                    split = jnp.concatenate([jnp.where(first, x_here, none), jnp.where(first, none, x_here)], axis=0)
                    meets = nt_dot(split, dyl_scr[sb * HALF :, :])
                    mixes = [[], []]
                    lane_sum = [None, None]
                    for tb in range(sb, blocks):
                        t_here = slice(tb * HALF, (tb + 1) * HALF)
                        contact = st_scr[s_here, t_here]
                        touched = None
                        for k in range(2):
                            h = 2 * pair + k
                            gap = rws[h : h + 1, t_here] - cols[s_here, h : h + 1]
                            if sb == tb:
                                gap = jnp.where(causal, gap, NEG)
                            decay = jnp.exp2(gap)
                            meet = meets[k * HALF : (k + 1) * HALF, (tb - sb) * HALF : (tb - sb + 1) * HALF]
                            through = decay * meet
                            both = through * contact
                            touched = through if touched is None else touched + through
                            mixes[k].append((decay * contact).astype(BF16))
                            lane_sum[k] = both if lane_sum[k] is None else lane_sum[k] + both
                            falling = fewer(both)
                            row_part[k][tb] = falling if row_part[k][tb] is None else row_part[k][tb] + falling
                        ds_scr[s_here, t_here] += touched
                    mix = jnp.concatenate([jnp.concatenate(m, axis=1) if len(m) > 1 else m[0] for m in mixes], axis=0)
                    out = nn_dot(mix, dyl_scr[sb * HALF :, :])
                    for k in range(2):
                        total = jnp.sum(lane_sum[k], axis=1, keepdims=True)
                        col_sums[sb] = jnp.where(lane_row == 2 * pair + k, total, col_sums[sb])
                    pieces.append(jnp.where(first, out[:HALF], out[HALF:]))
                for k in range(2):
                    for tb in range(blocks):
                        total = jnp.sum(row_part[k][tb], axis=0, keepdims=True)
                        row_sums[tb] = jnp.where(sub == 2 * pair + k, total, row_sums[tb])
                dx = jnp.concatenate(pieces, axis=0)
                dc = (dx + taps[6:7, here] * dy_scr[...]) * slope_scr[...]
                dv, tap_sums = conv_back(dc, v_scr[j, :, here], taps[:, here])
                dv_scr[:, col] = dv.astype(BF16)
                for row, one in enumerate(tap_sums):
                    sum_ref[row : row + 1, col] = past[row : row + 1, here] + one
            colr_scr[j] = jnp.concatenate(col_sums, axis=0)
            rowr_scr[head_rows, :] = jnp.concatenate(row_sums, axis=1)
            dzp_scr[...] = dz_scr[j]
            dvp_scr[...] = dv_scr[:, lanes(j)]
            dz_copy(j).start()
            return carry

        for at in range(0, rows, CHUNK):
            at = slice(at, at + CHUNK)
            q = vr_scr[at, 3 * STATE - 1 :]
            pull = q * q * (jnp.sum(we_scr[at, :], axis=1, keepdims=True) * (1.0 / inner))
            q_scr[at, :] = jnp.broadcast_to(q, (CHUNK, HALF))
            pull_scr[at, :] = jnp.broadcast_to(pull, (CHUNK, HALF))
        dzp_scr[...] = jnp.zeros_like(dzp_scr)
        dvp_scr[...] = jnp.zeros_like(dvp_scr)
        lax.fori_loop(0, groups, second_pass, 0)
        dn_scr[...] += nt_dot(dzp_scr[...], fold(wz_scr[groups - 1])) + nt_dot(dvp_scr[...], fold(wx_scr[groups - 1]))
        act = act_scr[...]
        ds = ds_scr[...].astype(BF16)
        act_low = act.astype(BF16)
        d_b = nn_dot(ds, act_low[:, STATE:])
        d_c = lax.dot_general(ds, act_low[:, :STATE], (((0,), (0,)), ((), ())), preferred_element_type=F32)
        pre = cr_scr[...]
        sp = sigmoid(pre)
        d_pre = jnp.concatenate([d_b, d_c], axis=1) * (sp * (1.0 + pre * (1.0 - sp)))
        narrow = slice(inner, inner + 2 * STATE)
        d_raw, tap_sums = conv_back(d_pre, vr_scr[:, : 2 * STATE], chanr_ref[...])
        for row, one in enumerate(tap_sums):
            sum_ref[row : row + 1, narrow] = past_ref[row : row + 1, narrow] + one
        sum_ref[5:7, narrow] = jnp.zeros((2, 2 * STATE), F32)
        col_total = colr_scr[0]
        for g in range(1, groups):
            col_total = col_total + pltpu.roll(colr_scr[g], g * GROUP, 1)
        d_sums = rowr_scr[...].T - col_total
        at_row = lax.broadcasted_iota(jnp.int32, (rows, rows), 0)
        of_row = lax.broadcasted_iota(jnp.int32, (rows, rows), 1)
        upper = (of_row >= at_row).astype(F32)
        d_log = jnp.dot(upper, d_sums, precision=EXACT, preferred_element_type=F32)
        step = step_scr[...]
        rate = -jnp.exp(head_ref[1:2, :])
        d_step = col_total / step + rate * d_log
        raw_step = vr_scr[:, 2 * STATE : 3 * STATE] + head_ref[0:1, :]
        used = lax.broadcasted_iota(jnp.int32, (rows, HALF), 1) < inner // HEAD_DIM
        d_raw_step = jnp.where(used, d_step * jax.nn.sigmoid(raw_step), 0.0)
        last = past_ref[7:8, :]
        sum_ref[7:8, width : width + HALF] = last[:, width : width + HALF] + jnp.sum(d_raw_step, axis=0, keepdims=True)
        sum_ref[7:8, width + HALF : width + 2 * HALF] = last[:, width + HALF : width + 2 * HALF] + jnp.sum(
            jnp.where(used, d_log * step * rate, 0.0), axis=0, keepdims=True
        )
        sum_ref[7:8, width + 2 * HALF :] = jnp.zeros((1, inner - width), F32)
        dr = jnp.concatenate([d_raw, d_raw_step], axis=1).astype(BF16)
        dv_scr[:, inner:] = dr
        dv_copy.start()
        wait_all(of_rest())
        for k in range(3):
            dn_scr[...] += nt_dot(dr[:, k * STATE : (k + 1) * STATE], fold(wr_scr[k]))
        u_copy.wait()
        norm_sum = jnp.zeros((SUB, width), F32)
        for at in range(0, rows, 16):
            at = slice(at, at + 16)
            u = u_scr[at, :].astype(F32)
            dn = dn_scr[at, :]
            p = lax.rsqrt(jnp.mean(u * u, axis=1, keepdims=True) + EPS)
            e = dn * norm_ref[...]
            du = g_scr[at, :].astype(F32) + p * e - u * (p * p * p * jnp.mean(u * e, axis=1, keepdims=True))
            dob_scr[at, :] = du.astype(BF16)
            norm_sum = norm_sum + fewer(u * p * dn)
        du_copy.start()
        sum_ref[7:8, :width] = last[:, :width] + jnp.sum(norm_sum, axis=0, keepdims=True)
        for j in range(groups):
            dz_copy(j).wait()
        dv_copy.wait()
        du_copy.wait()


def conv_back(dc, values, taps):
    total, sums = 0.0, [None] * CONV
    for ahead in range(CONV):
        moved = down(dc, -ahead) if ahead else dc
        tap = CONV - 1 - ahead
        total = total + taps[tap : tap + 1, :] * moved
        sums[tap] = jnp.sum(fewer(moved * values), axis=0, keepdims=True)
    return total, sums + [jnp.sum(fewer(dc), axis=0, keepdims=True)]


def backward_slot(place, numbers, kept, grads, past, g, u, w_all, view, norm_gain, chan, chan_r, heads):
    rows, width = g.shape
    inner = chan.shape[1]
    groups = inner // WIDE
    parts, _, depth, _ = view.shape
    far = pl.BlockSpec(memory_space=pl.ANY)
    near = pl.BlockSpec(memory_space=pltpu.VMEM)
    args = [numbers, g, u, w_all, view, *kept, norm_gain, chan, chan_r, heads, past]
    in_specs = [pl.BlockSpec(memory_space=pltpu.SMEM)] + [far] * 10 + [near] * 5
    aliases = {}
    if grads is not None:
        for k, arr in enumerate(grads):
            aliases[len(args)] = k + 1
            args.append(arr)
            in_specs.append(far)
    tall = pltpu.VMEM((groups, parts, depth, WIDE), BF16)
    wide = pltpu.VMEM((groups, rows, WIDE), F32)
    slot = pltpu.VMEM((rows, width), BF16)
    return pl.pallas_call(
        functools.partial(backward_kernel, place),
        in_specs=in_specs,
        out_specs=[far, far, far, near],
        out_shape=[
            jax.ShapeDtypeStruct((rows, width), BF16),
            jax.ShapeDtypeStruct((rows, inner), BF16),
            jax.ShapeDtypeStruct((rows, inner + 3 * STATE), BF16),
            jax.ShapeDtypeStruct((8, inner + 2 * STATE), F32),
        ],
        scratch_shapes=[
            slot,
            slot,
            pltpu.VMEM((groups, WIDE, width), BF16),
            tall,
            tall,
            pltpu.VMEM((3, parts, depth, HALF), BF16),
            pltpu.VMEM((groups, rows, WIDE), BF16),
            wide,
            wide,
            wide,
            pltpu.VMEM((rows, 3 * STATE), F32),
            pltpu.VMEM((rows, 2 * STATE), F32),
            pltpu.VMEM((groups, rows, WIDE), BF16),
            pltpu.VMEM((rows, inner + 3 * STATE), BF16),
            slot,
            wide,
            pltpu.VMEM((rows, WIDE), BF16),
            pltpu.VMEM((rows, WIDE), BF16),
            pltpu.VMEM((rows, HALF), F32),
            pltpu.VMEM((rows, HALF), F32),
            pltpu.VMEM((rows, HALF), F32),
            pltpu.VMEM((rows, HALF), BF16),
            pltpu.VMEM((rows, HALF), BF16),
            pltpu.VMEM((rows, HALF), F32),
            pltpu.VMEM((rows, HALF), F32),
            pltpu.VMEM((rows, HALF), F32),
            pltpu.VMEM((rows, rows), F32),
            pltpu.VMEM((rows, rows), F32),
            pltpu.VMEM((groups, rows, HALF), F32),
            pltpu.VMEM((HALF, rows), F32),
            pltpu.VMEM((groups, rows, HALF), F32),
            pltpu.VMEM((HALF, rows), F32),
            pltpu.VMEM((rows, HALF), F32),
            pltpu.VMEM((rows, 2 * STATE), F32),
            pltpu.VMEM((rows, width), F32),
            pltpu.SemaphoreType.DMA((7 * groups + 7,)),
            pltpu.SemaphoreType.DMA((groups + 2,)),
        ],
        input_output_aliases=aliases,
        compiler_params=pltpu.CompilerParams(vmem_limit_bytes=VMEM),
        cost_estimate=pl.CostEstimate(flops=10**9, bytes_accessed=10**6, transcendentals=0),
        name="backward_slot",
    )(*args)


def pack_kernel(inner, in_ref, out_ref, packed_ref):
    depth, width = in_ref.shape[0], out_ref.shape[1]
    mid, end = 2 * inner + 2 * STATE, in_ref.shape[1]
    packed_ref[:, :width] = out_ref[...]
    tail = width + inner
    for half in range(2):
        rows = slice(half * depth, (half + 1) * depth)
        packed_ref[rows, width:tail] = in_ref[:, half * inner : (half + 1) * inner]
        packed_ref[rows, tail : tail + STATE] = in_ref[:, mid - 2 * STATE + half * STATE : mid - STATE + half * STATE]
        packed_ref[rows, tail + STATE :] = jnp.zeros((depth, STATE), BF16)
    packed_ref[:depth, tail + STATE : tail + STATE + end - mid] = in_ref[:, mid:]


def pack(in_shard, out_shard, inner):
    depth, width = in_shard.shape[0], out_shard.shape[1]
    return pl.pallas_call(
        functools.partial(pack_kernel, inner),
        out_shape=jax.ShapeDtypeStruct((2 * depth, width + inner + 2 * STATE), BF16),
        name="pack",
    )(in_shard, out_shard)


def order_kernel(at_ref, a_ref, own_ref, other_ref, turn_scr):
    turn_scr[...] = a_ref[0].astype(F32).T.reshape(turn_scr.shape)
    spots = own_ref.shape[1]
    for spot in range(spots):
        own_ref[0, spot] = turn_scr[at_ref[1 + spot]].astype(BF16)
        other_ref[0, spot] = turn_scr[at_ref[1 + spots + spot]].astype(BF16)


def by_owner(table, values, micro):
    _, rows, total = values.shape
    count = table.shape[0] - 1
    depth = total // count
    out = pl.BlockSpec((1, count // 2, depth, rows), lambda i, n: (i, 0, 0, 0))
    made = jax.ShapeDtypeStruct((micro, count // 2, depth, rows), BF16)
    parts = pl.pallas_call(
        order_kernel,
        grid_spec=pltpu.PrefetchScalarGridSpec(
            num_scalar_prefetch=1,
            grid=(micro,),
            in_specs=[pl.BlockSpec((1, rows, total), lambda i, n: (n[0] + i, 0, 0))],
            out_specs=[out, out],
            scratch_shapes=[pltpu.VMEM((count, depth, rows), F32)],
        ),
        out_shape=[made, made],
        compiler_params=pltpu.CompilerParams(vmem_limit_bytes=VMEM),
        cost_estimate=pl.CostEstimate(flops=3 * 10**9, bytes_accessed=2 * 10**6, transcendentals=0),
        name="by_owner",
    )(table, values)
    return [a.reshape(micro, total // 2, rows) for a in parts]


def outer_kernel(with_extra, own_ref, sib_ref, *rest):
    rights, outs = rest[:-2], rest[-2:]
    micro, high = own_ref.shape[0], outs[0].shape[0]
    if with_extra:
        extra_ref, rights = rights[-1], rights[:-1]
    right = jnp.concatenate([ref[...] for ref in rights], axis=0)
    for part, out_ref in enumerate(outs):
        rows = slice(part * high, (part + 1) * high)
        left = jnp.concatenate([ref[m, rows] for ref in (own_ref, sib_ref) for m in range(micro)], axis=1)
        total = nn_dot(left, right)
        out_ref[...] = total.astype(BF16)
        if with_extra:
            extra = extra_ref[rows, :]

            @pl.when(pl.program_id(0) == pl.num_programs(0) - 1)
            def _():
                out_ref[:, -HALF:] = (total[:, -HALF:] + extra).astype(BF16)


def outer_sum(own, sib, rights, start, stop, block, extra=None):
    _, total, rows = own.shape
    low, steps = start // block, (stop - start) // block
    full = pl.BlockSpec(own.shape, lambda i: (0, 0, 0))
    out = pl.BlockSpec((total // 2, block), lambda i: (0, i))
    made = jax.ShapeDtypeStruct((total // 2, stop - start), BF16)
    more = [] if extra is None else [extra]
    return pl.pallas_call(
        functools.partial(outer_kernel, extra is not None),
        grid=(steps,),
        in_specs=[full, full]
        + [pl.BlockSpec((rows, block), lambda i: (0, low + i)) for _ in rights]
        + [pl.BlockSpec(a.shape, lambda i: (0, 0)) for a in more],
        out_specs=[out, out],
        out_shape=[made, made],
        compiler_params=pltpu.CompilerParams(vmem_limit_bytes=VMEM),
        cost_estimate=pl.CostEstimate(flops=10**9, bytes_accessed=10**6, transcendentals=0),
        name="outer_sum",
    )(own, sib, *rights, *more)


def swap(values, axis, bit):
    return lax.ppermute(values, axis, [(a, a ^ bit) for a in range(lax.axis_size(axis))])


def all_rows_of(row, axis):
    count = lax.axis_size(axis)
    place = lax.axis_index(axis)
    table = jnp.where(jnp.arange(count, dtype=jnp.int32)[:, None] == place, row[None], jnp.zeros((), row.dtype))
    bit = 1
    while bit < count:
        table = table + swap(table, axis, bit)
        bit *= 2
    return table


def held(value, *after):
    return lax.optimization_barrier((value, after))[0]


def total_of(terms):
    return sum(a.astype(F32) for a in terms)


def exchange(terms, axis, bit):
    half = terms[0].shape[0] // 2
    sent = total_of([a[half:] for a in terms]).astype(BF16)
    return [a[:half] for a in terms] + [swap(sent, axis, bit)], sent


def spots_of(order):
    return [sum(bit for k, bit in enumerate(order) if p >> (len(order) - 1 - k) & 1) for p in range(2 ** len(order))]


def body(
    block_input,
    cotangent,
    lengths,
    in_weight,
    out_weight,
    conv_weight,
    conv_bias,
    norm_gain,
    gate_gain,
    dt_bias,
    a_log,
    skip_d,
):
    axis = "fsdp"
    count = lax.axis_size(axis)
    section = lax.axis_index("section")
    micro, rows, width = block_input.shape
    depth, proj_cols = in_weight.shape[1:]
    inner = gate_gain.shape[1] * count
    channels = conv_bias.shape[1] * count
    heads = dt_bias.shape[1]
    small = [a.reshape(-1) for a in (conv_weight[0], conv_bias[0], norm_gain[0], gate_gain[0])]
    sizes = [a.shape[0] for a in small]
    w_all = lax.all_gather(pack(in_weight[0], out_weight[0], inner), axis, axis=0, tiled=True)
    view = w_all.reshape(count, 2, depth, -1)
    if depth % 16:
        view = view.transpose(1, 0, 2, 3).reshape(1, 2, width, -1)
    flat = all_rows_of(jnp.concatenate(small), axis).astype(F32)
    cuts = [0]
    for size in sizes:
        cuts.append(cuts[-1] + size)
    taps = flat[:, cuts[0] : cuts[1]].reshape(count, CONV, -1).transpose(1, 0, 2).reshape(CONV, channels)
    bias = flat[:, cuts[1] : cuts[2]].reshape(1, channels)
    norm = flat[:, cuts[2] : cuts[3]].reshape(1, width)
    gate = flat[:, cuts[3] : cuts[4]].reshape(1, inner)
    skip = jnp.repeat(skip_d[0], HEAD_DIM)[None]
    chan = jnp.concatenate([taps[:, :inner], bias[:, :inner], gate, skip, jnp.zeros((1, inner), F32)], axis=0)
    chan_r = jnp.concatenate([taps[:, inner:], bias[:, inner:], jnp.zeros((3, channels - inner), F32)], axis=0)
    head_rows = jnp.pad(jnp.stack([dt_bias[0], a_log[0]]), ((0, 6), (0, HALF - heads)))
    places = jnp.arange(rows, dtype=jnp.int32)
    live = [(places < lengths[m, 0])[:, None] for m in range(micro)]

    def numbers(m, stage):
        return jnp.stack([lengths[m, 0], (section == stage).astype(jnp.int32)])

    kept = None
    first, second = [], []
    for m in range(micro):
        kept, h = forward_slot(
            m, numbers(m, 0), kept, block_input[m], w_all, view, norm, chan, chan_r, head_rows, gate, 2 * micro
        )
        first.append(h)
    arrived = [lax.ppermute(h, "section", [(0, 1)]) for h in first]
    for m in range(micro):
        kept, h = forward_slot(
            micro + m, numbers(m, 1), kept, arrived[m], w_all, view, norm, chan, chan_r, head_rows, gate, 2 * micro
        )
        second.append(h)
    outputs = jnp.stack([jnp.where(section == 0, a, b) for a, b in zip(first, second)])

    def run_backward(place, m, stage, grads, sums, g, u):
        return backward_slot(
            place, numbers(m, stage), kept[1:], grads, sums, g, u, w_all, view, norm, chan, chan_r, head_rows
        )

    is_last = section == 1
    sums = jnp.zeros((8, inner + 2 * STATE), F32)
    grads, late_grads, early_grads, returned = [None] * micro, [None] * micro, [None] * micro, [None] * micro
    for m in reversed(range(micro)):
        late_grads[m], *grads[m], sums = run_backward(micro + m, m, 1, None, sums, cotangent[m], arrived[m])
        returned[m] = lax.ppermute(late_grads[m], "section", [(1, 0)])

    place = lax.axis_index(axis).astype(jnp.int32)
    line = [4 << k for k in range(count.bit_length() - 3)]
    in_order, out_order = [2] + line, line + [2]

    def table_of(order):
        spots = jnp.array(spots_of(order), jnp.int32)
        return jnp.concatenate([(section * micro)[None].astype(jnp.int32), place ^ spots, place ^ 1 ^ spots])

    nb, gb, _ = lax.optimization_barrier((kept[0], kept[1], late_grads[0]))
    out_own, out_other = by_owner(table_of(out_order), gb, micro)
    in_own, in_other = by_owner(table_of(in_order), nb, micro)
    out_sib, in_sib = swap(out_other, axis, 1), swap(in_other, axis, 1)
    returned[-1], out_own, in_own = lax.optimization_barrier((returned[-1], out_own, in_own))

    branch, branch_sib, z_sib, v_sib = [None] * micro, [None] * micro, [None] * micro, [None] * micro

    def take_branch(m):
        branch[m] = jnp.where(live[m], jnp.where(is_last, cotangent[m], returned[m]), jnp.zeros((), BF16))
        branch_sib[m] = swap(branch[m], axis, 1)

    for m in reversed(range(1, micro)):
        take_branch(m)
        early_grads[m], *grads[m], sums = run_backward(m, m, 0, grads[m], sums, returned[m], block_input[m])
        z_sib[m], v_sib[m] = (swap(a, axis, 1) for a in grads[m])
    returned[0], early_grads[-1] = lax.optimization_barrier((returned[0], early_grads[-1]))
    take_branch(0)

    out_keep, out_send = outer_sum(out_own, out_sib, branch + branch_sib, 0, width, WIDE)
    returned[0] = held(returned[0], out_send)
    out_terms = [out_keep, swap(out_send, axis, out_order[0])]
    early_grads[0], *grads[0], sums = run_backward(0, 0, 0, grads[0], sums, returned[0], block_input[0])
    z_sib[0], v_sib[0] = (swap(a, axis, 1) for a in grads[0])
    input_grads = jnp.stack([jnp.where(is_last, a, b) for a, b in zip(late_grads, early_grads)])

    z_rows = [a for a, _ in grads] + z_sib
    v_rows = [a for _, a in grads] + v_sib
    cut, block, end = 5 * 384, 384, inner + 3 * STATE
    z_keep, z_send = outer_sum(in_own, in_sib, z_rows, 0, inner, 2 * WIDE)
    (z_keep, z_send), out_terms[-1] = lax.optimization_barrier(((z_keep, z_send), out_terms[-1]))
    token = z_send
    for bit in out_order[1:-1]:
        out_terms, token = exchange(out_terms, axis, bit)
    sums, v_rows[0] = held((sums, v_rows[0]), token)
    sums = sums + swap(sums, axis, 1)
    per_owner = lambda rows: rows.reshape(-1, count, rows.shape[1] // count).transpose(1, 0, 2).reshape(count, -1)
    skip_g = sums[6, :inner].reshape(heads, HEAD_DIM).sum(axis=1)
    shared = jnp.concatenate([sums[7, width : width + heads], sums[7, width + HALF : width + HALF + heads], skip_g])
    listed = jnp.concatenate(
        [
            per_owner(sums[:CONV]),
            per_owner(sums[CONV : CONV + 1]),
            per_owner(sums[7:8, :width]),
            per_owner(sums[5:6, :inner]),
            jnp.broadcast_to(shared, (count, shared.shape[0])),
        ],
        axis=1,
    )
    listed_cols = -(-listed.shape[1] // depth)
    listed = jnp.pad(listed, ((0, 0), (0, listed_cols * depth - listed.shape[1]))).reshape(count, depth, listed_cols)
    listed = jnp.take(listed, place ^ jnp.array(spots_of(in_order), jnp.int32), axis=0).reshape(width // 2, listed_cols)
    at_lane = (proj_cols - inner) % HALF
    extra = jnp.pad(listed, ((0, 0), (at_lane, HALF - at_lane - listed_cols)))
    mid = end - 2 * block
    pairs = [
        (z_keep, z_send),
        outer_sum(in_own, in_sib, v_rows, 0, cut, 640),
        outer_sum(in_own, in_sib, v_rows, mid, end, block, extra),
        outer_sum(in_own, in_sib, [held(v_rows[0], out_terms[-1])] + v_rows[1:], cut, mid, block),
    ]
    sends = [send for _, send in pairs]
    chunks = [[keep, swap(send, axis, 2)] for keep, send in pairs]
    token, out_came = sends[:-1], out_terms[-1]
    last = len(chunks) - 1

    def first_step(k, token):
        chunks[k][-1] = held(chunks[k][-1], token)
        chunks[k], token = exchange(chunks[k], axis, line[0])
        return token

    def other_steps(k, token):
        for bit in line[1:]:
            chunks[k][-1] = held(chunks[k][-1], token)
            chunks[k], token = exchange(chunks[k], axis, bit)
        return token

    token = first_step(0, token)
    for k in range(1, last):
        token = first_step(k, token)
        token = other_steps(k - 1, (token, out_came) if k == 1 else token)
    token = first_step(last, token)
    out_terms[-1] = held(out_terms[-1], token)
    out_terms, _ = exchange(out_terms, axis, 2)
    token = other_steps(last - 1, token)
    token = other_steps(last, token)
    out_grad = total_of(out_terms)
    in_parts = [total_of(terms) for terms in chunks]
    tail = in_parts[2]
    own_cols = proj_cols - inner - mid
    in_grad = jnp.concatenate([in_parts[0], in_parts[1], in_parts[3], tail[:, :own_cols]], axis=1)
    own_list = tail[:, own_cols : own_cols + listed_cols].reshape(-1)
    cuts = [0]
    for size in sizes + [heads] * 3:
        cuts.append(cuts[-1] + size)
    lists = [own_list[a:b] for a, b in zip(cuts[:-1], cuts[1:])]
    return (
        outputs[None],
        input_grads[None],
        in_grad[None],
        out_grad[None],
        lists[0].reshape(1, CONV, -1),
        *[one[None] for one in lists[1:]],
    )


def solution(mesh):
    in_specs = (
        P(None, "fsdp", None),
        P(None, "fsdp", None),
        P(None, "fsdp"),
        P("section", "fsdp", None),
        P("section", "fsdp", None),
        P("section", None, "fsdp"),
        P("section", "fsdp"),
        P("section", "fsdp"),
        P("section", "fsdp"),
        P("section", None),
        P("section", None),
        P("section", None),
    )
    out_specs = (
        P("section", None, "fsdp", None),
        P("section", None, "fsdp", None),
        P("section", "fsdp", None),
        P("section", "fsdp", None),
        P("section", None, "fsdp"),
        P("section", "fsdp"),
        P("section", "fsdp"),
        P("section", "fsdp"),
        P("section", None),
        P("section", None),
        P("section", None),
    )
    return jax.shard_map(body, mesh=mesh, in_specs=in_specs, out_specs=out_specs, check_vma=False)
```

```python
import functools

import jax
import jax.numpy as jnp
from jax import lax
from jax.experimental import pallas as pl
from jax.experimental.pallas import tpu as pltpu
from jax.sharding import PartitionSpec as P

HEAD_DIM = 64
STATE = 128
CONV = 4
EPS = 1e-05
LOG2E = 1.4426950408889634
HALF = 128
WIDE = 512
GROUP = WIDE // HEAD_DIM
TINY = 1e-30
SUB = 8
CHUNK = 64
NEG = -1e30
VMEM = 60 * 1024 * 1024
F32 = jnp.float32
BF16 = jnp.bfloat16
EXACT = lax.Precision.HIGHEST


def nt_dot(a, b):
    return lax.dot_general(a, b, (((1,), (1,)), ((), ())), preferred_element_type=F32)


def nn_dot(a, b):
    return jnp.dot(a, b, preferred_element_type=F32)


def sigmoid(v):
    return 0.5 * jnp.tanh(0.5 * v) + 0.5


def down(values, steps):
    count = values.shape[0]
    moved = pltpu.roll(values, steps % count, 0)
    rows = lax.broadcasted_iota(jnp.int32, (SUB, values.shape[1]), 0)
    if steps > 0:
        return jnp.concatenate([jnp.where(rows >= steps, moved[:SUB], 0.0), moved[SUB:]], axis=0)
    return jnp.concatenate([moved[:-SUB], jnp.where(rows < SUB + steps, moved[-SUB:], 0.0)], axis=0)


def conv_rows(values, taps, bias):
    total = bias + taps[CONV - 1 : CONV, :] * values
    for back in range(1, CONV):
        total = total + taps[CONV - 1 - back : CONV - back, :] * down(values, back)
    return total


def fewer(block):
    total = block[:SUB]
    for at in range(SUB, block.shape[0], SUB):
        total = total + block[at : at + SUB]
    return total


def piece_of(scr, j, piece, pieces):
    _, parts, depth, _ = scr.shape
    if parts % pieces == 0:
        return fold(scr[j, piece * (parts // pieces) : (piece + 1) * (parts // pieces)])
    size = parts * depth // pieces
    return fold(scr[j])[piece * size : (piece + 1) * size]


def softplus(v):
    return jnp.maximum(v, 0.0) + jnp.log1p(jnp.exp(-jnp.abs(v)))


def step_terms(step_raw, head_ref):
    rows = step_raw.shape[0]
    step = jnp.maximum(softplus(step_raw + head_ref[0:1, :]), TINY)
    rate = -jnp.exp(head_ref[1:2, :])
    at = lax.broadcasted_iota(jnp.int32, (rows, rows), 0)
    of = lax.broadcasted_iota(jnp.int32, (rows, rows), 1)
    lower = (at >= of).astype(F32)
    sums = jnp.dot(lower, step * rate, precision=EXACT, preferred_element_type=F32) * LOG2E
    return step, rate, sums, sums - jnp.log2(step)


def spread(target, values, groups):
    for g in range(groups):
        target[g] = pltpu.roll(values, (HALF - g * GROUP) % HALF, 1) if g else values


def fold(block):
    return block.reshape(-1, block.shape[-1])


def lanes(index):
    return pl.ds(pl.multiple_of(index * WIDE, WIDE), WIDE)


def in_copies(view_ref, wz_scr, wx_scr, wr_scr, sem, base):
    parts, _, depth, _ = view_ref.shape
    width, groups = parts * depth, wz_scr.shape[0]
    tail = width + groups * WIDE

    def of_group(j):
        here = pl.ds(pl.multiple_of(width + j * WIDE, WIDE), WIDE)
        return [
            pltpu.make_async_copy(view_ref.at[:, 0, :, here], wz_scr.at[j], sem.at[base + j]),
            pltpu.make_async_copy(view_ref.at[:, 1, :, here], wx_scr.at[j], sem.at[base + groups + j]),
        ]

    def of_rest():
        return [
            pltpu.make_async_copy(view_ref.at[:, half, :, pl.ds(at, HALF)], wr_scr.at[k], sem.at[base + 2 * groups + k])
            for k, (half, at) in enumerate(((0, tail), (1, tail), (0, tail + HALF)))
        ]

    return of_group, of_rest


def start_all(copies):
    for copy in copies:
        copy.start()


def wait_all(copies):
    for copy in copies:
        copy.wait()


def forward_kernel(place, at_ref, u_hbm, w_hbm, view_hbm, norm_ref, chan_ref, chanr_ref, head_ref, gate_ref, *rest):
    (
        nb_hbm, gb_hbm, z_hbm, v_hbm, y_hbm, vr_hbm, cr_hbm, h_hbm,
        u_scr, wz_scr, wx_scr, wr_scr, wo_scr, nb_scr, gb_scr, z_scr, v_scr, y_scr, vr_scr, cr_scr, h_scr,
        w_scr, sq_scr, s_scr, col_scr, row_scr, sem, out_sem,
    ) = rest[-28:]
    groups, rows, _ = w_scr.shape
    of_group, of_rest = in_copies(view_hbm, wz_scr, wx_scr, wr_scr, sem, 1)
    spare = 2 * groups + 4
    u_copy = pltpu.make_async_copy(u_hbm, u_scr, sem.at[0])

    def of_out(k):
        return pltpu.make_async_copy(w_hbm.at[:, lanes(k)], wo_scr.at[k], sem.at[spare + k])

    def kept_copies(j):
        return [
            pltpu.make_async_copy(scr.at[j], hbm.at[place, :, lanes(j)], out_sem.at[k * groups + j])
            for k, (scr, hbm) in enumerate(((z_scr, z_hbm), (v_scr, v_hbm), (y_scr, y_hbm)))
        ]

    last = 3 * groups
    whole_copies = [
        pltpu.make_async_copy(scr, hbm.at[place], out_sem.at[last + k])
        for k, (scr, hbm) in enumerate(((nb_scr, nb_hbm), (gb_scr, gb_hbm), (vr_scr, vr_hbm), (cr_scr, cr_hbm)))
    ]
    h_copy = pltpu.make_async_copy(h_scr, h_hbm, out_sem.at[last + 4])

    @pl.when(at_ref[1] == 1)
    def _():
        u_copy.start()
        start_all(of_rest())
        for j in range(groups):
            start_all(of_group(j))
        for k in range(wo_scr.shape[0]):
            of_out(k).start()

        u_copy.wait()
        u = u_scr[...].astype(F32)
        scale = lax.rsqrt(jnp.mean(u * u, axis=1, keepdims=True) + EPS)
        nb_scr[...] = (u * scale * norm_ref[...]).astype(BF16)
        nb = nb_scr[...]
        wait_all(of_rest())
        raw = jnp.concatenate([nn_dot(nb, fold(wr_scr[0])), nn_dot(nb, fold(wr_scr[1]))], axis=1)
        steps = nn_dot(nb, fold(wr_scr[2]))
        vr_scr[:, : 2 * STATE] = raw
        vr_scr[:, 2 * STATE :] = steps
        pre = conv_rows(raw, chanr_ref[0:4, :], chanr_ref[4:5, :])
        cr_scr[...] = pre
        act = pre * sigmoid(pre)
        s_scr[...] = lax.dot_general(
            act[:, STATE:], act[:, :STATE], (((1,), (1,)), ((), ())), precision=EXACT, preferred_element_type=F32
        )
        _, _, sums, shifted = step_terms(steps, head_ref)
        spread(col_scr, sums, groups)
        row_scr[...] = shifted.T
        sq_scr[...] = jnp.zeros_like(sq_scr)

        def group(j, carry):
            wait_all(of_group(j))
            nb = nb_scr[...]
            z = nn_dot(nb, fold(wz_scr[j]))
            z_scr[j] = z
            v = nn_dot(nb, fold(wx_scr[j]))
            v_scr[j] = v
            taps = chan_ref[:, lanes(j)]
            c = conv_rows(v, taps[0:4, :], taps[4:5, :])
            x = c * sigmoid(c)
            x_low = x.astype(BF16)
            cols = col_scr[j]
            rws = row_scr[pl.ds(pl.multiple_of(j * GROUP, GROUP), GROUP), :]
            lane = lax.broadcasted_iota(jnp.int32, (HALF, HALF), 1)
            causal = lax.broadcasted_iota(jnp.int32, (HALF, HALF), 0) >= lane
            first = lane < HEAD_DIM
            parts = []
            for pair in range(GROUP // 2):
                here = slice(pair * HALF, (pair + 1) * HALF)
                pieces = []
                for tb in range(rows // HALF):
                    t_here = slice(tb * HALF, (tb + 1) * HALF)
                    both = []
                    for h in (2 * pair, 2 * pair + 1):
                        col = cols[t_here, h : h + 1]
                        mix = []
                        for sb in range(tb + 1):
                            s_here = slice(sb * HALF, (sb + 1) * HALF)
                            gap = col - rws[h : h + 1, s_here]
                            if sb == tb:
                                gap = jnp.where(causal, gap, NEG)
                            mix.append((jnp.exp2(gap) * s_scr[t_here, s_here]).astype(BF16))
                        mix = jnp.concatenate(mix, axis=1) if len(mix) > 1 else mix[0]
                        both.append(nn_dot(mix, x_low[: (tb + 1) * HALF, here]))
                    pieces.append(jnp.where(first, both[0], both[1]))
                parts.append(jnp.concatenate(pieces, axis=0))
            y = jnp.concatenate(parts, axis=1) + taps[6:7, :] * x
            y_scr[j] = y
            w = y * (z * sigmoid(z))
            w_scr[j] = w
            sq_scr[...] += jnp.sum(w * w, axis=1, keepdims=True)
            start_all(kept_copies(j))
            return carry

        lax.fori_loop(0, groups, group, 0)
        scale = lax.rsqrt(sq_scr[...] * (1.0 / (groups * WIDE)) + EPS)
        vr_scr[:, 3 * STATE - 1 :] = scale
        for g in range(groups):
            here = slice(g * WIDE, (g + 1) * WIDE)
            gb_scr[:, here] = (w_scr[g] * scale * gate_ref[:, here]).astype(BF16)
        start_all(whole_copies)
        live = lax.broadcasted_iota(jnp.int32, (rows, 1), 0) < at_ref[0]
        for k in range(wo_scr.shape[0]):
            here = slice(k * WIDE, (k + 1) * WIDE)
            of_out(k).wait()
            branch = jnp.where(live, nn_dot(gb_scr[...], wo_scr[k]), 0.0)
            h_scr[:, here] = (u_scr[:, here].astype(F32) + branch).astype(BF16)
        h_copy.start()
        for j in range(groups):
            wait_all(kept_copies(j))
        wait_all(whole_copies)
        h_copy.wait()


def forward_slot(place, numbers, kept, u, w_all, view, norm_gain, chan, chan_r, heads, gate_gain, slots):
    rows, width = u.shape
    inner = chan.shape[1]
    groups = inner // WIDE
    parts, _, depth, _ = view.shape
    shapes = [((rows, width), BF16), ((rows, inner), BF16)] + [((rows, inner), F32)] * 3
    shapes += [((rows, 3 * STATE), F32), ((rows, 2 * STATE), F32)]
    far = pl.BlockSpec(memory_space=pl.ANY)
    near = pl.BlockSpec(memory_space=pltpu.VMEM)
    args = [numbers, u, w_all, view, norm_gain, chan, chan_r, heads, gate_gain]
    in_specs = [pl.BlockSpec(memory_space=pltpu.SMEM), far, far, far] + [near] * 5
    aliases = {}
    if kept is not None:
        for k, arr in enumerate(kept):
            aliases[len(args)] = k
            args.append(arr)
            in_specs.append(far)
    out_shape = [jax.ShapeDtypeStruct((slots,) + s, d) for s, d in shapes]
    tall = pltpu.VMEM((groups, parts, depth, WIDE), BF16)
    wide = pltpu.VMEM((groups, rows, WIDE), F32)
    *kept, h = pl.pallas_call(
        functools.partial(forward_kernel, place),
        in_specs=in_specs,
        out_specs=[far] * 8,
        out_shape=out_shape + [jax.ShapeDtypeStruct((rows, width), BF16)],
        scratch_shapes=[
            pltpu.VMEM((rows, width), BF16),
            tall,
            tall,
            pltpu.VMEM((3, parts, depth, HALF), BF16),
            pltpu.VMEM((width // WIDE, inner, WIDE), BF16),
            pltpu.VMEM((rows, width), BF16),
            pltpu.VMEM((rows, inner), BF16),
            wide,
            wide,
            wide,
            pltpu.VMEM((rows, 3 * STATE), F32),
            pltpu.VMEM((rows, 2 * STATE), F32),
            pltpu.VMEM((rows, width), BF16),
            wide,
            pltpu.VMEM((rows, 1), F32),
            pltpu.VMEM((rows, rows), F32),
            pltpu.VMEM((groups, rows, HALF), F32),
            pltpu.VMEM((HALF, rows), F32),
            pltpu.SemaphoreType.DMA((2 * groups + 4 + width // WIDE,)),
            pltpu.SemaphoreType.DMA((3 * groups + 5,)),
        ],
        input_output_aliases=aliases,
        compiler_params=pltpu.CompilerParams(vmem_limit_bytes=VMEM),
        cost_estimate=pl.CostEstimate(flops=22 * 10**9, bytes_accessed=60 * 10**6, transcendentals=0),
        name="forward_slot",
    )(*args)
    return kept, h


def backward_kernel(
    place, at_ref, g_hbm, u_hbm, w_hbm, view_hbm, gb_hbm, z_hbm, v_hbm, y_hbm, vr_hbm, cr_hbm,
    norm_ref, chan_ref, chanr_ref, head_ref, past_ref, *rest
):
    (
        du_hbm, dz_hbm, dv_hbm, sum_ref,
        g_scr, u_scr, wo_scr, wz_scr, wx_scr, wr_scr, gb_scr, z_scr, v_scr, y_scr, vr_scr, cr_scr, dz_scr, dv_scr,
        dob_scr, dgb_scr, dzp_scr, dvp_scr, c_scr, dy_scr, slope_scr, xl_scr, dyl_scr, q_scr, pull_scr, we_scr, st_scr, ds_scr, bcol_scr, trow_scr, colr_scr, rowr_scr, step_scr, act_scr, dn_scr,
        sem, out_sem,
    ) = rest[-41:]
    groups, rows, _ = dgb_scr.shape
    width = g_scr.shape[1]
    inner = groups * WIDE
    of_group, of_rest = in_copies(view_hbm, wz_scr, wx_scr, wr_scr, sem, 4)
    base = 2 * groups + 7
    g_copy = pltpu.make_async_copy(g_hbm, g_scr, sem.at[0])
    u_copy = pltpu.make_async_copy(u_hbm, u_scr, sem.at[1])
    vr_copy = pltpu.make_async_copy(vr_hbm.at[place], vr_scr, sem.at[2])
    cr_copy = pltpu.make_async_copy(cr_hbm.at[place], cr_scr, sem.at[3])

    def early(j):
        tall = pl.ds(pl.multiple_of(j * WIDE, WIDE), WIDE)
        return [
            pltpu.make_async_copy(w_hbm.at[tall, pl.ds(0, width)], wo_scr.at[j], sem.at[base + j]),
            pltpu.make_async_copy(gb_hbm.at[place, :, lanes(j)], gb_scr.at[j], sem.at[base + 4 * groups + j]),
        ]

    def late(j):
        return of_group(j) + [
            pltpu.make_async_copy(z_hbm.at[place, :, lanes(j)], z_scr.at[j], sem.at[base + groups + j]),
            pltpu.make_async_copy(y_hbm.at[place, :, lanes(j)], y_scr.at[j], sem.at[base + 2 * groups + j]),
            pltpu.make_async_copy(v_hbm.at[place, :, lanes(j)], v_scr.at[j], sem.at[base + 3 * groups + j]),
        ]

    def dz_copy(j):
        return pltpu.make_async_copy(dz_scr.at[j], dz_hbm.at[:, lanes(j)], out_sem.at[j])

    dv_copy = pltpu.make_async_copy(dv_scr, dv_hbm, out_sem.at[groups])
    du_copy = pltpu.make_async_copy(dob_scr, du_hbm, out_sem.at[groups + 1])

    @pl.when(at_ref[1] != 1)
    def _():
        sum_ref[...] = past_ref[...]

    @pl.when(at_ref[1] == 1)
    def _():
        start_all([g_copy, vr_copy, cr_copy])
        for j in range(groups):
            start_all(early(j))
        for j in range(groups):
            start_all(late(j))
        start_all(of_rest() + [u_copy])

        we_scr[...] = jnp.zeros_like(we_scr)
        ds_scr[...] = jnp.zeros_like(ds_scr)
        dn_scr[...] = jnp.zeros_like(dn_scr)
        rowr_scr[...] = jnp.zeros_like(rowr_scr)
        g_copy.wait()
        live = lax.broadcasted_iota(jnp.int32, (rows, 1), 0) < at_ref[0]
        dob_scr[...] = jnp.where(live, g_scr[...].astype(F32), 0.0).astype(BF16)
        cr_copy.wait()
        pre = cr_scr[...]
        act = pre * sigmoid(pre)
        act_scr[...] = act
        st_scr[...] = lax.dot_general(
            act[:, :STATE], act[:, STATE:], (((1,), (1,)), ((), ())), precision=EXACT, preferred_element_type=F32
        )
        vr_copy.wait()
        step, rate, sums, shifted = step_terms(vr_scr[:, 2 * STATE : 3 * STATE], head_ref)
        step_scr[...] = step
        spread(bcol_scr, shifted, groups)
        trow_scr[...] = sums.T

        def first_pass(j, carry):
            wait_all(early(j))
            for half in range(2):
                wide = slice(half * 2 * HALF, (half + 1) * 2 * HALF)
                dgb = nt_dot(dob_scr[...], wo_scr[j, wide, :])
                dgb_scr[j, :, wide] = dgb
                for at in range(0, rows, CHUNK):
                    at = slice(at, at + CHUNK)
                    product = dgb[at] * gb_scr[j, at, wide].astype(F32)
                    we_scr[at, :] += product[:, :HALF] + product[:, HALF:]
            return carry

        lax.fori_loop(0, groups, first_pass, 0)

        def second_pass(j, carry):
            wait_all(late(j))
            taps = chan_ref[:, lanes(j)]
            past = past_ref[:, lanes(j)]
            before = jnp.maximum(j - 1, 0)
            cols = bcol_scr[j]
            head_rows = pl.ds(pl.multiple_of(j * GROUP, GROUP), GROUP)
            rws = trow_scr[head_rows, :]
            lane = lax.broadcasted_iota(jnp.int32, (HALF, HALF), 1)
            causal = lane >= lax.broadcasted_iota(jnp.int32, (HALF, HALF), 0)
            first = lane < HEAD_DIM
            lane_row = lax.broadcasted_iota(jnp.int32, (1, HALF), 1)
            sub = lax.broadcasted_iota(jnp.int32, (GROUP, HALF), 0)
            blocks = rows // HALF
            pairs = GROUP // 2
            col_sums = [jnp.zeros((HALF, HALF), F32) for _ in range(blocks)]
            row_sums = [jnp.zeros((GROUP, HALF), F32) for _ in range(blocks)]
            for pair in range(pairs):
                here = slice(pair * HALF, (pair + 1) * HALF)
                col = pl.ds(pl.multiple_of(j * WIDE + pair * HALF, HALF), HALF)
                share = slice(pair * (width // pairs), (pair + 1) * (width // pairs))
                dn_scr[:, share] += nt_dot(dzp_scr[...], piece_of(wz_scr, before, pair, pairs)) + nt_dot(
                    dvp_scr[...], piece_of(wx_scr, before, pair, pairs)
                )
                c_scr[...] = conv_rows(v_scr[j, :, here], taps[0:4, here], taps[4:5, here])
                gate_sum = jnp.zeros((SUB, HALF), F32)
                skip_sum = jnp.zeros((SUB, HALF), F32)
                for at in range(0, rows, CHUNK):
                    at = slice(at, at + CHUNK)
                    q = q_scr[at, :]
                    dgb = dgb_scr[j, at, here]
                    z = z_scr[j, at, here]
                    y = y_scr[j, at, here]
                    sz = sigmoid(z)
                    silu_z = z * sz
                    w = y * silu_z
                    scaled = q * dgb
                    dw = scaled * taps[5:6, here] - w * pull_scr[at, :]
                    gate_sum = gate_sum + fewer(w * scaled)
                    dy = dw * silu_z
                    dy_scr[at, :] = dy
                    dyl_scr[at, :] = dy.astype(BF16)
                    dz_scr[j, at, here] = (dw * y * (sz + silu_z * (1.0 - sz))).astype(BF16)
                    c = c_scr[at, :]
                    sc = sigmoid(c)
                    x = c * sc
                    xl_scr[at, :] = x.astype(BF16)
                    slope_scr[at, :] = sc + x * (1.0 - sc)
                    skip_sum = skip_sum + fewer(dy * x)
                sum_ref[5:6, col] = past[5:6, here] + jnp.sum(gate_sum, axis=0, keepdims=True)
                sum_ref[6:7, col] = past[6:7, here] + jnp.sum(skip_sum, axis=0, keepdims=True)

                pieces = []
                row_part = [[None] * blocks, [None] * blocks]
                for sb in range(blocks):
                    s_here = slice(sb * HALF, (sb + 1) * HALF)
                    x_here = xl_scr[s_here, :]
                    none = jnp.zeros_like(x_here)
                    split = jnp.concatenate([jnp.where(first, x_here, none), jnp.where(first, none, x_here)], axis=0)
                    meets = nt_dot(split, dyl_scr[sb * HALF :, :])
                    mixes = [[], []]
                    lane_sum = [None, None]
                    for tb in range(sb, blocks):
                        t_here = slice(tb * HALF, (tb + 1) * HALF)
                        contact = st_scr[s_here, t_here]
                        touched = None
                        for k in range(2):
                            h = 2 * pair + k
                            gap = rws[h : h + 1, t_here] - cols[s_here, h : h + 1]
                            if sb == tb:
                                gap = jnp.where(causal, gap, NEG)
                            decay = jnp.exp2(gap)
                            meet = meets[k * HALF : (k + 1) * HALF, (tb - sb) * HALF : (tb - sb + 1) * HALF]
                            through = decay * meet
                            both = through * contact
                            touched = through if touched is None else touched + through
                            mixes[k].append((decay * contact).astype(BF16))
                            lane_sum[k] = both if lane_sum[k] is None else lane_sum[k] + both
                            falling = fewer(both)
                            row_part[k][tb] = falling if row_part[k][tb] is None else row_part[k][tb] + falling
                        ds_scr[s_here, t_here] += touched
                    mix = jnp.concatenate([jnp.concatenate(m, axis=1) if len(m) > 1 else m[0] for m in mixes], axis=0)
                    out = nn_dot(mix, dyl_scr[sb * HALF :, :])
                    for k in range(2):
                        total = jnp.sum(lane_sum[k], axis=1, keepdims=True)
                        col_sums[sb] = jnp.where(lane_row == 2 * pair + k, total, col_sums[sb])
                    pieces.append(jnp.where(first, out[:HALF], out[HALF:]))
                for k in range(2):
                    for tb in range(blocks):
                        total = jnp.sum(row_part[k][tb], axis=0, keepdims=True)
                        row_sums[tb] = jnp.where(sub == 2 * pair + k, total, row_sums[tb])
                dx = jnp.concatenate(pieces, axis=0)
                dc = (dx + taps[6:7, here] * dy_scr[...]) * slope_scr[...]
                dv, tap_sums = conv_back(dc, v_scr[j, :, here], taps[:, here])
                dv_scr[:, col] = dv.astype(BF16)
                for row, one in enumerate(tap_sums):
                    sum_ref[row : row + 1, col] = past[row : row + 1, here] + one
            colr_scr[j] = jnp.concatenate(col_sums, axis=0)
            rowr_scr[head_rows, :] = jnp.concatenate(row_sums, axis=1)
            dzp_scr[...] = dz_scr[j]
            dvp_scr[...] = dv_scr[:, lanes(j)]
            dz_copy(j).start()
            return carry

        for at in range(0, rows, CHUNK):
            at = slice(at, at + CHUNK)
            q = vr_scr[at, 3 * STATE - 1 :]
            pull = q * q * (jnp.sum(we_scr[at, :], axis=1, keepdims=True) * (1.0 / inner))
            q_scr[at, :] = jnp.broadcast_to(q, (CHUNK, HALF))
            pull_scr[at, :] = jnp.broadcast_to(pull, (CHUNK, HALF))
        dzp_scr[...] = jnp.zeros_like(dzp_scr)
        dvp_scr[...] = jnp.zeros_like(dvp_scr)
        lax.fori_loop(0, groups, second_pass, 0)
        dn_scr[...] += nt_dot(dzp_scr[...], fold(wz_scr[groups - 1])) + nt_dot(dvp_scr[...], fold(wx_scr[groups - 1]))
        act = act_scr[...]
        ds = ds_scr[...].astype(BF16)
        act_low = act.astype(BF16)
        d_b = nn_dot(ds, act_low[:, STATE:])
        d_c = lax.dot_general(ds, act_low[:, :STATE], (((0,), (0,)), ((), ())), preferred_element_type=F32)
        pre = cr_scr[...]
        sp = sigmoid(pre)
        d_pre = jnp.concatenate([d_b, d_c], axis=1) * (sp * (1.0 + pre * (1.0 - sp)))
        narrow = slice(inner, inner + 2 * STATE)
        d_raw, tap_sums = conv_back(d_pre, vr_scr[:, : 2 * STATE], chanr_ref[...])
        for row, one in enumerate(tap_sums):
            sum_ref[row : row + 1, narrow] = past_ref[row : row + 1, narrow] + one
        sum_ref[5:7, narrow] = jnp.zeros((2, 2 * STATE), F32)
        col_total = colr_scr[0]
        for g in range(1, groups):
            col_total = col_total + pltpu.roll(colr_scr[g], g * GROUP, 1)
        d_sums = rowr_scr[...].T - col_total
        at_row = lax.broadcasted_iota(jnp.int32, (rows, rows), 0)
        of_row = lax.broadcasted_iota(jnp.int32, (rows, rows), 1)
        upper = (of_row >= at_row).astype(F32)
        d_log = jnp.dot(upper, d_sums, precision=EXACT, preferred_element_type=F32)
        step = step_scr[...]
        rate = -jnp.exp(head_ref[1:2, :])
        d_step = col_total / step + rate * d_log
        raw_step = vr_scr[:, 2 * STATE : 3 * STATE] + head_ref[0:1, :]
        used = lax.broadcasted_iota(jnp.int32, (rows, HALF), 1) < inner // HEAD_DIM
        d_raw_step = jnp.where(used, d_step * jax.nn.sigmoid(raw_step), 0.0)
        last = past_ref[7:8, :]
        sum_ref[7:8, width : width + HALF] = last[:, width : width + HALF] + jnp.sum(d_raw_step, axis=0, keepdims=True)
        sum_ref[7:8, width + HALF : width + 2 * HALF] = last[:, width + HALF : width + 2 * HALF] + jnp.sum(
            jnp.where(used, d_log * step * rate, 0.0), axis=0, keepdims=True
        )
        sum_ref[7:8, width + 2 * HALF :] = jnp.zeros((1, inner - width), F32)
        dr = jnp.concatenate([d_raw, d_raw_step], axis=1).astype(BF16)
        dv_scr[:, inner:] = dr
        dv_copy.start()
        wait_all(of_rest())
        for k in range(3):
            dn_scr[...] += nt_dot(dr[:, k * STATE : (k + 1) * STATE], fold(wr_scr[k]))
        u_copy.wait()
        norm_sum = jnp.zeros((SUB, width), F32)
        for at in range(0, rows, 16):
            at = slice(at, at + 16)
            u = u_scr[at, :].astype(F32)
            dn = dn_scr[at, :]
            p = lax.rsqrt(jnp.mean(u * u, axis=1, keepdims=True) + EPS)
            e = dn * norm_ref[...]
            du = g_scr[at, :].astype(F32) + p * e - u * (p * p * p * jnp.mean(u * e, axis=1, keepdims=True))
            dob_scr[at, :] = du.astype(BF16)
            norm_sum = norm_sum + fewer(u * p * dn)
        du_copy.start()
        sum_ref[7:8, :width] = last[:, :width] + jnp.sum(norm_sum, axis=0, keepdims=True)
        for j in range(groups):
            dz_copy(j).wait()
        dv_copy.wait()
        du_copy.wait()


def conv_back(dc, values, taps):
    total, sums = 0.0, [None] * CONV
    for ahead in range(CONV):
        moved = down(dc, -ahead) if ahead else dc
        tap = CONV - 1 - ahead
        total = total + taps[tap : tap + 1, :] * moved
        sums[tap] = jnp.sum(fewer(moved * values), axis=0, keepdims=True)
    return total, sums + [jnp.sum(fewer(dc), axis=0, keepdims=True)]


def backward_slot(place, numbers, kept, grads, past, g, u, w_all, view, norm_gain, chan, chan_r, heads):
    rows, width = g.shape
    inner = chan.shape[1]
    groups = inner // WIDE
    parts, _, depth, _ = view.shape
    far = pl.BlockSpec(memory_space=pl.ANY)
    near = pl.BlockSpec(memory_space=pltpu.VMEM)
    args = [numbers, g, u, w_all, view, *kept, norm_gain, chan, chan_r, heads, past]
    in_specs = [pl.BlockSpec(memory_space=pltpu.SMEM)] + [far] * 10 + [near] * 5
    aliases = {}
    if grads is not None:
        for k, arr in enumerate(grads):
            aliases[len(args)] = k + 1
            args.append(arr)
            in_specs.append(far)
    tall = pltpu.VMEM((groups, parts, depth, WIDE), BF16)
    wide = pltpu.VMEM((groups, rows, WIDE), F32)
    slot = pltpu.VMEM((rows, width), BF16)
    return pl.pallas_call(
        functools.partial(backward_kernel, place),
        in_specs=in_specs,
        out_specs=[far, far, far, near],
        out_shape=[
            jax.ShapeDtypeStruct((rows, width), BF16),
            jax.ShapeDtypeStruct((rows, inner), BF16),
            jax.ShapeDtypeStruct((rows, inner + 3 * STATE), BF16),
            jax.ShapeDtypeStruct((8, inner + 2 * STATE), F32),
        ],
        scratch_shapes=[
            slot,
            slot,
            pltpu.VMEM((groups, WIDE, width), BF16),
            tall,
            tall,
            pltpu.VMEM((3, parts, depth, HALF), BF16),
            pltpu.VMEM((groups, rows, WIDE), BF16),
            wide,
            wide,
            wide,
            pltpu.VMEM((rows, 3 * STATE), F32),
            pltpu.VMEM((rows, 2 * STATE), F32),
            pltpu.VMEM((groups, rows, WIDE), BF16),
            pltpu.VMEM((rows, inner + 3 * STATE), BF16),
            slot,
            wide,
            pltpu.VMEM((rows, WIDE), BF16),
            pltpu.VMEM((rows, WIDE), BF16),
            pltpu.VMEM((rows, HALF), F32),
            pltpu.VMEM((rows, HALF), F32),
            pltpu.VMEM((rows, HALF), F32),
            pltpu.VMEM((rows, HALF), BF16),
            pltpu.VMEM((rows, HALF), BF16),
            pltpu.VMEM((rows, HALF), F32),
            pltpu.VMEM((rows, HALF), F32),
            pltpu.VMEM((rows, HALF), F32),
            pltpu.VMEM((rows, rows), F32),
            pltpu.VMEM((rows, rows), F32),
            pltpu.VMEM((groups, rows, HALF), F32),
            pltpu.VMEM((HALF, rows), F32),
            pltpu.VMEM((groups, rows, HALF), F32),
            pltpu.VMEM((HALF, rows), F32),
            pltpu.VMEM((rows, HALF), F32),
            pltpu.VMEM((rows, 2 * STATE), F32),
            pltpu.VMEM((rows, width), F32),
            pltpu.SemaphoreType.DMA((7 * groups + 7,)),
            pltpu.SemaphoreType.DMA((groups + 2,)),
        ],
        input_output_aliases=aliases,
        compiler_params=pltpu.CompilerParams(vmem_limit_bytes=VMEM),
        cost_estimate=pl.CostEstimate(flops=10**9, bytes_accessed=10**6, transcendentals=0),
        name="backward_slot",
    )(*args)


def pack_kernel(inner, in_ref, out_ref, packed_ref):
    depth, width = in_ref.shape[0], out_ref.shape[1]
    mid, end = 2 * inner + 2 * STATE, in_ref.shape[1]
    packed_ref[:, :width] = out_ref[...]
    tail = width + inner
    for half in range(2):
        rows = slice(half * depth, (half + 1) * depth)
        packed_ref[rows, width:tail] = in_ref[:, half * inner : (half + 1) * inner]
        packed_ref[rows, tail : tail + STATE] = in_ref[:, mid - 2 * STATE + half * STATE : mid - STATE + half * STATE]
        packed_ref[rows, tail + STATE :] = jnp.zeros((depth, STATE), BF16)
    packed_ref[:depth, tail + STATE : tail + STATE + end - mid] = in_ref[:, mid:]


def pack(in_shard, out_shard, inner):
    depth, width = in_shard.shape[0], out_shard.shape[1]
    return pl.pallas_call(
        functools.partial(pack_kernel, inner),
        out_shape=jax.ShapeDtypeStruct((2 * depth, width + inner + 2 * STATE), BF16),
        name="pack",
    )(in_shard, out_shard)


def order_kernel(at_ref, a_ref, own_ref, other_ref, turn_scr):
    turn_scr[...] = a_ref[0].astype(F32).T.reshape(turn_scr.shape)
    spots = own_ref.shape[1]
    for spot in range(spots):
        own_ref[0, spot] = turn_scr[at_ref[1 + spot]].astype(BF16)
        other_ref[0, spot] = turn_scr[at_ref[1 + spots + spot]].astype(BF16)


def by_owner(table, values, micro):
    _, rows, total = values.shape
    count = table.shape[0] - 1
    depth = total // count
    out = pl.BlockSpec((1, count // 2, depth, rows), lambda i, n: (i, 0, 0, 0))
    made = jax.ShapeDtypeStruct((micro, count // 2, depth, rows), BF16)
    parts = pl.pallas_call(
        order_kernel,
        grid_spec=pltpu.PrefetchScalarGridSpec(
            num_scalar_prefetch=1,
            grid=(micro,),
            in_specs=[pl.BlockSpec((1, rows, total), lambda i, n: (n[0] + i, 0, 0))],
            out_specs=[out, out],
            scratch_shapes=[pltpu.VMEM((count, depth, rows), F32)],
        ),
        out_shape=[made, made],
        compiler_params=pltpu.CompilerParams(vmem_limit_bytes=VMEM),
        cost_estimate=pl.CostEstimate(flops=3 * 10**9, bytes_accessed=2 * 10**6, transcendentals=0),
        name="by_owner",
    )(table, values)
    return [a.reshape(micro, total // 2, rows) for a in parts]


def outer_kernel(with_extra, picks, own_ref, sib_ref, *rest):
    rights, outs = rest[:-2], rest[-2:]
    micro, high = own_ref.shape[0], outs[0].shape[0]

    def left_of(part):
        size = high // len(picks[part])
        rows = [
            [ref[m, k * size : (k + 1) * size] for ref in (own_ref, sib_ref) for m in range(micro)] for k in picks[part]
        ]
        return jnp.concatenate([jnp.concatenate(row, axis=1) for row in rows], axis=0)

    if with_extra:
        extra_ref, rights = rights[-1], rights[:-1]
    right = jnp.concatenate([ref[...] for ref in rights], axis=0)
    for part, out_ref in enumerate(outs):
        rows = slice(part * high, (part + 1) * high)
        total = nn_dot(left_of(part), right)
        out_ref[...] = total.astype(BF16)
        if with_extra:
            extra = extra_ref[rows, :]

            @pl.when(pl.program_id(0) == pl.num_programs(0) - 1)
            def _():
                out_ref[:, -HALF:] = (total[:, -HALF:] + extra).astype(BF16)


def outer_sum(own, sib, rights, start, stop, block, extra=None, picks=((0,), (1,))):
    _, total, rows = own.shape
    low, steps = start // block, (stop - start) // block
    full = pl.BlockSpec(own.shape, lambda i: (0, 0, 0))
    out = pl.BlockSpec((total // 2, block), lambda i: (0, i))
    made = jax.ShapeDtypeStruct((total // 2, stop - start), BF16)
    more = [] if extra is None else [extra]
    return pl.pallas_call(
        functools.partial(outer_kernel, extra is not None, picks),
        grid=(steps,),
        in_specs=[full, full]
        + [pl.BlockSpec((rows, block), lambda i: (0, low + i)) for _ in rights]
        + [pl.BlockSpec(a.shape, lambda i: (0, 0)) for a in more],
        out_specs=[out, out],
        out_shape=[made, made],
        compiler_params=pltpu.CompilerParams(vmem_limit_bytes=VMEM),
        cost_estimate=pl.CostEstimate(flops=10**9, bytes_accessed=10**6, transcendentals=0),
        name="outer_sum",
    )(own, sib, *rights, *more)


def listing(sizes, span):
    return [-(-size // span) for size in sizes]


def spread_sums_kernel(sizes, inner, width, lane, spot_ref, own_ref, sib_ref, out_ref):
    total = own_ref[...] + sib_ref[...]
    cols, spots = total.shape[1], spot_ref.shape[0]
    depth, span = out_ref.shape[0] // spots, HALF - lane
    keep = lax.broadcasted_iota(jnp.int32, (8, HALF), 1) >= lane
    head = lax.broadcasted_iota(jnp.int32, (inner, HALF), 0) // HEAD_DIM
    group = (head == lax.broadcasted_iota(jnp.int32, (inner, HALF), 1)).astype(F32)
    skip = jnp.dot(total[:, :inner], group, precision=EXACT, preferred_element_type=F32)
    shared = [total[:, width : width + HALF], total[:, width + HALF : width + 2 * HALF], skip]
    shared = [jnp.where(keep, pltpu.roll(a, lane, 1), 0.0) for a in shared]
    out_ref[...] = jnp.zeros_like(out_ref)
    for spot in range(spots):
        row = spot * depth
        for size, low, high in ((sizes[0], 0, 5), (sizes[1], 5, 6), (sizes[2], 7, 8)):
            for part in range(-(-size // span)):
                start = spot_ref[spot] * size + part * span - lane
                here = pltpu.roll(total, lax.rem(2 * cols - start, cols), 1)[:, :HALF]
                out_ref[row : row + high - low, :] = jnp.where(keep, here, 0.0)[low:high]
                row += high - low
        for a, at in zip(shared, (7, 7, 6)):
            out_ref[row : row + 1, :] = a[at : at + 1]
            row += 1


def spread_sums(spots, own, sib, sizes, inner, width, lane):
    return pl.pallas_call(
        functools.partial(spread_sums_kernel, sizes, inner, width, lane),
        in_specs=[pl.BlockSpec(memory_space=pltpu.SMEM)] + [pl.BlockSpec(memory_space=pltpu.VMEM)] * 2,
        out_shape=jax.ShapeDtypeStruct((width // 2, HALF), F32),
        compiler_params=pltpu.CompilerParams(vmem_limit_bytes=VMEM),
        cost_estimate=pl.CostEstimate(flops=0, bytes_accessed=0, transcendentals=0),
        name="spread_sums",
    )(spots, own, sib)


def swap(values, axis, bit):
    return lax.ppermute(values, axis, [(a, a ^ bit) for a in range(lax.axis_size(axis))])


def all_rows_of(row, axis):
    count = lax.axis_size(axis)
    place = lax.axis_index(axis)
    table = jnp.where(jnp.arange(count, dtype=jnp.int32)[:, None] == place, row[None], jnp.zeros((), row.dtype))
    bit = 1
    while bit < count:
        table = table + swap(table, axis, bit)
        bit *= 2
    return table


def held(value, *after):
    return lax.optimization_barrier((value, after))[0]


def total_of(terms):
    return sum(a.astype(F32) for a in terms)


def exchange(terms, axis, bit):
    half = terms[0].shape[0] // 2
    sent = total_of([a[half:] for a in terms]).astype(BF16)
    return [a[:half] for a in terms] + [swap(sent, axis, bit)], sent


def spots_of(order):
    return [sum(bit for k, bit in enumerate(order) if p >> (len(order) - 1 - k) & 1) for p in range(2 ** len(order))]


def body(
    block_input,
    cotangent,
    lengths,
    in_weight,
    out_weight,
    conv_weight,
    conv_bias,
    norm_gain,
    gate_gain,
    dt_bias,
    a_log,
    skip_d,
):
    axis = "fsdp"
    count = lax.axis_size(axis)
    section = lax.axis_index("section")
    micro, rows, width = block_input.shape
    depth, proj_cols = in_weight.shape[1:]
    inner = gate_gain.shape[1] * count
    channels = conv_bias.shape[1] * count
    heads = dt_bias.shape[1]
    small = [a.reshape(-1) for a in (conv_weight[0], conv_bias[0], norm_gain[0], gate_gain[0])]
    sizes = [a.shape[0] for a in small]
    w_all = lax.all_gather(pack(in_weight[0], out_weight[0], inner), axis, axis=0, tiled=True)
    view = w_all.reshape(count, 2, depth, -1)
    if depth % 16:
        view = view.transpose(1, 0, 2, 3).reshape(1, 2, width, -1)
    flat = all_rows_of(jnp.concatenate(small), axis).astype(F32)
    cuts = [0]
    for size in sizes:
        cuts.append(cuts[-1] + size)
    taps = flat[:, cuts[0] : cuts[1]].reshape(count, CONV, -1).transpose(1, 0, 2).reshape(CONV, channels)
    bias = flat[:, cuts[1] : cuts[2]].reshape(1, channels)
    norm = flat[:, cuts[2] : cuts[3]].reshape(1, width)
    gate = flat[:, cuts[3] : cuts[4]].reshape(1, inner)
    skip = jnp.repeat(skip_d[0], HEAD_DIM)[None]
    chan = jnp.concatenate([taps[:, :inner], bias[:, :inner], gate, skip, jnp.zeros((1, inner), F32)], axis=0)
    chan_r = jnp.concatenate([taps[:, inner:], bias[:, inner:], jnp.zeros((3, channels - inner), F32)], axis=0)
    head_rows = jnp.pad(jnp.stack([dt_bias[0], a_log[0]]), ((0, 6), (0, HALF - heads)))
    places = jnp.arange(rows, dtype=jnp.int32)
    live = [(places < lengths[m, 0])[:, None] for m in range(micro)]

    def numbers(m, stage):
        return jnp.stack([lengths[m, 0], (section == stage).astype(jnp.int32)])

    kept = None
    first, second = [], []
    for m in range(micro):
        kept, h = forward_slot(
            m, numbers(m, 0), kept, block_input[m], w_all, view, norm, chan, chan_r, head_rows, gate, 2 * micro
        )
        first.append(h)
    arrived = [lax.ppermute(h, "section", [(0, 1)]) for h in first]
    for m in range(micro):
        kept, h = forward_slot(
            micro + m, numbers(m, 1), kept, arrived[m], w_all, view, norm, chan, chan_r, head_rows, gate, 2 * micro
        )
        second.append(h)
    outputs = jnp.stack([jnp.where(section == 0, a, b) for a, b in zip(first, second)])

    def run_backward(place, m, stage, grads, sums, g, u):
        return backward_slot(
            place, numbers(m, stage), kept[1:], grads, sums, g, u, w_all, view, norm, chan, chan_r, head_rows
        )

    is_last = section == 1
    sums = jnp.zeros((8, inner + 2 * STATE), F32)
    grads, late_grads, early_grads, returned = [None] * micro, [None] * micro, [None] * micro, [None] * micro
    for m in reversed(range(micro)):
        late_grads[m], *grads[m], sums = run_backward(micro + m, m, 1, None, sums, cotangent[m], arrived[m])
        returned[m] = lax.ppermute(late_grads[m], "section", [(1, 0)])

    place = lax.axis_index(axis).astype(jnp.int32)
    line = [4 << k for k in range(count.bit_length() - 3)]
    in_order, out_order = [2] + line, line + [2]

    def table_of(order):
        spots = jnp.array(spots_of(order), jnp.int32)
        return jnp.concatenate([(section * micro)[None].astype(jnp.int32), place ^ spots, place ^ 1 ^ spots])

    nb, gb, _ = lax.optimization_barrier((kept[0], kept[1], late_grads[0]))
    out_own, out_other = by_owner(table_of(out_order), gb, micro)
    in_own, in_other = by_owner(table_of(in_order), nb, micro)
    out_sib, in_sib = swap(out_other, axis, 1), swap(in_other, axis, 1)
    returned[-1], out_own, in_own = lax.optimization_barrier((returned[-1], out_own, in_own))

    branch, branch_sib, z_sib, v_sib = [None] * micro, [None] * micro, [None] * micro, [None] * micro

    def take_branch(m):
        branch[m] = jnp.where(live[m], jnp.where(is_last, cotangent[m], returned[m]), jnp.zeros((), BF16))
        branch_sib[m] = swap(branch[m], axis, 1)

    for m in reversed(range(1, micro)):
        take_branch(m)
        early_grads[m], *grads[m], sums = run_backward(m, m, 0, grads[m], sums, returned[m], block_input[m])
        z_sib[m], v_sib[m] = (swap(a, axis, 1) for a in grads[m])
    returned[0], early_grads[-1] = lax.optimization_barrier((returned[0], early_grads[-1]))
    take_branch(0)

    half = width // 2
    a_keep, a_send = outer_sum(out_own, out_sib, branch + branch_sib, 0, half, half)
    branch[0] = held(branch[0], a_send)
    every = range(count // 2)
    b_keep, b_send = outer_sum(
        out_own, out_sib, branch + branch_sib, half, width, half, picks=(every[::2], every[1::2])
    )
    returned[0], a_send, b_send = lax.optimization_barrier((returned[0], a_send, b_send))
    out_a = [a_keep, swap(a_send, axis, line[0])]
    out_b = [b_keep, swap(b_send, axis, 2)]
    early_grads[0], *grads[0], sums = run_backward(0, 0, 0, grads[0], sums, returned[0], block_input[0])
    grads[0], out_a[-1], out_b[-1] = lax.optimization_barrier((grads[0], out_a[-1], out_b[-1]))
    z_sib[0], v_sib[0] = (swap(a, axis, 1) for a in grads[0])
    for bit in line[1:]:
        out_a, a_token = exchange(out_a, axis, bit)
    out_b, b_token = exchange(out_b, axis, line[0])
    input_grads = jnp.stack([jnp.where(is_last, a, b) for a, b in zip(late_grads, early_grads)])

    z_rows = [a for a, _ in grads] + z_sib
    v_rows = [a for _, a in grads] + v_sib
    cut, block, end = 5 * 384, 384, inner + 3 * STATE
    z_rows[-micro] = held(z_rows[-micro], a_token, b_token)
    half = inner // 2
    z_pairs = [outer_sum(in_own, in_sib, z_rows, 0, half, WIDE)]
    z_rows[-1] = held(z_rows[-1], z_pairs[0][1])
    z_pairs.append(outer_sum(in_own, in_sib, z_rows, half, inner, WIDE))
    out_b[-1] = held(out_b[-1], z_pairs[1][1])
    for bit in line[1:]:
        out_b, b_token = exchange(out_b, axis, bit)
    chunks = [[keep, swap(send, axis, 2)] for keep, send in z_pairs]
    sums, v_rows[0] = held((sums, v_rows[0]), b_token, out_a[-1])
    at_lane = (proj_cols - inner) % HALF
    per = [channels // count, inner // count, width // count]
    in_spots = place ^ jnp.array(spots_of(in_order), jnp.int32)
    extra = spread_sums(in_spots, sums, swap(sums, axis, 1), per, inner, width, at_lane)
    mid = end - 2 * block
    pairs = [outer_sum(in_own, in_sib, v_rows, 0, cut, 640)]
    v_rows[0] = held(v_rows[0], pairs[0][1], out_b[-1], chunks[0][-1])
    pairs.append(outer_sum(in_own, in_sib, v_rows, mid, end, block, extra))
    v_rows[0] = held(v_rows[0], pairs[1][1], chunks[1][-1])
    pairs.append(outer_sum(in_own, in_sib, v_rows, cut, mid, block))
    chunks += [[keep, swap(send, axis, 2)] for keep, send in pairs]
    token = pairs[0][1]
    last = len(chunks) - 1

    def first_step(k, token):
        chunks[k][-1] = held(chunks[k][-1], token)
        chunks[k], token = exchange(chunks[k], axis, line[0])
        return token

    def other_steps(k, token):
        for bit in line[1:]:
            chunks[k][-1] = held(chunks[k][-1], token)
            chunks[k], token = exchange(chunks[k], axis, bit)
        return token

    token = first_step(0, token)
    for k in range(1, last):
        token = first_step(k, (token, chunks[0][-1]) if k == 2 else token)
        token = other_steps(k - 1, token)
    token = first_step(last, token)
    out_a[-1] = held(out_a[-1], token)
    out_a, _ = exchange(out_a, axis, 2)
    token = other_steps(last - 1, token)
    token = other_steps(last, token)
    out_grad = jnp.concatenate([total_of(out_a), total_of(out_b)], axis=1)
    in_parts = [total_of(terms) for terms in chunks]
    tail = in_parts[3]
    own_cols = proj_cols - inner - mid
    in_grad = jnp.concatenate([in_parts[0], in_parts[1], in_parts[2], in_parts[4], tail[:, :own_cols]], axis=1)
    span = HALF - at_lane
    tap_parts, gate_parts, norm_parts = listing(per, span)
    rows_of = lambda low, high: tail[low:high, own_cols : own_cols + span]
    cut_rows = [0, 5 * tap_parts, 5 * tap_parts + gate_parts, 5 * tap_parts + gate_parts + norm_parts]
    taps_g = rows_of(0, cut_rows[1]).reshape(tap_parts, 5, span).transpose(1, 0, 2).reshape(5, -1)[:, : per[0]]
    gate_g = rows_of(cut_rows[1], cut_rows[2]).reshape(1, -1)[:, : per[1]]
    norm_g = rows_of(cut_rows[2], cut_rows[3]).reshape(1, -1)[:, : per[2]]
    shared_g = rows_of(cut_rows[3], cut_rows[3] + 3)[:, :heads]
    return (
        outputs[None],
        input_grads[None],
        in_grad[None],
        out_grad[None],
        taps_g[None, :CONV],
        taps_g[CONV:],
        norm_g,
        gate_g,
        shared_g[0:1],
        shared_g[1:2],
        shared_g[2:3],
    )


def solution(mesh):
    in_specs = (
        P(None, "fsdp", None),
        P(None, "fsdp", None),
        P(None, "fsdp"),
        P("section", "fsdp", None),
        P("section", "fsdp", None),
        P("section", None, "fsdp"),
        P("section", "fsdp"),
        P("section", "fsdp"),
        P("section", "fsdp"),
        P("section", None),
        P("section", None),
        P("section", None),
    )
    out_specs = (
        P("section", None, "fsdp", None),
        P("section", None, "fsdp", None),
        P("section", "fsdp", None),
        P("section", "fsdp", None),
        P("section", None, "fsdp"),
        P("section", "fsdp"),
        P("section", "fsdp"),
        P("section", "fsdp"),
        P("section", None),
        P("section", None),
        P("section", None),
    )
    return jax.shard_map(body, mesh=mesh, in_specs=in_specs, out_specs=out_specs, check_vma=False)
```

```python
import functools

import jax
import jax.numpy as jnp
from jax import lax
from jax.experimental import pallas as pl
from jax.experimental.pallas import tpu as pltpu
from jax.sharding import PartitionSpec as P

HEAD_DIM = 64
STATE = 128
CONV = 4
EPS = 1e-05
LOG2E = 1.4426950408889634
HALF = 128
WIDE = 512
GROUP = WIDE // HEAD_DIM
TINY = 1e-30
SUB = 8
CHUNK = 64
NEG = -1e30
VMEM = 60 * 1024 * 1024
F32 = jnp.float32
BF16 = jnp.bfloat16
EXACT = lax.Precision.HIGHEST


def nt_dot(a, b):
    return lax.dot_general(a, b, (((1,), (1,)), ((), ())), preferred_element_type=F32)


def nn_dot(a, b):
    return jnp.dot(a, b, preferred_element_type=F32)


def sigmoid(v):
    return 0.5 * jnp.tanh(0.5 * v) + 0.5


def down(values, steps):
    count = values.shape[0]
    moved = pltpu.roll(values, steps % count, 0)
    rows = lax.broadcasted_iota(jnp.int32, (SUB, values.shape[1]), 0)
    if steps > 0:
        return jnp.concatenate([jnp.where(rows >= steps, moved[:SUB], 0.0), moved[SUB:]], axis=0)
    return jnp.concatenate([moved[:-SUB], jnp.where(rows < SUB + steps, moved[-SUB:], 0.0)], axis=0)


def conv_rows(values, taps, bias):
    total = bias + taps[CONV - 1 : CONV, :] * values
    for back in range(1, CONV):
        total = total + taps[CONV - 1 - back : CONV - back, :] * down(values, back)
    return total


def fewer(block):
    total = block[:SUB]
    for at in range(SUB, block.shape[0], SUB):
        total = total + block[at : at + SUB]
    return total


def piece_of(scr, j, piece, pieces):
    _, parts, depth, _ = scr.shape
    if parts % pieces == 0:
        return fold(scr[j, piece * (parts // pieces) : (piece + 1) * (parts // pieces)])
    size = parts * depth // pieces
    return fold(scr[j])[piece * size : (piece + 1) * size]


def softplus(v):
    return jnp.maximum(v, 0.0) + jnp.log1p(jnp.exp(-jnp.abs(v)))


def step_terms(step_raw, head_ref):
    rows = step_raw.shape[0]
    step = jnp.maximum(softplus(step_raw + head_ref[0:1, :]), TINY)
    rate = -jnp.exp(head_ref[1:2, :])
    at = lax.broadcasted_iota(jnp.int32, (rows, rows), 0)
    of = lax.broadcasted_iota(jnp.int32, (rows, rows), 1)
    lower = (at >= of).astype(F32)
    sums = jnp.dot(lower, step * rate, precision=EXACT, preferred_element_type=F32) * LOG2E
    return step, rate, sums, sums - jnp.log2(step)


def spread(target, values, groups):
    for g in range(groups):
        target[g] = pltpu.roll(values, (HALF - g * GROUP) % HALF, 1) if g else values


def fold(block):
    return block.reshape(-1, block.shape[-1])


def lanes(index):
    return pl.ds(pl.multiple_of(index * WIDE, WIDE), WIDE)


def in_copies(view_ref, wz_scr, wx_scr, wr_scr, sem, base):
    parts, _, depth, _ = view_ref.shape
    width, groups = parts * depth, wz_scr.shape[0]
    tail = width + groups * WIDE

    def of_group(j):
        here = pl.ds(pl.multiple_of(width + j * WIDE, WIDE), WIDE)
        return [
            pltpu.make_async_copy(view_ref.at[:, 0, :, here], wz_scr.at[j], sem.at[base + j]),
            pltpu.make_async_copy(view_ref.at[:, 1, :, here], wx_scr.at[j], sem.at[base + groups + j]),
        ]

    def of_rest():
        return [
            pltpu.make_async_copy(view_ref.at[:, half, :, pl.ds(at, HALF)], wr_scr.at[k], sem.at[base + 2 * groups + k])
            for k, (half, at) in enumerate(((0, tail), (1, tail), (0, tail + HALF)))
        ]

    return of_group, of_rest


def start_all(copies):
    for copy in copies:
        copy.start()


def wait_all(copies):
    for copy in copies:
        copy.wait()


def forward_kernel(place, at_ref, u_hbm, w_hbm, view_hbm, norm_ref, chan_ref, chanr_ref, head_ref, gate_ref, *rest):
    (
        nb_hbm, gb_hbm, z_hbm, v_hbm, y_hbm, vr_hbm, cr_hbm, h_hbm,
        u_scr, wz_scr, wx_scr, wr_scr, wo_scr, nb_scr, gb_scr, z_scr, v_scr, y_scr, vr_scr, cr_scr, h_scr,
        w_scr, sq_scr, s_scr, col_scr, row_scr, sem, out_sem,
    ) = rest[-28:]
    groups, rows, _ = w_scr.shape
    of_group, of_rest = in_copies(view_hbm, wz_scr, wx_scr, wr_scr, sem, 1)
    spare = 2 * groups + 4
    u_copy = pltpu.make_async_copy(u_hbm, u_scr, sem.at[0])

    def of_out(k):
        return pltpu.make_async_copy(w_hbm.at[:, lanes(k)], wo_scr.at[k], sem.at[spare + k])

    def kept_copies(j):
        return [
            pltpu.make_async_copy(scr.at[j], hbm.at[place, :, lanes(j)], out_sem.at[k * groups + j])
            for k, (scr, hbm) in enumerate(((z_scr, z_hbm), (v_scr, v_hbm), (y_scr, y_hbm)))
        ]

    last = 3 * groups
    whole_copies = [
        pltpu.make_async_copy(scr, hbm.at[place], out_sem.at[last + k])
        for k, (scr, hbm) in enumerate(((nb_scr, nb_hbm), (gb_scr, gb_hbm), (vr_scr, vr_hbm), (cr_scr, cr_hbm)))
    ]
    h_copy = pltpu.make_async_copy(h_scr, h_hbm, out_sem.at[last + 4])

    @pl.when(at_ref[1] == 1)
    def _():
        u_copy.start()
        start_all(of_rest())
        for j in range(groups):
            start_all(of_group(j))
        for k in range(wo_scr.shape[0]):
            of_out(k).start()

        u_copy.wait()
        u = u_scr[...].astype(F32)
        scale = lax.rsqrt(jnp.mean(u * u, axis=1, keepdims=True) + EPS)
        nb_scr[...] = (u * scale * norm_ref[...]).astype(BF16)
        nb = nb_scr[...]
        wait_all(of_rest())
        raw = jnp.concatenate([nn_dot(nb, fold(wr_scr[0])), nn_dot(nb, fold(wr_scr[1]))], axis=1)
        steps = nn_dot(nb, fold(wr_scr[2]))
        vr_scr[:, : 2 * STATE] = raw
        vr_scr[:, 2 * STATE :] = steps
        pre = conv_rows(raw, chanr_ref[0:4, :], chanr_ref[4:5, :])
        cr_scr[...] = pre
        act = pre * sigmoid(pre)
        s_scr[...] = lax.dot_general(
            act[:, STATE:], act[:, :STATE], (((1,), (1,)), ((), ())), precision=EXACT, preferred_element_type=F32
        )
        _, _, sums, shifted = step_terms(steps, head_ref)
        spread(col_scr, sums, groups)
        row_scr[...] = shifted.T
        sq_scr[...] = jnp.zeros_like(sq_scr)

        def group(j, carry):
            wait_all(of_group(j))
            nb = nb_scr[...]
            z = nn_dot(nb, fold(wz_scr[j]))
            z_scr[j] = z
            v = nn_dot(nb, fold(wx_scr[j]))
            v_scr[j] = v
            taps = chan_ref[:, lanes(j)]
            c = conv_rows(v, taps[0:4, :], taps[4:5, :])
            x = c * sigmoid(c)
            x_low = x.astype(BF16)
            cols = col_scr[j]
            rws = row_scr[pl.ds(pl.multiple_of(j * GROUP, GROUP), GROUP), :]
            lane = lax.broadcasted_iota(jnp.int32, (HALF, HALF), 1)
            causal = lax.broadcasted_iota(jnp.int32, (HALF, HALF), 0) >= lane
            first = lane < HEAD_DIM
            parts = []
            for pair in range(GROUP // 2):
                here = slice(pair * HALF, (pair + 1) * HALF)
                pieces = []
                for tb in range(rows // HALF):
                    t_here = slice(tb * HALF, (tb + 1) * HALF)
                    both = []
                    for h in (2 * pair, 2 * pair + 1):
                        col = cols[t_here, h : h + 1]
                        mix = []
                        for sb in range(tb + 1):
                            s_here = slice(sb * HALF, (sb + 1) * HALF)
                            gap = col - rws[h : h + 1, s_here]
                            if sb == tb:
                                gap = jnp.where(causal, gap, NEG)
                            mix.append((jnp.exp2(gap) * s_scr[t_here, s_here]).astype(BF16))
                        mix = jnp.concatenate(mix, axis=1) if len(mix) > 1 else mix[0]
                        both.append(nn_dot(mix, x_low[: (tb + 1) * HALF, here]))
                    pieces.append(jnp.where(first, both[0], both[1]))
                parts.append(jnp.concatenate(pieces, axis=0))
            y = jnp.concatenate(parts, axis=1) + taps[6:7, :] * x
            y_scr[j] = y
            w = y * (z * sigmoid(z))
            w_scr[j] = w
            sq_scr[...] += jnp.sum(w * w, axis=1, keepdims=True)
            start_all(kept_copies(j))
            return carry

        lax.fori_loop(0, groups, group, 0)
        scale = lax.rsqrt(sq_scr[...] * (1.0 / (groups * WIDE)) + EPS)
        vr_scr[:, 3 * STATE - 1 :] = scale
        for g in range(groups):
            here = slice(g * WIDE, (g + 1) * WIDE)
            gb_scr[:, here] = (w_scr[g] * scale * gate_ref[:, here]).astype(BF16)
        start_all(whole_copies)
        live = lax.broadcasted_iota(jnp.int32, (rows, 1), 0) < at_ref[0]
        for k in range(wo_scr.shape[0]):
            here = slice(k * WIDE, (k + 1) * WIDE)
            of_out(k).wait()
            branch = jnp.where(live, nn_dot(gb_scr[...], wo_scr[k]), 0.0)
            h_scr[:, here] = (u_scr[:, here].astype(F32) + branch).astype(BF16)
        h_copy.start()
        for j in range(groups):
            wait_all(kept_copies(j))
        wait_all(whole_copies)
        h_copy.wait()


def forward_slot(place, numbers, kept, u, w_all, view, norm_gain, chan, chan_r, heads, gate_gain, slots):
    rows, width = u.shape
    inner = chan.shape[1]
    groups = inner // WIDE
    parts, _, depth, _ = view.shape
    shapes = [((rows, width), BF16), ((rows, inner), BF16)] + [((rows, inner), F32)] * 3
    shapes += [((rows, 3 * STATE), F32), ((rows, 2 * STATE), F32)]
    far = pl.BlockSpec(memory_space=pl.ANY)
    near = pl.BlockSpec(memory_space=pltpu.VMEM)
    args = [numbers, u, w_all, view, norm_gain, chan, chan_r, heads, gate_gain]
    in_specs = [pl.BlockSpec(memory_space=pltpu.SMEM), far, far, far] + [near] * 5
    aliases = {}
    if kept is not None:
        for k, arr in enumerate(kept):
            aliases[len(args)] = k
            args.append(arr)
            in_specs.append(far)
    out_shape = [jax.ShapeDtypeStruct((slots,) + s, d) for s, d in shapes]
    tall = pltpu.VMEM((groups, parts, depth, WIDE), BF16)
    wide = pltpu.VMEM((groups, rows, WIDE), F32)
    *kept, h = pl.pallas_call(
        functools.partial(forward_kernel, place),
        in_specs=in_specs,
        out_specs=[far] * 8,
        out_shape=out_shape + [jax.ShapeDtypeStruct((rows, width), BF16)],
        scratch_shapes=[
            pltpu.VMEM((rows, width), BF16),
            tall,
            tall,
            pltpu.VMEM((3, parts, depth, HALF), BF16),
            pltpu.VMEM((width // WIDE, inner, WIDE), BF16),
            pltpu.VMEM((rows, width), BF16),
            pltpu.VMEM((rows, inner), BF16),
            wide,
            wide,
            wide,
            pltpu.VMEM((rows, 3 * STATE), F32),
            pltpu.VMEM((rows, 2 * STATE), F32),
            pltpu.VMEM((rows, width), BF16),
            wide,
            pltpu.VMEM((rows, 1), F32),
            pltpu.VMEM((rows, rows), F32),
            pltpu.VMEM((groups, rows, HALF), F32),
            pltpu.VMEM((HALF, rows), F32),
            pltpu.SemaphoreType.DMA((2 * groups + 4 + width // WIDE,)),
            pltpu.SemaphoreType.DMA((3 * groups + 5,)),
        ],
        input_output_aliases=aliases,
        compiler_params=pltpu.CompilerParams(vmem_limit_bytes=VMEM),
        cost_estimate=pl.CostEstimate(flops=22 * 10**9, bytes_accessed=60 * 10**6, transcendentals=0),
        name="forward_slot",
    )(*args)
    return kept, h


def backward_kernel(
    place, at_ref, g_hbm, u_hbm, w_hbm, view_hbm, gb_hbm, z_hbm, v_hbm, y_hbm, vr_hbm, cr_hbm,
    norm_ref, chan_ref, chanr_ref, head_ref, past_ref, *rest
):
    (
        du_hbm, dz_hbm, dv_hbm, sum_ref,
        g_scr, u_scr, wo_scr, wz_scr, wx_scr, wr_scr, gb_scr, z_scr, v_scr, y_scr, vr_scr, cr_scr, dz_scr, dv_scr,
        dob_scr, dgb_scr, dzp_scr, dvp_scr, c_scr, dy_scr, slope_scr, xl_scr, dyl_scr, q_scr, pull_scr, we_scr, st_scr, ds_scr, bcol_scr, trow_scr, colr_scr, rowr_scr, step_scr, act_scr, dn_scr,
        sem, out_sem,
    ) = rest[-41:]
    groups, rows, _ = dgb_scr.shape
    width = g_scr.shape[1]
    inner = groups * WIDE
    of_group, of_rest = in_copies(view_hbm, wz_scr, wx_scr, wr_scr, sem, 4)
    base = 2 * groups + 7
    g_copy = pltpu.make_async_copy(g_hbm, g_scr, sem.at[0])
    u_copy = pltpu.make_async_copy(u_hbm, u_scr, sem.at[1])
    vr_copy = pltpu.make_async_copy(vr_hbm.at[place], vr_scr, sem.at[2])
    cr_copy = pltpu.make_async_copy(cr_hbm.at[place], cr_scr, sem.at[3])

    def early(j):
        tall = pl.ds(pl.multiple_of(j * WIDE, WIDE), WIDE)
        return [
            pltpu.make_async_copy(w_hbm.at[tall, pl.ds(0, width)], wo_scr.at[j], sem.at[base + j]),
            pltpu.make_async_copy(gb_hbm.at[place, :, lanes(j)], gb_scr.at[j], sem.at[base + 4 * groups + j]),
        ]

    def late(j):
        return of_group(j) + [
            pltpu.make_async_copy(z_hbm.at[place, :, lanes(j)], z_scr.at[j], sem.at[base + groups + j]),
            pltpu.make_async_copy(y_hbm.at[place, :, lanes(j)], y_scr.at[j], sem.at[base + 2 * groups + j]),
            pltpu.make_async_copy(v_hbm.at[place, :, lanes(j)], v_scr.at[j], sem.at[base + 3 * groups + j]),
        ]

    def dz_copy(j):
        return pltpu.make_async_copy(dz_scr.at[j], dz_hbm.at[:, lanes(j)], out_sem.at[j])

    dv_copy = pltpu.make_async_copy(dv_scr, dv_hbm, out_sem.at[groups])
    du_copy = pltpu.make_async_copy(dob_scr, du_hbm, out_sem.at[groups + 1])

    @pl.when(at_ref[1] != 1)
    def _():
        sum_ref[...] = past_ref[...]

    @pl.when(at_ref[1] == 1)
    def _():
        start_all([g_copy, vr_copy, cr_copy])
        for j in range(groups):
            start_all(early(j))
        for j in range(groups):
            start_all(late(j))
        start_all(of_rest() + [u_copy])

        we_scr[...] = jnp.zeros_like(we_scr)
        ds_scr[...] = jnp.zeros_like(ds_scr)
        dn_scr[...] = jnp.zeros_like(dn_scr)
        rowr_scr[...] = jnp.zeros_like(rowr_scr)
        g_copy.wait()
        live = lax.broadcasted_iota(jnp.int32, (rows, 1), 0) < at_ref[0]
        dob_scr[...] = jnp.where(live, g_scr[...].astype(F32), 0.0).astype(BF16)
        cr_copy.wait()
        pre = cr_scr[...]
        act = pre * sigmoid(pre)
        act_scr[...] = act
        st_scr[...] = lax.dot_general(
            act[:, :STATE], act[:, STATE:], (((1,), (1,)), ((), ())), precision=EXACT, preferred_element_type=F32
        )
        vr_copy.wait()
        step, rate, sums, shifted = step_terms(vr_scr[:, 2 * STATE : 3 * STATE], head_ref)
        step_scr[...] = step
        spread(bcol_scr, shifted, groups)
        trow_scr[...] = sums.T

        def first_pass(j, carry):
            wait_all(early(j))
            for half in range(2):
                wide = slice(half * 2 * HALF, (half + 1) * 2 * HALF)
                dgb = nt_dot(dob_scr[...], wo_scr[j, wide, :])
                dgb_scr[j, :, wide] = dgb
                for at in range(0, rows, CHUNK):
                    at = slice(at, at + CHUNK)
                    product = dgb[at] * gb_scr[j, at, wide].astype(F32)
                    we_scr[at, :] += product[:, :HALF] + product[:, HALF:]
            return carry

        lax.fori_loop(0, groups, first_pass, 0)

        def second_pass(j, carry):
            wait_all(late(j))
            taps = chan_ref[:, lanes(j)]
            past = past_ref[:, lanes(j)]
            before = jnp.maximum(j - 1, 0)
            cols = bcol_scr[j]
            head_rows = pl.ds(pl.multiple_of(j * GROUP, GROUP), GROUP)
            rws = trow_scr[head_rows, :]
            lane = lax.broadcasted_iota(jnp.int32, (HALF, HALF), 1)
            causal = lane >= lax.broadcasted_iota(jnp.int32, (HALF, HALF), 0)
            first = lane < HEAD_DIM
            lane_row = lax.broadcasted_iota(jnp.int32, (1, HALF), 1)
            sub = lax.broadcasted_iota(jnp.int32, (GROUP, HALF), 0)
            blocks = rows // HALF
            pairs = GROUP // 2
            col_sums = [jnp.zeros((HALF, HALF), F32) for _ in range(blocks)]
            row_sums = [jnp.zeros((GROUP, HALF), F32) for _ in range(blocks)]
            for pair in range(pairs):
                here = slice(pair * HALF, (pair + 1) * HALF)
                col = pl.ds(pl.multiple_of(j * WIDE + pair * HALF, HALF), HALF)
                share = slice(pair * (width // pairs), (pair + 1) * (width // pairs))
                dn_scr[:, share] += nt_dot(dzp_scr[...], piece_of(wz_scr, before, pair, pairs)) + nt_dot(
                    dvp_scr[...], piece_of(wx_scr, before, pair, pairs)
                )
                c_scr[...] = conv_rows(v_scr[j, :, here], taps[0:4, here], taps[4:5, here])
                gate_sum = jnp.zeros((SUB, HALF), F32)
                skip_sum = jnp.zeros((SUB, HALF), F32)
                for at in range(0, rows, CHUNK):
                    at = slice(at, at + CHUNK)
                    q = q_scr[at, :]
                    dgb = dgb_scr[j, at, here]
                    z = z_scr[j, at, here]
                    y = y_scr[j, at, here]
                    sz = sigmoid(z)
                    silu_z = z * sz
                    w = y * silu_z
                    scaled = q * dgb
                    dw = scaled * taps[5:6, here] - w * pull_scr[at, :]
                    gate_sum = gate_sum + fewer(w * scaled)
                    dy = dw * silu_z
                    dy_scr[at, :] = dy
                    dyl_scr[at, :] = dy.astype(BF16)
                    dz_scr[j, at, here] = (dw * y * (sz + silu_z * (1.0 - sz))).astype(BF16)
                    c = c_scr[at, :]
                    sc = sigmoid(c)
                    x = c * sc
                    xl_scr[at, :] = x.astype(BF16)
                    slope_scr[at, :] = sc + x * (1.0 - sc)
                    skip_sum = skip_sum + fewer(dy * x)
                sum_ref[5:6, col] = past[5:6, here] + jnp.sum(gate_sum, axis=0, keepdims=True)
                sum_ref[6:7, col] = past[6:7, here] + jnp.sum(skip_sum, axis=0, keepdims=True)

                pieces = []
                row_part = [[None] * blocks, [None] * blocks]
                for sb in range(blocks):
                    s_here = slice(sb * HALF, (sb + 1) * HALF)
                    x_here = xl_scr[s_here, :]
                    none = jnp.zeros_like(x_here)
                    split = jnp.concatenate([jnp.where(first, x_here, none), jnp.where(first, none, x_here)], axis=0)
                    meets = nt_dot(split, dyl_scr[sb * HALF :, :])
                    mixes = [[], []]
                    lane_sum = [None, None]
                    for tb in range(sb, blocks):
                        t_here = slice(tb * HALF, (tb + 1) * HALF)
                        contact = st_scr[s_here, t_here]
                        touched = None
                        for k in range(2):
                            h = 2 * pair + k
                            gap = rws[h : h + 1, t_here] - cols[s_here, h : h + 1]
                            if sb == tb:
                                gap = jnp.where(causal, gap, NEG)
                            decay = jnp.exp2(gap)
                            meet = meets[k * HALF : (k + 1) * HALF, (tb - sb) * HALF : (tb - sb + 1) * HALF]
                            through = decay * meet
                            both = through * contact
                            touched = through if touched is None else touched + through
                            mixes[k].append((decay * contact).astype(BF16))
                            lane_sum[k] = both if lane_sum[k] is None else lane_sum[k] + both
                            falling = fewer(both)
                            row_part[k][tb] = falling if row_part[k][tb] is None else row_part[k][tb] + falling
                        ds_scr[s_here, t_here] += touched
                    mix = jnp.concatenate([jnp.concatenate(m, axis=1) if len(m) > 1 else m[0] for m in mixes], axis=0)
                    out = nn_dot(mix, dyl_scr[sb * HALF :, :])
                    for k in range(2):
                        total = jnp.sum(lane_sum[k], axis=1, keepdims=True)
                        col_sums[sb] = jnp.where(lane_row == 2 * pair + k, total, col_sums[sb])
                    pieces.append(jnp.where(first, out[:HALF], out[HALF:]))
                for k in range(2):
                    for tb in range(blocks):
                        total = jnp.sum(row_part[k][tb], axis=0, keepdims=True)
                        row_sums[tb] = jnp.where(sub == 2 * pair + k, total, row_sums[tb])
                dx = jnp.concatenate(pieces, axis=0)
                dc = (dx + taps[6:7, here] * dy_scr[...]) * slope_scr[...]
                dv, tap_sums = conv_back(dc, v_scr[j, :, here], taps[:, here])
                dv_scr[:, col] = dv.astype(BF16)
                for row, one in enumerate(tap_sums):
                    sum_ref[row : row + 1, col] = past[row : row + 1, here] + one
            colr_scr[j] = jnp.concatenate(col_sums, axis=0)
            rowr_scr[head_rows, :] = jnp.concatenate(row_sums, axis=1)
            dzp_scr[...] = dz_scr[j]
            dvp_scr[...] = dv_scr[:, lanes(j)]
            dz_copy(j).start()
            return carry

        for at in range(0, rows, CHUNK):
            at = slice(at, at + CHUNK)
            q = vr_scr[at, 3 * STATE - 1 :]
            pull = q * q * (jnp.sum(we_scr[at, :], axis=1, keepdims=True) * (1.0 / inner))
            q_scr[at, :] = jnp.broadcast_to(q, (CHUNK, HALF))
            pull_scr[at, :] = jnp.broadcast_to(pull, (CHUNK, HALF))
        dzp_scr[...] = jnp.zeros_like(dzp_scr)
        dvp_scr[...] = jnp.zeros_like(dvp_scr)
        lax.fori_loop(0, groups, second_pass, 0)
        dn_scr[...] += nt_dot(dzp_scr[...], fold(wz_scr[groups - 1])) + nt_dot(dvp_scr[...], fold(wx_scr[groups - 1]))
        act = act_scr[...]
        ds = ds_scr[...].astype(BF16)
        act_low = act.astype(BF16)
        d_b = nn_dot(ds, act_low[:, STATE:])
        d_c = lax.dot_general(ds, act_low[:, :STATE], (((0,), (0,)), ((), ())), preferred_element_type=F32)
        pre = cr_scr[...]
        sp = sigmoid(pre)
        d_pre = jnp.concatenate([d_b, d_c], axis=1) * (sp * (1.0 + pre * (1.0 - sp)))
        narrow = slice(inner, inner + 2 * STATE)
        d_raw, tap_sums = conv_back(d_pre, vr_scr[:, : 2 * STATE], chanr_ref[...])
        for row, one in enumerate(tap_sums):
            sum_ref[row : row + 1, narrow] = past_ref[row : row + 1, narrow] + one
        sum_ref[5:7, narrow] = jnp.zeros((2, 2 * STATE), F32)
        col_total = colr_scr[0]
        for g in range(1, groups):
            col_total = col_total + pltpu.roll(colr_scr[g], g * GROUP, 1)
        d_sums = rowr_scr[...].T - col_total
        at_row = lax.broadcasted_iota(jnp.int32, (rows, rows), 0)
        of_row = lax.broadcasted_iota(jnp.int32, (rows, rows), 1)
        upper = (of_row >= at_row).astype(F32)
        d_log = jnp.dot(upper, d_sums, precision=EXACT, preferred_element_type=F32)
        step = step_scr[...]
        rate = -jnp.exp(head_ref[1:2, :])
        d_step = col_total / step + rate * d_log
        raw_step = vr_scr[:, 2 * STATE : 3 * STATE] + head_ref[0:1, :]
        used = lax.broadcasted_iota(jnp.int32, (rows, HALF), 1) < inner // HEAD_DIM
        d_raw_step = jnp.where(used, d_step * jax.nn.sigmoid(raw_step), 0.0)
        last = past_ref[7:8, :]
        sum_ref[7:8, width : width + HALF] = last[:, width : width + HALF] + jnp.sum(d_raw_step, axis=0, keepdims=True)
        sum_ref[7:8, width + HALF : width + 2 * HALF] = last[:, width + HALF : width + 2 * HALF] + jnp.sum(
            jnp.where(used, d_log * step * rate, 0.0), axis=0, keepdims=True
        )
        sum_ref[7:8, width + 2 * HALF :] = jnp.zeros((1, inner - width), F32)
        dr = jnp.concatenate([d_raw, d_raw_step], axis=1).astype(BF16)
        dv_scr[:, inner:] = dr
        dv_copy.start()
        wait_all(of_rest())
        for k in range(3):
            dn_scr[...] += nt_dot(dr[:, k * STATE : (k + 1) * STATE], fold(wr_scr[k]))
        u_copy.wait()
        norm_sum = jnp.zeros((SUB, width), F32)
        for at in range(0, rows, 16):
            at = slice(at, at + 16)
            u = u_scr[at, :].astype(F32)
            dn = dn_scr[at, :]
            p = lax.rsqrt(jnp.mean(u * u, axis=1, keepdims=True) + EPS)
            e = dn * norm_ref[...]
            du = g_scr[at, :].astype(F32) + p * e - u * (p * p * p * jnp.mean(u * e, axis=1, keepdims=True))
            dob_scr[at, :] = du.astype(BF16)
            norm_sum = norm_sum + fewer(u * p * dn)
        du_copy.start()
        sum_ref[7:8, :width] = last[:, :width] + jnp.sum(norm_sum, axis=0, keepdims=True)
        for j in range(groups):
            dz_copy(j).wait()
        dv_copy.wait()
        du_copy.wait()


def conv_back(dc, values, taps):
    total, sums = 0.0, [None] * CONV
    for ahead in range(CONV):
        moved = down(dc, -ahead) if ahead else dc
        tap = CONV - 1 - ahead
        total = total + taps[tap : tap + 1, :] * moved
        sums[tap] = jnp.sum(fewer(moved * values), axis=0, keepdims=True)
    return total, sums + [jnp.sum(fewer(dc), axis=0, keepdims=True)]


def backward_slot(place, numbers, kept, grads, past, g, u, w_all, view, norm_gain, chan, chan_r, heads):
    rows, width = g.shape
    inner = chan.shape[1]
    groups = inner // WIDE
    parts, _, depth, _ = view.shape
    far = pl.BlockSpec(memory_space=pl.ANY)
    near = pl.BlockSpec(memory_space=pltpu.VMEM)
    args = [numbers, g, u, w_all, view, *kept, norm_gain, chan, chan_r, heads, past]
    in_specs = [pl.BlockSpec(memory_space=pltpu.SMEM)] + [far] * 10 + [near] * 5
    aliases = {}
    if grads is not None:
        for k, arr in enumerate(grads):
            aliases[len(args)] = k + 1
            args.append(arr)
            in_specs.append(far)
    tall = pltpu.VMEM((groups, parts, depth, WIDE), BF16)
    wide = pltpu.VMEM((groups, rows, WIDE), F32)
    slot = pltpu.VMEM((rows, width), BF16)
    return pl.pallas_call(
        functools.partial(backward_kernel, place),
        in_specs=in_specs,
        out_specs=[far, far, far, near],
        out_shape=[
            jax.ShapeDtypeStruct((rows, width), BF16),
            jax.ShapeDtypeStruct((rows, inner), BF16),
            jax.ShapeDtypeStruct((rows, inner + 3 * STATE), BF16),
            jax.ShapeDtypeStruct((8, inner + 2 * STATE), F32),
        ],
        scratch_shapes=[
            slot,
            slot,
            pltpu.VMEM((groups, WIDE, width), BF16),
            tall,
            tall,
            pltpu.VMEM((3, parts, depth, HALF), BF16),
            pltpu.VMEM((groups, rows, WIDE), BF16),
            wide,
            wide,
            wide,
            pltpu.VMEM((rows, 3 * STATE), F32),
            pltpu.VMEM((rows, 2 * STATE), F32),
            pltpu.VMEM((groups, rows, WIDE), BF16),
            pltpu.VMEM((rows, inner + 3 * STATE), BF16),
            slot,
            wide,
            pltpu.VMEM((rows, WIDE), BF16),
            pltpu.VMEM((rows, WIDE), BF16),
            pltpu.VMEM((rows, HALF), F32),
            pltpu.VMEM((rows, HALF), F32),
            pltpu.VMEM((rows, HALF), F32),
            pltpu.VMEM((rows, HALF), BF16),
            pltpu.VMEM((rows, HALF), BF16),
            pltpu.VMEM((rows, HALF), F32),
            pltpu.VMEM((rows, HALF), F32),
            pltpu.VMEM((rows, HALF), F32),
            pltpu.VMEM((rows, rows), F32),
            pltpu.VMEM((rows, rows), F32),
            pltpu.VMEM((groups, rows, HALF), F32),
            pltpu.VMEM((HALF, rows), F32),
            pltpu.VMEM((groups, rows, HALF), F32),
            pltpu.VMEM((HALF, rows), F32),
            pltpu.VMEM((rows, HALF), F32),
            pltpu.VMEM((rows, 2 * STATE), F32),
            pltpu.VMEM((rows, width), F32),
            pltpu.SemaphoreType.DMA((7 * groups + 7,)),
            pltpu.SemaphoreType.DMA((groups + 2,)),
        ],
        input_output_aliases=aliases,
        compiler_params=pltpu.CompilerParams(vmem_limit_bytes=VMEM),
        cost_estimate=pl.CostEstimate(flops=10**9, bytes_accessed=10**6, transcendentals=0),
        name="backward_slot",
    )(*args)


def pack_kernel(inner, in_ref, out_ref, packed_ref):
    depth, width = in_ref.shape[0], out_ref.shape[1]
    mid, end = 2 * inner + 2 * STATE, in_ref.shape[1]
    packed_ref[:, :width] = out_ref[...]
    tail = width + inner
    for half in range(2):
        rows = slice(half * depth, (half + 1) * depth)
        packed_ref[rows, width:tail] = in_ref[:, half * inner : (half + 1) * inner]
        packed_ref[rows, tail : tail + STATE] = in_ref[:, mid - 2 * STATE + half * STATE : mid - STATE + half * STATE]
        packed_ref[rows, tail + STATE :] = jnp.zeros((depth, STATE), BF16)
    packed_ref[:depth, tail + STATE : tail + STATE + end - mid] = in_ref[:, mid:]


def pack(in_shard, out_shard, inner):
    depth, width = in_shard.shape[0], out_shard.shape[1]
    return pl.pallas_call(
        functools.partial(pack_kernel, inner),
        out_shape=jax.ShapeDtypeStruct((2 * depth, width + inner + 2 * STATE), BF16),
        name="pack",
    )(in_shard, out_shard)


def order_kernel(at_ref, a_ref, own_ref, other_ref, turn_scr):
    turn_scr[...] = a_ref[0].astype(F32).T.reshape(turn_scr.shape)
    spots = own_ref.shape[1]
    for spot in range(spots):
        own_ref[0, spot] = turn_scr[at_ref[1 + spot]].astype(BF16)
        other_ref[0, spot] = turn_scr[at_ref[1 + spots + spot]].astype(BF16)


def by_owner(table, values, micro):
    _, rows, total = values.shape
    count = table.shape[0] - 1
    depth = total // count
    out = pl.BlockSpec((1, count // 2, depth, rows), lambda i, n: (i, 0, 0, 0))
    made = jax.ShapeDtypeStruct((micro, count // 2, depth, rows), BF16)
    parts = pl.pallas_call(
        order_kernel,
        grid_spec=pltpu.PrefetchScalarGridSpec(
            num_scalar_prefetch=1,
            grid=(micro,),
            in_specs=[pl.BlockSpec((1, rows, total), lambda i, n: (n[0] + i, 0, 0))],
            out_specs=[out, out],
            scratch_shapes=[pltpu.VMEM((count, depth, rows), F32)],
        ),
        out_shape=[made, made],
        compiler_params=pltpu.CompilerParams(vmem_limit_bytes=VMEM),
        cost_estimate=pl.CostEstimate(flops=3 * 10**9, bytes_accessed=2 * 10**6, transcendentals=0),
        name="by_owner",
    )(table, values)
    return [a.reshape(micro, total // 2, rows) for a in parts]


def outer_kernel(with_extra, picks, own_ref, sib_ref, *rest):
    rights, outs = rest[:-2], rest[-2:]
    micro, high = own_ref.shape[0], outs[0].shape[0]

    def left_of(part):
        size = high // len(picks[part])
        rows = [
            [ref[m, k * size : (k + 1) * size] for ref in (own_ref, sib_ref) for m in range(micro)] for k in picks[part]
        ]
        return jnp.concatenate([jnp.concatenate(row, axis=1) for row in rows], axis=0)

    if with_extra:
        extra_ref, rights = rights[-1], rights[:-1]
    right = jnp.concatenate([ref[...] for ref in rights], axis=0)
    for part, out_ref in enumerate(outs):
        rows = slice(part * high, (part + 1) * high)
        total = nn_dot(left_of(part), right)
        out_ref[...] = total.astype(BF16)
        if with_extra:
            extra = extra_ref[rows, :]

            @pl.when(pl.program_id(0) == pl.num_programs(0) - 1)
            def _():
                out_ref[:, -HALF:] = (total[:, -HALF:] + extra).astype(BF16)


def outer_sum(own, sib, rights, start, stop, block, extra=None, picks=((0,), (1,))):
    _, total, rows = own.shape
    low, steps = start // block, (stop - start) // block
    full = pl.BlockSpec(own.shape, lambda i: (0, 0, 0))
    out = pl.BlockSpec((total // 2, block), lambda i: (0, i))
    made = jax.ShapeDtypeStruct((total // 2, stop - start), BF16)
    more = [] if extra is None else [extra]
    return pl.pallas_call(
        functools.partial(outer_kernel, extra is not None, picks),
        grid=(steps,),
        in_specs=[full, full]
        + [pl.BlockSpec((rows, block), lambda i: (0, low + i)) for _ in rights]
        + [pl.BlockSpec(a.shape, lambda i: (0, 0)) for a in more],
        out_specs=[out, out],
        out_shape=[made, made],
        compiler_params=pltpu.CompilerParams(vmem_limit_bytes=VMEM),
        cost_estimate=pl.CostEstimate(flops=10**9, bytes_accessed=10**6, transcendentals=0),
        name="outer_sum",
    )(own, sib, *rights, *more)


def listing(sizes, span):
    return [-(-size // span) for size in sizes]


def spread_sums_kernel(sizes, inner, width, lane, spot_ref, own_ref, sib_ref, out_ref):
    total = own_ref[...] + sib_ref[...]
    cols, spots = total.shape[1], spot_ref.shape[0]
    depth, span = out_ref.shape[0] // spots, HALF - lane
    keep = lax.broadcasted_iota(jnp.int32, (8, HALF), 1) >= lane
    head = lax.broadcasted_iota(jnp.int32, (inner, HALF), 0) // HEAD_DIM
    group = (head == lax.broadcasted_iota(jnp.int32, (inner, HALF), 1)).astype(F32)
    skip = jnp.dot(total[:, :inner], group, precision=EXACT, preferred_element_type=F32)
    shared = [total[:, width : width + HALF], total[:, width + HALF : width + 2 * HALF], skip]
    shared = [jnp.where(keep, pltpu.roll(a, lane, 1), 0.0) for a in shared]
    out_ref[...] = jnp.zeros_like(out_ref)
    for spot in range(spots):
        row = spot * depth
        for size, low, high in ((sizes[0], 0, 5), (sizes[1], 5, 6), (sizes[2], 7, 8)):
            for part in range(-(-size // span)):
                start = spot_ref[spot] * size + part * span - lane
                here = pltpu.roll(total, lax.rem(2 * cols - start, cols), 1)[:, :HALF]
                out_ref[row : row + high - low, :] = jnp.where(keep, here, 0.0)[low:high]
                row += high - low
        for a, at in zip(shared, (7, 7, 6)):
            out_ref[row : row + 1, :] = a[at : at + 1]
            row += 1


def spread_sums(spots, own, sib, sizes, inner, width, lane):
    return pl.pallas_call(
        functools.partial(spread_sums_kernel, sizes, inner, width, lane),
        in_specs=[pl.BlockSpec(memory_space=pltpu.SMEM)] + [pl.BlockSpec(memory_space=pltpu.VMEM)] * 2,
        out_shape=jax.ShapeDtypeStruct((width // 2, HALF), F32),
        compiler_params=pltpu.CompilerParams(vmem_limit_bytes=VMEM),
        cost_estimate=pl.CostEstimate(flops=0, bytes_accessed=0, transcendentals=0),
        name="spread_sums",
    )(spots, own, sib)


def swap(values, axis, bit):
    return lax.ppermute(values, axis, [(a, a ^ bit) for a in range(lax.axis_size(axis))])


def all_rows_of(row, axis):
    count = lax.axis_size(axis)
    place = lax.axis_index(axis)
    table = jnp.where(jnp.arange(count, dtype=jnp.int32)[:, None] == place, row[None], jnp.zeros((), row.dtype))
    bit = 1
    while bit < count:
        table = table + swap(table, axis, bit)
        bit *= 2
    return table


def held(value, *after):
    return lax.optimization_barrier((value, after))[0]


def total_of(terms):
    return sum(a.astype(F32) for a in terms)


def exchange(terms, axis, bit):
    half = terms[0].shape[0] // 2
    sent = total_of([a[half:] for a in terms]).astype(BF16)
    return [a[:half] for a in terms] + [swap(sent, axis, bit)], sent


def spots_of(order):
    return [sum(bit for k, bit in enumerate(order) if p >> (len(order) - 1 - k) & 1) for p in range(2 ** len(order))]


def body(
    block_input,
    cotangent,
    lengths,
    in_weight,
    out_weight,
    conv_weight,
    conv_bias,
    norm_gain,
    gate_gain,
    dt_bias,
    a_log,
    skip_d,
):
    axis = "fsdp"
    count = lax.axis_size(axis)
    section = lax.axis_index("section")
    micro, rows, width = block_input.shape
    depth, proj_cols = in_weight.shape[1:]
    inner = gate_gain.shape[1] * count
    channels = conv_bias.shape[1] * count
    heads = dt_bias.shape[1]
    small = [a.reshape(-1) for a in (conv_weight[0], conv_bias[0], norm_gain[0], gate_gain[0])]
    sizes = [a.shape[0] for a in small]
    w_all = lax.all_gather(pack(in_weight[0], out_weight[0], inner), axis, axis=0, tiled=True)
    view = w_all.reshape(count, 2, depth, -1)
    if depth % 16:
        view = view.transpose(1, 0, 2, 3).reshape(1, 2, width, -1)
    flat = all_rows_of(jnp.concatenate(small), axis).astype(F32)
    cuts = [0]
    for size in sizes:
        cuts.append(cuts[-1] + size)
    taps = flat[:, cuts[0] : cuts[1]].reshape(count, CONV, -1).transpose(1, 0, 2).reshape(CONV, channels)
    bias = flat[:, cuts[1] : cuts[2]].reshape(1, channels)
    norm = flat[:, cuts[2] : cuts[3]].reshape(1, width)
    gate = flat[:, cuts[3] : cuts[4]].reshape(1, inner)
    skip = jnp.repeat(skip_d[0], HEAD_DIM)[None]
    chan = jnp.concatenate([taps[:, :inner], bias[:, :inner], gate, skip, jnp.zeros((1, inner), F32)], axis=0)
    chan_r = jnp.concatenate([taps[:, inner:], bias[:, inner:], jnp.zeros((3, channels - inner), F32)], axis=0)
    head_rows = jnp.pad(jnp.stack([dt_bias[0], a_log[0]]), ((0, 6), (0, HALF - heads)))
    places = jnp.arange(rows, dtype=jnp.int32)
    live = [(places < lengths[m, 0])[:, None] for m in range(micro)]

    def numbers(m, stage):
        return jnp.stack([lengths[m, 0], (section == stage).astype(jnp.int32)])

    kept = None
    first, second = [], []
    for m in range(micro):
        kept, h = forward_slot(
            m, numbers(m, 0), kept, block_input[m], w_all, view, norm, chan, chan_r, head_rows, gate, 2 * micro
        )
        first.append(h)
    arrived = [lax.ppermute(h, "section", [(0, 1)]) for h in first]
    for m in range(micro):
        kept, h = forward_slot(
            micro + m, numbers(m, 1), kept, arrived[m], w_all, view, norm, chan, chan_r, head_rows, gate, 2 * micro
        )
        second.append(h)

    def run_backward(place, m, stage, grads, sums, g, u):
        return backward_slot(
            place, numbers(m, stage), kept[1:], grads, sums, g, u, w_all, view, norm, chan, chan_r, head_rows
        )

    is_last = section == 1
    sums = jnp.zeros((8, inner + 2 * STATE), F32)
    grads, late_grads, early_grads, returned = [None] * micro, [None] * micro, [None] * micro, [None] * micro
    for m in reversed(range(micro)):
        late_grads[m], *grads[m], sums = run_backward(micro + m, m, 1, None, sums, cotangent[m], arrived[m])
        returned[m] = lax.ppermute(late_grads[m], "section", [(1, 0)])

    place = lax.axis_index(axis).astype(jnp.int32)
    line = [4 << k for k in range(count.bit_length() - 3)]
    in_order, out_order = [2] + line, line + [2]

    def table_of(order):
        spots = jnp.array(spots_of(order), jnp.int32)
        return jnp.concatenate([(section * micro)[None].astype(jnp.int32), place ^ spots, place ^ 1 ^ spots])

    nb, gb, _ = lax.optimization_barrier((kept[0], kept[1], late_grads[0]))
    out_own, out_other = by_owner(table_of(out_order), gb, micro)
    in_own, in_other = by_owner(table_of(in_order), nb, micro)
    out_sib, in_sib = swap(out_other, axis, 1), swap(in_other, axis, 1)
    returned[-1], out_own, in_own = lax.optimization_barrier((returned[-1], out_own, in_own))

    branch, branch_sib, z_sib, v_sib = [None] * micro, [None] * micro, [None] * micro, [None] * micro

    def take_branch(m):
        branch[m] = jnp.where(live[m], jnp.where(is_last, cotangent[m], returned[m]), jnp.zeros((), BF16))
        branch_sib[m] = swap(branch[m], axis, 1)

    for m in reversed(range(1, micro)):
        take_branch(m)
        early_grads[m], *grads[m], sums = run_backward(m, m, 0, grads[m], sums, returned[m], block_input[m])
        z_sib[m], v_sib[m] = (swap(a, axis, 1) for a in grads[m])
    returned[0], early_grads[-1] = lax.optimization_barrier((returned[0], early_grads[-1]))
    take_branch(0)

    half = width // 2
    a_keep, a_send = outer_sum(out_own, out_sib, branch + branch_sib, 0, half, half)
    branch[0] = held(branch[0], a_send)
    every = range(count // 2)
    b_keep, b_send = outer_sum(
        out_own, out_sib, branch + branch_sib, half, width, half, picks=(every[::2], every[1::2])
    )
    returned[0], a_send, b_send = lax.optimization_barrier((returned[0], a_send, b_send))
    out_a = [a_keep, swap(a_send, axis, line[0])]
    out_b = [b_keep, swap(b_send, axis, 2)]
    early_grads[0], *grads[0], sums = run_backward(0, 0, 0, grads[0], sums, returned[0], block_input[0])
    grads[0], out_a[-1], out_b[-1] = lax.optimization_barrier((grads[0], out_a[-1], out_b[-1]))
    z_sib[0], v_sib[0] = (swap(a, axis, 1) for a in grads[0])
    for bit in line[1:]:
        out_a, a_token = exchange(out_a, axis, bit)
    out_b, b_token = exchange(out_b, axis, line[0])

    z_rows = [a for a, _ in grads] + z_sib
    v_rows = [a for _, a in grads] + v_sib
    cut, block, end = 5 * 384, 384, inner + 3 * STATE
    z_rows[-micro] = held(z_rows[-micro], a_token, b_token)
    half = inner // 2
    z_pairs = [outer_sum(in_own, in_sib, z_rows, 0, half, WIDE)]
    z_rows[-1] = held(z_rows[-1], z_pairs[0][1])
    z_pairs.append(outer_sum(in_own, in_sib, z_rows, half, inner, WIDE))
    out_b[-1] = held(out_b[-1], z_pairs[1][1])
    for bit in line[1:]:
        out_b, b_token = exchange(out_b, axis, bit)
    chunks = [[keep, swap(send, axis, 2)] for keep, send in z_pairs]
    sums, v_rows[0] = held((sums, v_rows[0]), b_token, out_a[-1])
    at_lane = (proj_cols - inner) % HALF
    per = [channels // count, inner // count, width // count]
    in_spots = place ^ jnp.array(spots_of(in_order), jnp.int32)
    extra = spread_sums(in_spots, sums, swap(sums, axis, 1), per, inner, width, at_lane)
    mid = end - 2 * block
    pairs = [outer_sum(in_own, in_sib, v_rows, 0, cut, 640)]
    v_rows[0] = held(v_rows[0], pairs[0][1], out_b[-1], chunks[0][-1])
    pairs.append(outer_sum(in_own, in_sib, v_rows, mid, end, block, extra))
    v_rows[0] = held(v_rows[0], pairs[1][1], chunks[1][-1])
    pairs.append(outer_sum(in_own, in_sib, v_rows, cut, mid, block))
    chunks += [[keep, swap(send, axis, 2)] for keep, send in pairs]
    token = pairs[0][1]
    last = len(chunks) - 1

    def first_step(k, token):
        chunks[k][-1] = held(chunks[k][-1], token)
        chunks[k], token = exchange(chunks[k], axis, line[0])
        return token

    def other_steps(k, token):
        for bit in line[1:]:
            chunks[k][-1] = held(chunks[k][-1], token)
            chunks[k], token = exchange(chunks[k], axis, bit)
        return token

    token = first_step(0, token)
    for k in range(1, last):
        token = first_step(k, (token, chunks[0][-1]) if k == 2 else token)
        token = other_steps(k - 1, token)
    token = first_step(last, token)
    early_grads[0], second = held((early_grads[0], second), token)
    outputs = jnp.stack([jnp.where(section == 0, a, b) for a, b in zip(first, second)])
    input_grads = jnp.stack([jnp.where(is_last, a, b) for a, b in zip(late_grads, early_grads)])
    out_a[-1] = held(out_a[-1], token)
    out_a, _ = exchange(out_a, axis, 2)
    token = other_steps(last - 1, token)
    token = other_steps(last, token)
    chunks[last - 1][-1] = held(chunks[last - 1][-1], token)
    out_grad = jnp.concatenate([total_of(out_a), total_of(out_b)], axis=1)
    in_parts = [total_of(terms) for terms in chunks]
    tail = in_parts[3]
    own_cols = proj_cols - inner - mid
    in_grad = jnp.concatenate([in_parts[0], in_parts[1], in_parts[2], in_parts[4], tail[:, :own_cols]], axis=1)
    span = HALF - at_lane
    tap_parts, gate_parts, norm_parts = listing(per, span)
    rows_of = lambda low, high: tail[low:high, own_cols : own_cols + span]
    cut_rows = [0, 5 * tap_parts, 5 * tap_parts + gate_parts, 5 * tap_parts + gate_parts + norm_parts]
    taps_g = rows_of(0, cut_rows[1]).reshape(tap_parts, 5, span).transpose(1, 0, 2).reshape(5, -1)[:, : per[0]]
    gate_g = rows_of(cut_rows[1], cut_rows[2]).reshape(1, -1)[:, : per[1]]
    norm_g = rows_of(cut_rows[2], cut_rows[3]).reshape(1, -1)[:, : per[2]]
    shared_g = rows_of(cut_rows[3], cut_rows[3] + 3)[:, :heads]
    return (
        outputs[None],
        input_grads[None],
        in_grad[None],
        out_grad[None],
        taps_g[None, :CONV],
        taps_g[CONV:],
        norm_g,
        gate_g,
        shared_g[0:1],
        shared_g[1:2],
        shared_g[2:3],
    )


def solution(mesh):
    in_specs = (
        P(None, "fsdp", None),
        P(None, "fsdp", None),
        P(None, "fsdp"),
        P("section", "fsdp", None),
        P("section", "fsdp", None),
        P("section", None, "fsdp"),
        P("section", "fsdp"),
        P("section", "fsdp"),
        P("section", "fsdp"),
        P("section", None),
        P("section", None),
        P("section", None),
    )
    out_specs = (
        P("section", None, "fsdp", None),
        P("section", None, "fsdp", None),
        P("section", "fsdp", None),
        P("section", "fsdp", None),
        P("section", None, "fsdp"),
        P("section", "fsdp"),
        P("section", "fsdp"),
        P("section", "fsdp"),
        P("section", None),
        P("section", None),
        P("section", None),
    )
    return jax.shard_map(body, mesh=mesh, in_specs=in_specs, out_specs=out_specs, check_vma=False)
```

```python
import functools

import jax
import jax.numpy as jnp
from jax import lax
from jax.experimental import pallas as pl
from jax.experimental.pallas import tpu as pltpu
from jax.sharding import PartitionSpec as P

HEAD_DIM = 64
STATE = 128
CONV = 4
EPS = 1e-05
LOG2E = 1.4426950408889634
HALF = 128
WIDE = 512
GROUP = WIDE // HEAD_DIM
TINY = 1e-30
SUB = 8
CHUNK = 64
NEG = -1e30
VMEM = 60 * 1024 * 1024
F32 = jnp.float32
BF16 = jnp.bfloat16
EXACT = lax.Precision.HIGHEST


def nt_dot(a, b):
    return lax.dot_general(a, b, (((1,), (1,)), ((), ())), preferred_element_type=F32)


def nn_dot(a, b):
    return jnp.dot(a, b, preferred_element_type=F32)


def sigmoid(v):
    return 0.5 * jnp.tanh(0.5 * v) + 0.5


def down(values, steps):
    count = values.shape[0]
    moved = pltpu.roll(values, steps % count, 0)
    rows = lax.broadcasted_iota(jnp.int32, (SUB, values.shape[1]), 0)
    if steps > 0:
        return jnp.concatenate([jnp.where(rows >= steps, moved[:SUB], 0.0), moved[SUB:]], axis=0)
    return jnp.concatenate([moved[:-SUB], jnp.where(rows < SUB + steps, moved[-SUB:], 0.0)], axis=0)


def conv_rows(values, taps, bias):
    total = bias + taps[CONV - 1 : CONV, :] * values
    for back in range(1, CONV):
        total = total + taps[CONV - 1 - back : CONV - back, :] * down(values, back)
    return total


def fewer(block):
    total = block[:SUB]
    for at in range(SUB, block.shape[0], SUB):
        total = total + block[at : at + SUB]
    return total


def piece_of(scr, j, piece, pieces):
    _, parts, depth, _ = scr.shape
    if parts % pieces == 0:
        return fold(scr[j, piece * (parts // pieces) : (piece + 1) * (parts // pieces)])
    size = parts * depth // pieces
    return fold(scr[j])[piece * size : (piece + 1) * size]


def softplus(v):
    return jnp.maximum(v, 0.0) + jnp.log1p(jnp.exp(-jnp.abs(v)))


def step_terms(step_raw, head_ref):
    rows = step_raw.shape[0]
    step = jnp.maximum(softplus(step_raw + head_ref[0:1, :]), TINY)
    rate = -jnp.exp(head_ref[1:2, :])
    at = lax.broadcasted_iota(jnp.int32, (rows, rows), 0)
    of = lax.broadcasted_iota(jnp.int32, (rows, rows), 1)
    lower = (at >= of).astype(F32)
    sums = jnp.dot(lower, step * rate, precision=EXACT, preferred_element_type=F32) * LOG2E
    return step, rate, sums, sums - jnp.log2(step)


def spread(target, values, groups):
    for g in range(groups):
        target[g] = pltpu.roll(values, (HALF - g * GROUP) % HALF, 1) if g else values


def fold(block):
    return block.reshape(-1, block.shape[-1])


def lanes(index):
    return pl.ds(pl.multiple_of(index * WIDE, WIDE), WIDE)


def in_copies(view_ref, wz_scr, wx_scr, wr_scr, sem, base):
    parts, _, depth, _ = view_ref.shape
    width, groups = parts * depth, wz_scr.shape[0]
    tail = width + groups * WIDE

    def of_group(j):
        here = pl.ds(pl.multiple_of(width + j * WIDE, WIDE), WIDE)
        return [
            pltpu.make_async_copy(view_ref.at[:, 0, :, here], wz_scr.at[j], sem.at[base + j]),
            pltpu.make_async_copy(view_ref.at[:, 1, :, here], wx_scr.at[j], sem.at[base + groups + j]),
        ]

    def of_rest():
        return [
            pltpu.make_async_copy(view_ref.at[:, half, :, pl.ds(at, HALF)], wr_scr.at[k], sem.at[base + 2 * groups + k])
            for k, (half, at) in enumerate(((0, tail), (1, tail), (0, tail + HALF)))
        ]

    return of_group, of_rest


def start_all(copies):
    for copy in copies:
        copy.start()


def wait_all(copies):
    for copy in copies:
        copy.wait()


def forward_kernel(place, at_ref, u_hbm, w_hbm, view_hbm, norm_ref, chan_ref, chanr_ref, head_ref, gate_ref, *rest):
    (
        nb_hbm, gb_hbm, z_hbm, v_hbm, y_hbm, vr_hbm, cr_hbm, h_hbm,
        u_scr, wz_scr, wx_scr, wr_scr, wo_scr, nb_scr, gb_scr, z_scr, v_scr, y_scr, vr_scr, cr_scr, h_scr,
        w_scr, sq_scr, s_scr, col_scr, row_scr, sem, out_sem,
    ) = rest[-28:]
    groups, rows, _ = w_scr.shape
    of_group, of_rest = in_copies(view_hbm, wz_scr, wx_scr, wr_scr, sem, 1)
    spare = 2 * groups + 4
    u_copy = pltpu.make_async_copy(u_hbm, u_scr, sem.at[0])

    def of_out(k):
        return pltpu.make_async_copy(w_hbm.at[:, lanes(k)], wo_scr.at[k], sem.at[spare + k])

    def kept_copies(j):
        return [
            pltpu.make_async_copy(scr.at[j], hbm.at[place, :, lanes(j)], out_sem.at[k * groups + j])
            for k, (scr, hbm) in enumerate(((z_scr, z_hbm), (v_scr, v_hbm), (y_scr, y_hbm)))
        ]

    last = 3 * groups
    whole_copies = [
        pltpu.make_async_copy(scr, hbm.at[place], out_sem.at[last + k])
        for k, (scr, hbm) in enumerate(((nb_scr, nb_hbm), (gb_scr, gb_hbm), (vr_scr, vr_hbm), (cr_scr, cr_hbm)))
    ]
    h_copy = pltpu.make_async_copy(h_scr, h_hbm, out_sem.at[last + 4])

    @pl.when(at_ref[1] == 1)
    def _():
        u_copy.start()
        start_all(of_rest())
        for j in range(groups):
            start_all(of_group(j))
        for k in range(wo_scr.shape[0]):
            of_out(k).start()

        u_copy.wait()
        u = u_scr[...].astype(F32)
        scale = lax.rsqrt(jnp.mean(u * u, axis=1, keepdims=True) + EPS)
        nb_scr[...] = (u * scale * norm_ref[...]).astype(BF16)
        nb = nb_scr[...]
        wait_all(of_rest())
        raw = jnp.concatenate([nn_dot(nb, fold(wr_scr[0])), nn_dot(nb, fold(wr_scr[1]))], axis=1)
        steps = nn_dot(nb, fold(wr_scr[2]))
        vr_scr[:, : 2 * STATE] = raw
        vr_scr[:, 2 * STATE :] = steps
        pre = conv_rows(raw, chanr_ref[0:4, :], chanr_ref[4:5, :])
        cr_scr[...] = pre
        act = pre * sigmoid(pre)
        s_scr[...] = lax.dot_general(
            act[:, STATE:], act[:, :STATE], (((1,), (1,)), ((), ())), precision=EXACT, preferred_element_type=F32
        )
        _, _, sums, shifted = step_terms(steps, head_ref)
        spread(col_scr, sums, groups)
        row_scr[...] = shifted.T
        sq_scr[...] = jnp.zeros_like(sq_scr)

        def group(j, carry):
            wait_all(of_group(j))
            nb = nb_scr[...]
            z = nn_dot(nb, fold(wz_scr[j]))
            z_scr[j] = z
            v = nn_dot(nb, fold(wx_scr[j]))
            v_scr[j] = v
            taps = chan_ref[:, lanes(j)]
            c = conv_rows(v, taps[0:4, :], taps[4:5, :])
            x = c * sigmoid(c)
            x_low = x.astype(BF16)
            cols = col_scr[j]
            rws = row_scr[pl.ds(pl.multiple_of(j * GROUP, GROUP), GROUP), :]
            lane = lax.broadcasted_iota(jnp.int32, (HALF, HALF), 1)
            causal = lax.broadcasted_iota(jnp.int32, (HALF, HALF), 0) >= lane
            first = lane < HEAD_DIM
            parts = []
            for pair in range(GROUP // 2):
                here = slice(pair * HALF, (pair + 1) * HALF)
                pieces = []
                for tb in range(rows // HALF):
                    t_here = slice(tb * HALF, (tb + 1) * HALF)
                    both = []
                    for h in (2 * pair, 2 * pair + 1):
                        col = cols[t_here, h : h + 1]
                        mix = []
                        for sb in range(tb + 1):
                            s_here = slice(sb * HALF, (sb + 1) * HALF)
                            gap = col - rws[h : h + 1, s_here]
                            if sb == tb:
                                gap = jnp.where(causal, gap, NEG)
                            mix.append((jnp.exp2(gap) * s_scr[t_here, s_here]).astype(BF16))
                        mix = jnp.concatenate(mix, axis=1) if len(mix) > 1 else mix[0]
                        both.append(nn_dot(mix, x_low[: (tb + 1) * HALF, here]))
                    pieces.append(jnp.where(first, both[0], both[1]))
                parts.append(jnp.concatenate(pieces, axis=0))
            y = jnp.concatenate(parts, axis=1) + taps[6:7, :] * x
            y_scr[j] = y
            w = y * (z * sigmoid(z))
            w_scr[j] = w
            sq_scr[...] += jnp.sum(w * w, axis=1, keepdims=True)
            start_all(kept_copies(j))
            return carry

        lax.fori_loop(0, groups, group, 0)
        scale = lax.rsqrt(sq_scr[...] * (1.0 / (groups * WIDE)) + EPS)
        vr_scr[:, 3 * STATE - 1 :] = scale
        for g in range(groups):
            here = slice(g * WIDE, (g + 1) * WIDE)
            gb_scr[:, here] = (w_scr[g] * scale * gate_ref[:, here]).astype(BF16)
        start_all(whole_copies)
        live = lax.broadcasted_iota(jnp.int32, (rows, 1), 0) < at_ref[0]
        for k in range(wo_scr.shape[0]):
            here = slice(k * WIDE, (k + 1) * WIDE)
            of_out(k).wait()
            branch = jnp.where(live, nn_dot(gb_scr[...], wo_scr[k]), 0.0)
            h_scr[:, here] = (u_scr[:, here].astype(F32) + branch).astype(BF16)
        h_copy.start()
        for j in range(groups):
            wait_all(kept_copies(j))
        wait_all(whole_copies)
        h_copy.wait()


def forward_slot(place, numbers, kept, u, w_all, view, norm_gain, chan, chan_r, heads, gate_gain, slots):
    rows, width = u.shape
    inner = chan.shape[1]
    groups = inner // WIDE
    parts, _, depth, _ = view.shape
    shapes = [((rows, width), BF16), ((rows, inner), BF16)] + [((rows, inner), F32)] * 3
    shapes += [((rows, 3 * STATE), F32), ((rows, 2 * STATE), F32)]
    far = pl.BlockSpec(memory_space=pl.ANY)
    near = pl.BlockSpec(memory_space=pltpu.VMEM)
    args = [numbers, u, w_all, view, norm_gain, chan, chan_r, heads, gate_gain]
    in_specs = [pl.BlockSpec(memory_space=pltpu.SMEM), far, far, far] + [near] * 5
    aliases = {}
    if kept is not None:
        for k, arr in enumerate(kept):
            aliases[len(args)] = k
            args.append(arr)
            in_specs.append(far)
    out_shape = [jax.ShapeDtypeStruct((slots,) + s, d) for s, d in shapes]
    tall = pltpu.VMEM((groups, parts, depth, WIDE), BF16)
    wide = pltpu.VMEM((groups, rows, WIDE), F32)
    *kept, h = pl.pallas_call(
        functools.partial(forward_kernel, place),
        in_specs=in_specs,
        out_specs=[far] * 8,
        out_shape=out_shape + [jax.ShapeDtypeStruct((rows, width), BF16)],
        scratch_shapes=[
            pltpu.VMEM((rows, width), BF16),
            tall,
            tall,
            pltpu.VMEM((3, parts, depth, HALF), BF16),
            pltpu.VMEM((width // WIDE, inner, WIDE), BF16),
            pltpu.VMEM((rows, width), BF16),
            pltpu.VMEM((rows, inner), BF16),
            wide,
            wide,
            wide,
            pltpu.VMEM((rows, 3 * STATE), F32),
            pltpu.VMEM((rows, 2 * STATE), F32),
            pltpu.VMEM((rows, width), BF16),
            wide,
            pltpu.VMEM((rows, 1), F32),
            pltpu.VMEM((rows, rows), F32),
            pltpu.VMEM((groups, rows, HALF), F32),
            pltpu.VMEM((HALF, rows), F32),
            pltpu.SemaphoreType.DMA((2 * groups + 4 + width // WIDE,)),
            pltpu.SemaphoreType.DMA((3 * groups + 5,)),
        ],
        input_output_aliases=aliases,
        compiler_params=pltpu.CompilerParams(vmem_limit_bytes=VMEM),
        cost_estimate=pl.CostEstimate(flops=22 * 10**9, bytes_accessed=60 * 10**6, transcendentals=0),
        name="forward_slot",
    )(*args)
    return kept, h


def backward_kernel(
    place, at_ref, g_hbm, u_hbm, w_hbm, view_hbm, gb_hbm, z_hbm, v_hbm, y_hbm, vr_hbm, cr_hbm,
    norm_ref, chan_ref, chanr_ref, head_ref, past_ref, *rest
):
    (
        du_hbm, dz_hbm, dv_hbm, sum_ref,
        g_scr, u_scr, wo_scr, wz_scr, wx_scr, wr_scr, gb_scr, z_scr, v_scr, y_scr, vr_scr, cr_scr, dz_scr, dv_scr,
        dob_scr, dgb_scr, dzp_scr, dvp_scr, c_scr, dy_scr, slope_scr, xl_scr, dyl_scr, q_scr, pull_scr, we_scr, st_scr, ds_scr, bcol_scr, trow_scr, colr_scr, rowr_scr, step_scr, act_scr, dn_scr,
        sem, out_sem,
    ) = rest[-41:]
    groups, rows, _ = dgb_scr.shape
    width = g_scr.shape[1]
    inner = groups * WIDE
    of_group, of_rest = in_copies(view_hbm, wz_scr, wx_scr, wr_scr, sem, 4)
    base = 2 * groups + 7
    g_copy = pltpu.make_async_copy(g_hbm, g_scr, sem.at[0])
    u_copy = pltpu.make_async_copy(u_hbm, u_scr, sem.at[1])
    vr_copy = pltpu.make_async_copy(vr_hbm.at[place], vr_scr, sem.at[2])
    cr_copy = pltpu.make_async_copy(cr_hbm.at[place], cr_scr, sem.at[3])

    def early(j):
        tall = pl.ds(pl.multiple_of(j * WIDE, WIDE), WIDE)
        return [
            pltpu.make_async_copy(w_hbm.at[tall, pl.ds(0, width)], wo_scr.at[j], sem.at[base + j]),
            pltpu.make_async_copy(gb_hbm.at[place, :, lanes(j)], gb_scr.at[j], sem.at[base + 4 * groups + j]),
        ]

    def late(j):
        return of_group(j) + [
            pltpu.make_async_copy(z_hbm.at[place, :, lanes(j)], z_scr.at[j], sem.at[base + groups + j]),
            pltpu.make_async_copy(y_hbm.at[place, :, lanes(j)], y_scr.at[j], sem.at[base + 2 * groups + j]),
            pltpu.make_async_copy(v_hbm.at[place, :, lanes(j)], v_scr.at[j], sem.at[base + 3 * groups + j]),
        ]

    def dz_copy(j):
        return pltpu.make_async_copy(dz_scr.at[j], dz_hbm.at[:, lanes(j)], out_sem.at[j])

    dv_copy = pltpu.make_async_copy(dv_scr, dv_hbm, out_sem.at[groups])
    du_copy = pltpu.make_async_copy(dob_scr, du_hbm, out_sem.at[groups + 1])

    @pl.when(at_ref[1] != 1)
    def _():
        sum_ref[...] = past_ref[...]

    @pl.when(at_ref[1] == 1)
    def _():
        start_all([g_copy, vr_copy, cr_copy])
        for j in range(groups):
            start_all(early(j))
        for j in range(groups):
            start_all(late(j))
        start_all(of_rest() + [u_copy])

        we_scr[...] = jnp.zeros_like(we_scr)
        ds_scr[...] = jnp.zeros_like(ds_scr)
        dn_scr[...] = jnp.zeros_like(dn_scr)
        rowr_scr[...] = jnp.zeros_like(rowr_scr)
        g_copy.wait()
        live = lax.broadcasted_iota(jnp.int32, (rows, 1), 0) < at_ref[0]
        dob_scr[...] = jnp.where(live, g_scr[...].astype(F32), 0.0).astype(BF16)
        cr_copy.wait()
        pre = cr_scr[...]
        act = pre * sigmoid(pre)
        act_scr[...] = act
        st_scr[...] = lax.dot_general(
            act[:, :STATE], act[:, STATE:], (((1,), (1,)), ((), ())), precision=EXACT, preferred_element_type=F32
        )
        vr_copy.wait()
        step, rate, sums, shifted = step_terms(vr_scr[:, 2 * STATE : 3 * STATE], head_ref)
        step_scr[...] = step
        spread(bcol_scr, shifted, groups)
        trow_scr[...] = sums.T

        def first_pass(j, carry):
            wait_all(early(j))
            for half in range(2):
                wide = slice(half * 2 * HALF, (half + 1) * 2 * HALF)
                dgb = nt_dot(dob_scr[...], wo_scr[j, wide, :])
                dgb_scr[j, :, wide] = dgb
                for at in range(0, rows, CHUNK):
                    at = slice(at, at + CHUNK)
                    product = dgb[at] * gb_scr[j, at, wide].astype(F32)
                    we_scr[at, :] += product[:, :HALF] + product[:, HALF:]
            return carry

        lax.fori_loop(0, groups, first_pass, 0)

        def second_pass(j, carry):
            wait_all(late(j))
            taps = chan_ref[:, lanes(j)]
            past = past_ref[:, lanes(j)]
            before = jnp.maximum(j - 1, 0)
            cols = bcol_scr[j]
            head_rows = pl.ds(pl.multiple_of(j * GROUP, GROUP), GROUP)
            rws = trow_scr[head_rows, :]
            lane = lax.broadcasted_iota(jnp.int32, (HALF, HALF), 1)
            causal = lane >= lax.broadcasted_iota(jnp.int32, (HALF, HALF), 0)
            first = lane < HEAD_DIM
            lane_row = lax.broadcasted_iota(jnp.int32, (1, HALF), 1)
            sub = lax.broadcasted_iota(jnp.int32, (GROUP, HALF), 0)
            blocks = rows // HALF
            pairs = GROUP // 2
            col_sums = [jnp.zeros((HALF, HALF), F32) for _ in range(blocks)]
            row_sums = [jnp.zeros((GROUP, HALF), F32) for _ in range(blocks)]
            for pair in range(pairs):
                here = slice(pair * HALF, (pair + 1) * HALF)
                col = pl.ds(pl.multiple_of(j * WIDE + pair * HALF, HALF), HALF)
                share = slice(pair * (width // pairs), (pair + 1) * (width // pairs))
                dn_scr[:, share] += nt_dot(dzp_scr[...], piece_of(wz_scr, before, pair, pairs)) + nt_dot(
                    dvp_scr[...], piece_of(wx_scr, before, pair, pairs)
                )
                c_scr[...] = conv_rows(v_scr[j, :, here], taps[0:4, here], taps[4:5, here])
                gate_sum = jnp.zeros((SUB, HALF), F32)
                skip_sum = jnp.zeros((SUB, HALF), F32)
                for at in range(0, rows, CHUNK):
                    at = slice(at, at + CHUNK)
                    q = q_scr[at, :]
                    dgb = dgb_scr[j, at, here]
                    z = z_scr[j, at, here]
                    y = y_scr[j, at, here]
                    sz = sigmoid(z)
                    silu_z = z * sz
                    w = y * silu_z
                    scaled = q * dgb
                    dw = scaled * taps[5:6, here] - w * pull_scr[at, :]
                    gate_sum = gate_sum + fewer(w * scaled)
                    dy = dw * silu_z
                    dy_scr[at, :] = dy
                    dyl_scr[at, :] = dy.astype(BF16)
                    dz_scr[j, at, here] = (dw * y * (sz + silu_z * (1.0 - sz))).astype(BF16)
                    c = c_scr[at, :]
                    sc = sigmoid(c)
                    x = c * sc
                    xl_scr[at, :] = x.astype(BF16)
                    slope_scr[at, :] = sc + x * (1.0 - sc)
                    skip_sum = skip_sum + fewer(dy * x)
                sum_ref[5:6, col] = past[5:6, here] + jnp.sum(gate_sum, axis=0, keepdims=True)
                sum_ref[6:7, col] = past[6:7, here] + jnp.sum(skip_sum, axis=0, keepdims=True)

                pieces = []
                row_part = [[None] * blocks, [None] * blocks]
                for sb in range(blocks):
                    s_here = slice(sb * HALF, (sb + 1) * HALF)
                    x_here = xl_scr[s_here, :]
                    none = jnp.zeros_like(x_here)
                    split = jnp.concatenate([jnp.where(first, x_here, none), jnp.where(first, none, x_here)], axis=0)
                    meets = nt_dot(split, dyl_scr[sb * HALF :, :])
                    mixes = [[], []]
                    lane_sum = [None, None]
                    for tb in range(sb, blocks):
                        t_here = slice(tb * HALF, (tb + 1) * HALF)
                        contact = st_scr[s_here, t_here]
                        touched = None
                        for k in range(2):
                            h = 2 * pair + k
                            gap = rws[h : h + 1, t_here] - cols[s_here, h : h + 1]
                            if sb == tb:
                                gap = jnp.where(causal, gap, NEG)
                            decay = jnp.exp2(gap)
                            meet = meets[k * HALF : (k + 1) * HALF, (tb - sb) * HALF : (tb - sb + 1) * HALF]
                            through = decay * meet
                            both = through * contact
                            touched = through if touched is None else touched + through
                            mixes[k].append((decay * contact).astype(BF16))
                            lane_sum[k] = both if lane_sum[k] is None else lane_sum[k] + both
                            falling = fewer(both)
                            row_part[k][tb] = falling if row_part[k][tb] is None else row_part[k][tb] + falling
                        ds_scr[s_here, t_here] += touched
                    mix = jnp.concatenate([jnp.concatenate(m, axis=1) if len(m) > 1 else m[0] for m in mixes], axis=0)
                    out = nn_dot(mix, dyl_scr[sb * HALF :, :])
                    for k in range(2):
                        total = jnp.sum(lane_sum[k], axis=1, keepdims=True)
                        col_sums[sb] = jnp.where(lane_row == 2 * pair + k, total, col_sums[sb])
                    pieces.append(jnp.where(first, out[:HALF], out[HALF:]))
                for k in range(2):
                    for tb in range(blocks):
                        total = jnp.sum(row_part[k][tb], axis=0, keepdims=True)
                        row_sums[tb] = jnp.where(sub == 2 * pair + k, total, row_sums[tb])
                dx = jnp.concatenate(pieces, axis=0)
                dc = (dx + taps[6:7, here] * dy_scr[...]) * slope_scr[...]
                dv, tap_sums = conv_back(dc, v_scr[j, :, here], taps[:, here])
                dv_scr[:, col] = dv.astype(BF16)
                for row, one in enumerate(tap_sums):
                    sum_ref[row : row + 1, col] = past[row : row + 1, here] + one
            colr_scr[j] = jnp.concatenate(col_sums, axis=0)
            rowr_scr[head_rows, :] = jnp.concatenate(row_sums, axis=1)
            dzp_scr[...] = dz_scr[j]
            dvp_scr[...] = dv_scr[:, lanes(j)]
            dz_copy(j).start()
            return carry

        for at in range(0, rows, CHUNK):
            at = slice(at, at + CHUNK)
            q = vr_scr[at, 3 * STATE - 1 :]
            pull = q * q * (jnp.sum(we_scr[at, :], axis=1, keepdims=True) * (1.0 / inner))
            q_scr[at, :] = jnp.broadcast_to(q, (CHUNK, HALF))
            pull_scr[at, :] = jnp.broadcast_to(pull, (CHUNK, HALF))
        dzp_scr[...] = jnp.zeros_like(dzp_scr)
        dvp_scr[...] = jnp.zeros_like(dvp_scr)
        lax.fori_loop(0, groups, second_pass, 0)
        dn_scr[...] += nt_dot(dzp_scr[...], fold(wz_scr[groups - 1])) + nt_dot(dvp_scr[...], fold(wx_scr[groups - 1]))
        act = act_scr[...]
        ds = ds_scr[...].astype(BF16)
        act_low = act.astype(BF16)
        d_b = nn_dot(ds, act_low[:, STATE:])
        d_c = lax.dot_general(ds, act_low[:, :STATE], (((0,), (0,)), ((), ())), preferred_element_type=F32)
        pre = cr_scr[...]
        sp = sigmoid(pre)
        d_pre = jnp.concatenate([d_b, d_c], axis=1) * (sp * (1.0 + pre * (1.0 - sp)))
        narrow = slice(inner, inner + 2 * STATE)
        d_raw, tap_sums = conv_back(d_pre, vr_scr[:, : 2 * STATE], chanr_ref[...])
        for row, one in enumerate(tap_sums):
            sum_ref[row : row + 1, narrow] = past_ref[row : row + 1, narrow] + one
        sum_ref[5:7, narrow] = jnp.zeros((2, 2 * STATE), F32)
        col_total = colr_scr[0]
        for g in range(1, groups):
            col_total = col_total + pltpu.roll(colr_scr[g], g * GROUP, 1)
        d_sums = rowr_scr[...].T - col_total
        at_row = lax.broadcasted_iota(jnp.int32, (rows, rows), 0)
        of_row = lax.broadcasted_iota(jnp.int32, (rows, rows), 1)
        upper = (of_row >= at_row).astype(F32)
        d_log = jnp.dot(upper, d_sums, precision=EXACT, preferred_element_type=F32)
        step = step_scr[...]
        rate = -jnp.exp(head_ref[1:2, :])
        d_step = col_total / step + rate * d_log
        raw_step = vr_scr[:, 2 * STATE : 3 * STATE] + head_ref[0:1, :]
        used = lax.broadcasted_iota(jnp.int32, (rows, HALF), 1) < inner // HEAD_DIM
        d_raw_step = jnp.where(used, d_step * jax.nn.sigmoid(raw_step), 0.0)
        last = past_ref[7:8, :]
        sum_ref[7:8, width : width + HALF] = last[:, width : width + HALF] + jnp.sum(d_raw_step, axis=0, keepdims=True)
        sum_ref[7:8, width + HALF : width + 2 * HALF] = last[:, width + HALF : width + 2 * HALF] + jnp.sum(
            jnp.where(used, d_log * step * rate, 0.0), axis=0, keepdims=True
        )
        sum_ref[7:8, width + 2 * HALF :] = jnp.zeros((1, inner - width), F32)
        dr = jnp.concatenate([d_raw, d_raw_step], axis=1).astype(BF16)
        dv_scr[:, inner:] = dr
        dv_copy.start()
        wait_all(of_rest())
        for k in range(3):
            dn_scr[...] += nt_dot(dr[:, k * STATE : (k + 1) * STATE], fold(wr_scr[k]))
        u_copy.wait()
        norm_sum = jnp.zeros((SUB, width), F32)
        for at in range(0, rows, 16):
            at = slice(at, at + 16)
            u = u_scr[at, :].astype(F32)
            dn = dn_scr[at, :]
            p = lax.rsqrt(jnp.mean(u * u, axis=1, keepdims=True) + EPS)
            e = dn * norm_ref[...]
            du = g_scr[at, :].astype(F32) + p * e - u * (p * p * p * jnp.mean(u * e, axis=1, keepdims=True))
            dob_scr[at, :] = du.astype(BF16)
            norm_sum = norm_sum + fewer(u * p * dn)
        du_copy.start()
        sum_ref[7:8, :width] = last[:, :width] + jnp.sum(norm_sum, axis=0, keepdims=True)
        for j in range(groups):
            dz_copy(j).wait()
        dv_copy.wait()
        du_copy.wait()


def conv_back(dc, values, taps):
    total, sums = 0.0, [None] * CONV
    for ahead in range(CONV):
        moved = down(dc, -ahead) if ahead else dc
        tap = CONV - 1 - ahead
        total = total + taps[tap : tap + 1, :] * moved
        sums[tap] = jnp.sum(fewer(moved * values), axis=0, keepdims=True)
    return total, sums + [jnp.sum(fewer(dc), axis=0, keepdims=True)]


def backward_slot(place, numbers, kept, grads, past, g, u, w_all, view, norm_gain, chan, chan_r, heads):
    rows, width = g.shape
    inner = chan.shape[1]
    groups = inner // WIDE
    parts, _, depth, _ = view.shape
    far = pl.BlockSpec(memory_space=pl.ANY)
    near = pl.BlockSpec(memory_space=pltpu.VMEM)
    args = [numbers, g, u, w_all, view, *kept, norm_gain, chan, chan_r, heads, past]
    in_specs = [pl.BlockSpec(memory_space=pltpu.SMEM)] + [far] * 10 + [near] * 5
    aliases = {}
    if grads is not None:
        for k, arr in enumerate(grads):
            aliases[len(args)] = k + 1
            args.append(arr)
            in_specs.append(far)
    tall = pltpu.VMEM((groups, parts, depth, WIDE), BF16)
    wide = pltpu.VMEM((groups, rows, WIDE), F32)
    slot = pltpu.VMEM((rows, width), BF16)
    return pl.pallas_call(
        functools.partial(backward_kernel, place),
        in_specs=in_specs,
        out_specs=[far, far, far, near],
        out_shape=[
            jax.ShapeDtypeStruct((rows, width), BF16),
            jax.ShapeDtypeStruct((rows, inner), BF16),
            jax.ShapeDtypeStruct((rows, inner + 3 * STATE), BF16),
            jax.ShapeDtypeStruct((8, inner + 2 * STATE), F32),
        ],
        scratch_shapes=[
            slot,
            slot,
            pltpu.VMEM((groups, WIDE, width), BF16),
            tall,
            tall,
            pltpu.VMEM((3, parts, depth, HALF), BF16),
            pltpu.VMEM((groups, rows, WIDE), BF16),
            wide,
            wide,
            wide,
            pltpu.VMEM((rows, 3 * STATE), F32),
            pltpu.VMEM((rows, 2 * STATE), F32),
            pltpu.VMEM((groups, rows, WIDE), BF16),
            pltpu.VMEM((rows, inner + 3 * STATE), BF16),
            slot,
            wide,
            pltpu.VMEM((rows, WIDE), BF16),
            pltpu.VMEM((rows, WIDE), BF16),
            pltpu.VMEM((rows, HALF), F32),
            pltpu.VMEM((rows, HALF), F32),
            pltpu.VMEM((rows, HALF), F32),
            pltpu.VMEM((rows, HALF), BF16),
            pltpu.VMEM((rows, HALF), BF16),
            pltpu.VMEM((rows, HALF), F32),
            pltpu.VMEM((rows, HALF), F32),
            pltpu.VMEM((rows, HALF), F32),
            pltpu.VMEM((rows, rows), F32),
            pltpu.VMEM((rows, rows), F32),
            pltpu.VMEM((groups, rows, HALF), F32),
            pltpu.VMEM((HALF, rows), F32),
            pltpu.VMEM((groups, rows, HALF), F32),
            pltpu.VMEM((HALF, rows), F32),
            pltpu.VMEM((rows, HALF), F32),
            pltpu.VMEM((rows, 2 * STATE), F32),
            pltpu.VMEM((rows, width), F32),
            pltpu.SemaphoreType.DMA((7 * groups + 7,)),
            pltpu.SemaphoreType.DMA((groups + 2,)),
        ],
        input_output_aliases=aliases,
        compiler_params=pltpu.CompilerParams(vmem_limit_bytes=VMEM),
        cost_estimate=pl.CostEstimate(flops=10**9, bytes_accessed=10**6, transcendentals=0),
        name="backward_slot",
    )(*args)


def pack_kernel(inner, in_ref, out_ref, packed_ref):
    depth, width = in_ref.shape[0], out_ref.shape[1]
    mid, end = 2 * inner + 2 * STATE, in_ref.shape[1]
    packed_ref[:, :width] = out_ref[...]
    tail = width + inner
    for half in range(2):
        rows = slice(half * depth, (half + 1) * depth)
        packed_ref[rows, width:tail] = in_ref[:, half * inner : (half + 1) * inner]
        packed_ref[rows, tail : tail + STATE] = in_ref[:, mid - 2 * STATE + half * STATE : mid - STATE + half * STATE]
        packed_ref[rows, tail + STATE :] = jnp.zeros((depth, STATE), BF16)
    packed_ref[:depth, tail + STATE : tail + STATE + end - mid] = in_ref[:, mid:]


def pack(in_shard, out_shard, inner):
    depth, width = in_shard.shape[0], out_shard.shape[1]
    return pl.pallas_call(
        functools.partial(pack_kernel, inner),
        out_shape=jax.ShapeDtypeStruct((2 * depth, width + inner + 2 * STATE), BF16),
        name="pack",
    )(in_shard, out_shard)


def order_kernel(at_ref, a_ref, own_ref, other_ref, turn_scr):
    turn_scr[...] = a_ref[0].astype(F32).T.reshape(turn_scr.shape)
    spots = own_ref.shape[1]
    for spot in range(spots):
        own_ref[0, spot] = turn_scr[at_ref[1 + spot]].astype(BF16)
        other_ref[0, spot] = turn_scr[at_ref[1 + spots + spot]].astype(BF16)


def by_owner(table, values, micro):
    _, rows, total = values.shape
    count = table.shape[0] - 1
    depth = total // count
    out = pl.BlockSpec((1, count // 2, depth, rows), lambda i, n: (i, 0, 0, 0))
    made = jax.ShapeDtypeStruct((micro, count // 2, depth, rows), BF16)
    parts = pl.pallas_call(
        order_kernel,
        grid_spec=pltpu.PrefetchScalarGridSpec(
            num_scalar_prefetch=1,
            grid=(micro,),
            in_specs=[pl.BlockSpec((1, rows, total), lambda i, n: (n[0] + i, 0, 0))],
            out_specs=[out, out],
            scratch_shapes=[pltpu.VMEM((count, depth, rows), F32)],
        ),
        out_shape=[made, made],
        compiler_params=pltpu.CompilerParams(vmem_limit_bytes=VMEM),
        cost_estimate=pl.CostEstimate(flops=3 * 10**9, bytes_accessed=2 * 10**6, transcendentals=0),
        name="by_owner",
    )(table, values)
    return [a.reshape(micro, total // 2, rows) for a in parts]


def outer_kernel(with_extra, picks, own_ref, sib_ref, *rest):
    rights, outs = rest[:-2], rest[-2:]
    micro, high = own_ref.shape[0], outs[0].shape[0]

    def left_of(part):
        size = high // len(picks[part])
        rows = [
            [ref[m, k * size : (k + 1) * size] for ref in (own_ref, sib_ref) for m in range(micro)] for k in picks[part]
        ]
        return jnp.concatenate([jnp.concatenate(row, axis=1) for row in rows], axis=0)

    if with_extra:
        extra_ref, rights = rights[-1], rights[:-1]
    right = jnp.concatenate([ref[...] for ref in rights], axis=0)
    for part, out_ref in enumerate(outs):
        rows = slice(part * high, (part + 1) * high)
        total = nn_dot(left_of(part), right)
        out_ref[...] = total.astype(BF16)
        if with_extra:
            extra = extra_ref[rows, :]

            @pl.when(pl.program_id(0) == pl.num_programs(0) - 1)
            def _():
                out_ref[:, -HALF:] = (total[:, -HALF:] + extra).astype(BF16)


def outer_sum(own, sib, rights, start, stop, block, extra=None, picks=((0,), (1,))):
    _, total, rows = own.shape
    low, steps = start // block, (stop - start) // block
    full = pl.BlockSpec(own.shape, lambda i: (0, 0, 0))
    out = pl.BlockSpec((total // 2, block), lambda i: (0, i))
    made = jax.ShapeDtypeStruct((total // 2, stop - start), BF16)
    more = [] if extra is None else [extra]
    return pl.pallas_call(
        functools.partial(outer_kernel, extra is not None, picks),
        grid=(steps,),
        in_specs=[full, full]
        + [pl.BlockSpec((rows, block), lambda i: (0, low + i)) for _ in rights]
        + [pl.BlockSpec(a.shape, lambda i: (0, 0)) for a in more],
        out_specs=[out, out],
        out_shape=[made, made],
        compiler_params=pltpu.CompilerParams(vmem_limit_bytes=VMEM),
        cost_estimate=pl.CostEstimate(flops=10**9, bytes_accessed=10**6, transcendentals=0),
        name="outer_sum",
    )(own, sib, *rights, *more)


def out_kernel(picks, own_ref, sib_ref, *rest):
    rights, outs = rest[:-4], rest[-4:]
    micro, high = own_ref.shape[0], outs[0].shape[0]
    right = jnp.concatenate([ref[...] for ref in rights], axis=0)

    def fill(two):
        for out_ref, spots in zip(outs[2 * two : 2 * two + 2], picks[two]):
            size = high // len(spots)
            rows = [
                [ref[m, k * size : (k + 1) * size] for ref in (own_ref, sib_ref) for m in range(micro)] for k in spots
            ]
            left = jnp.concatenate([jnp.concatenate(row, axis=1) for row in rows], axis=0)
            out_ref[...] = nn_dot(left, right).astype(BF16)

    for two in range(2):
        pl.when(pl.program_id(0) == two)(functools.partial(fill, two))


def out_sums(own, sib, rights, picks):
    _, total, rows = own.shape
    half = rights[0].shape[1] // 2
    full = pl.BlockSpec(own.shape, lambda i: (0, 0, 0))
    out = pl.BlockSpec((total // 2, half), lambda i: (0, 0))
    made = jax.ShapeDtypeStruct((total // 2, half), BF16)
    return pl.pallas_call(
        functools.partial(out_kernel, picks),
        grid=(2,),
        in_specs=[full, full] + [pl.BlockSpec((rows, half), lambda i: (0, i)) for _ in rights],
        out_specs=[out] * 4,
        out_shape=[made] * 4,
        compiler_params=pltpu.CompilerParams(vmem_limit_bytes=VMEM),
        cost_estimate=pl.CostEstimate(flops=10**9, bytes_accessed=10**6, transcendentals=0),
        name="out_sums",
    )(own, sib, *rights)


def listing(sizes, span):
    return [-(-size // span) for size in sizes]


def spread_sums_kernel(sizes, inner, width, lane, spot_ref, own_ref, sib_ref, out_ref):
    total = own_ref[...] + sib_ref[...]
    cols, spots = total.shape[1], spot_ref.shape[0]
    depth, span = out_ref.shape[0] // spots, HALF - lane
    keep = lax.broadcasted_iota(jnp.int32, (8, HALF), 1) >= lane
    head = lax.broadcasted_iota(jnp.int32, (inner, HALF), 0) // HEAD_DIM
    group = (head == lax.broadcasted_iota(jnp.int32, (inner, HALF), 1)).astype(F32)
    skip = jnp.dot(total[:, :inner], group, precision=EXACT, preferred_element_type=F32)
    shared = [total[:, width : width + HALF], total[:, width + HALF : width + 2 * HALF], skip]
    shared = [jnp.where(keep, pltpu.roll(a, lane, 1), 0.0) for a in shared]
    out_ref[...] = jnp.zeros_like(out_ref)
    for spot in range(spots):
        row = spot * depth
        for size, low, high in ((sizes[0], 0, 5), (sizes[1], 5, 6), (sizes[2], 7, 8)):
            for part in range(-(-size // span)):
                start = spot_ref[spot] * size + part * span - lane
                here = pltpu.roll(total, lax.rem(2 * cols - start, cols), 1)[:, :HALF]
                out_ref[row : row + high - low, :] = jnp.where(keep, here, 0.0)[low:high]
                row += high - low
        for a, at in zip(shared, (7, 7, 6)):
            out_ref[row : row + 1, :] = a[at : at + 1]
            row += 1


def spread_sums(spots, own, sib, sizes, inner, width, lane):
    return pl.pallas_call(
        functools.partial(spread_sums_kernel, sizes, inner, width, lane),
        in_specs=[pl.BlockSpec(memory_space=pltpu.SMEM)] + [pl.BlockSpec(memory_space=pltpu.VMEM)] * 2,
        out_shape=jax.ShapeDtypeStruct((width // 2, HALF), F32),
        compiler_params=pltpu.CompilerParams(vmem_limit_bytes=VMEM),
        cost_estimate=pl.CostEstimate(flops=0, bytes_accessed=0, transcendentals=0),
        name="spread_sums",
    )(spots, own, sib)


def swap(values, axis, bit):
    return lax.ppermute(values, axis, [(a, a ^ bit) for a in range(lax.axis_size(axis))])


def all_rows_of(row, axis):
    count = lax.axis_size(axis)
    place = lax.axis_index(axis)
    table = jnp.where(jnp.arange(count, dtype=jnp.int32)[:, None] == place, row[None], jnp.zeros((), row.dtype))
    bit = 1
    while bit < count:
        table = table + swap(table, axis, bit)
        bit *= 2
    return table


def held(value, *after):
    return lax.optimization_barrier((value, after))[0]


def total_of(terms):
    return sum(a.astype(F32) for a in terms)


def exchange(terms, axis, bit):
    half = terms[0].shape[0] // 2
    sent = total_of([a[half:] for a in terms]).astype(BF16)
    return [a[:half] for a in terms] + [swap(sent, axis, bit)], sent


def spots_of(order):
    return [sum(bit for k, bit in enumerate(order) if p >> (len(order) - 1 - k) & 1) for p in range(2 ** len(order))]


def body(
    block_input,
    cotangent,
    lengths,
    in_weight,
    out_weight,
    conv_weight,
    conv_bias,
    norm_gain,
    gate_gain,
    dt_bias,
    a_log,
    skip_d,
):
    axis = "fsdp"
    count = lax.axis_size(axis)
    section = lax.axis_index("section")
    micro, rows, width = block_input.shape
    depth, proj_cols = in_weight.shape[1:]
    inner = gate_gain.shape[1] * count
    channels = conv_bias.shape[1] * count
    heads = dt_bias.shape[1]
    small = [a.reshape(-1) for a in (conv_weight[0], conv_bias[0], norm_gain[0], gate_gain[0])]
    sizes = [a.shape[0] for a in small]
    w_all = lax.all_gather(pack(in_weight[0], out_weight[0], inner), axis, axis=0, tiled=True)
    view = w_all.reshape(count, 2, depth, -1)
    if depth % 16:
        view = view.transpose(1, 0, 2, 3).reshape(1, 2, width, -1)
    flat = all_rows_of(jnp.concatenate(small), axis).astype(F32)
    cuts = [0]
    for size in sizes:
        cuts.append(cuts[-1] + size)
    taps = flat[:, cuts[0] : cuts[1]].reshape(count, CONV, -1).transpose(1, 0, 2).reshape(CONV, channels)
    bias = flat[:, cuts[1] : cuts[2]].reshape(1, channels)
    norm = flat[:, cuts[2] : cuts[3]].reshape(1, width)
    gate = flat[:, cuts[3] : cuts[4]].reshape(1, inner)
    skip = jnp.repeat(skip_d[0], HEAD_DIM)[None]
    chan = jnp.concatenate([taps[:, :inner], bias[:, :inner], gate, skip, jnp.zeros((1, inner), F32)], axis=0)
    chan_r = jnp.concatenate([taps[:, inner:], bias[:, inner:], jnp.zeros((3, channels - inner), F32)], axis=0)
    head_rows = jnp.pad(jnp.stack([dt_bias[0], a_log[0]]), ((0, 6), (0, HALF - heads)))
    places = jnp.arange(rows, dtype=jnp.int32)
    live = [(places < lengths[m, 0])[:, None] for m in range(micro)]

    def numbers(m, stage):
        return jnp.stack([lengths[m, 0], (section == stage).astype(jnp.int32)])

    kept = None
    first, second = [], []
    for m in range(micro):
        kept, h = forward_slot(
            m, numbers(m, 0), kept, block_input[m], w_all, view, norm, chan, chan_r, head_rows, gate, 2 * micro
        )
        first.append(h)
    arrived = [lax.ppermute(h, "section", [(0, 1)]) for h in first]
    for m in range(micro):
        kept, h = forward_slot(
            micro + m, numbers(m, 1), kept, arrived[m], w_all, view, norm, chan, chan_r, head_rows, gate, 2 * micro
        )
        second.append(h)

    def run_backward(place, m, stage, grads, sums, g, u):
        return backward_slot(
            place, numbers(m, stage), kept[1:], grads, sums, g, u, w_all, view, norm, chan, chan_r, head_rows
        )

    is_last = section == 1
    sums = jnp.zeros((8, inner + 2 * STATE), F32)
    grads, late_grads, early_grads, returned = [None] * micro, [None] * micro, [None] * micro, [None] * micro
    for m in reversed(range(micro)):
        late_grads[m], *grads[m], sums = run_backward(micro + m, m, 1, None, sums, cotangent[m], arrived[m])
        returned[m] = lax.ppermute(late_grads[m], "section", [(1, 0)])

    place = lax.axis_index(axis).astype(jnp.int32)
    line = [4 << k for k in range(count.bit_length() - 3)]
    in_order, out_order = [2] + line, line + [2]

    def table_of(order):
        spots = jnp.array(spots_of(order), jnp.int32)
        return jnp.concatenate([(section * micro)[None].astype(jnp.int32), place ^ spots, place ^ 1 ^ spots])

    nb, gb, _ = lax.optimization_barrier((kept[0], kept[1], late_grads[0]))
    out_own, out_other = by_owner(table_of(out_order), gb, micro)
    in_own, in_other = by_owner(table_of(in_order), nb, micro)
    out_sib, in_sib = swap(out_other, axis, 1), swap(in_other, axis, 1)
    returned[-1], out_own, in_own = lax.optimization_barrier((returned[-1], out_own, in_own))

    branch, branch_sib, z_sib, v_sib = [None] * micro, [None] * micro, [None] * micro, [None] * micro

    def take_branch(m):
        branch[m] = jnp.where(live[m], jnp.where(is_last, cotangent[m], returned[m]), jnp.zeros((), BF16))
        branch_sib[m] = swap(branch[m], axis, 1)

    for m in reversed(range(1, micro)):
        take_branch(m)
        early_grads[m], *grads[m], sums = run_backward(m, m, 0, grads[m], sums, returned[m], block_input[m])
        z_sib[m], v_sib[m] = (swap(a, axis, 1) for a in grads[m])
    returned[0], early_grads[-1] = lax.optimization_barrier((returned[0], early_grads[-1]))
    take_branch(0)

    every = range(count // 2)
    a_keep, a_send, b_keep, b_send = out_sums(
        out_own, out_sib, branch + branch_sib, (((0,), (1,)), (every[::2], every[1::2]))
    )
    returned[0], a_send, b_send = lax.optimization_barrier((returned[0], a_send, b_send))
    out_a = [a_keep, swap(a_send, axis, line[0])]
    out_b = [b_keep, swap(b_send, axis, 2)]
    early_grads[0], *grads[0], sums = run_backward(0, 0, 0, grads[0], sums, returned[0], block_input[0])
    grads[0], out_a[-1], out_b[-1] = lax.optimization_barrier((grads[0], out_a[-1], out_b[-1]))
    z_sib[0], v_sib[0] = (swap(a, axis, 1) for a in grads[0])
    for bit in line[1:]:
        out_a, a_token = exchange(out_a, axis, bit)
    out_b, b_token = exchange(out_b, axis, line[0])

    z_rows = [a for a, _ in grads] + z_sib
    v_rows = [a for _, a in grads] + v_sib
    cut, block, end = 5 * 384, 384, inner + 3 * STATE
    z_rows[-micro] = held(z_rows[-micro], a_token, b_token)
    half = inner // 2
    z_pairs = [outer_sum(in_own, in_sib, z_rows, 0, half, WIDE)]
    z_rows[-1] = held(z_rows[-1], z_pairs[0][1])
    z_pairs.append(outer_sum(in_own, in_sib, z_rows, half, inner, WIDE))
    out_b[-1] = held(out_b[-1], z_pairs[1][1])
    for bit in line[1:]:
        out_b, b_token = exchange(out_b, axis, bit)
    chunks = [[keep, swap(send, axis, 2)] for keep, send in z_pairs]
    sums, v_rows[0] = held((sums, v_rows[0]), b_token, out_a[-1])
    at_lane = (proj_cols - inner) % HALF
    per = [channels // count, inner // count, width // count]
    in_spots = place ^ jnp.array(spots_of(in_order), jnp.int32)
    extra = spread_sums(in_spots, sums, swap(sums, axis, 1), per, inner, width, at_lane)
    mid = end - 2 * block
    pairs = [outer_sum(in_own, in_sib, v_rows, 0, cut, 640)]
    v_rows[0] = held(v_rows[0], pairs[0][1], out_b[-1], chunks[0][-1])
    pairs.append(outer_sum(in_own, in_sib, v_rows, mid, end, block, extra))
    v_rows[0] = held(v_rows[0], pairs[1][1], chunks[1][-1])
    pairs.append(outer_sum(in_own, in_sib, v_rows, cut, mid, block))
    chunks += [[keep, swap(send, axis, 2)] for keep, send in pairs]
    token = pairs[0][1]
    last = len(chunks) - 1

    def first_step(k, token):
        chunks[k][-1] = held(chunks[k][-1], token)
        chunks[k], token = exchange(chunks[k], axis, line[0])
        return token

    def other_steps(k, token):
        for bit in line[1:]:
            chunks[k][-1] = held(chunks[k][-1], token)
            chunks[k], token = exchange(chunks[k], axis, bit)
        return token

    token = first_step(0, token)
    for k in range(1, last):
        token = first_step(k, (token, chunks[0][-1]) if k == 2 else token)
        token = other_steps(k - 1, token)
    token = first_step(last, token)
    early_grads[0], second = held((early_grads[0], second), token)
    outputs = jnp.stack([jnp.where(section == 0, a, b) for a, b in zip(first, second)])
    input_grads = jnp.stack([jnp.where(is_last, a, b) for a, b in zip(late_grads, early_grads)])
    out_a[-1] = held(out_a[-1], token)
    out_a, _ = exchange(out_a, axis, 2)
    token = other_steps(last - 1, token)
    token = other_steps(last, token)
    chunks[last - 1][-1] = held(chunks[last - 1][-1], token)
    out_grad = jnp.concatenate([total_of(out_a), total_of(out_b)], axis=1)
    chunks[last - 1][-1], chunks[last][-1] = held((chunks[last - 1][-1], chunks[last][-1]), out_grad)
    in_parts = [total_of(terms) for terms in chunks]
    tail = in_parts[3]
    own_cols = proj_cols - inner - mid
    in_grad = jnp.concatenate([in_parts[0], in_parts[1], in_parts[2], in_parts[4], tail[:, :own_cols]], axis=1)
    span = HALF - at_lane
    tap_parts, gate_parts, norm_parts = listing(per, span)
    rows_of = lambda low, high: tail[low:high, own_cols : own_cols + span]
    cut_rows = [0, 5 * tap_parts, 5 * tap_parts + gate_parts, 5 * tap_parts + gate_parts + norm_parts]
    taps_g = rows_of(0, cut_rows[1]).reshape(tap_parts, 5, span).transpose(1, 0, 2).reshape(5, -1)[:, : per[0]]
    gate_g = rows_of(cut_rows[1], cut_rows[2]).reshape(1, -1)[:, : per[1]]
    norm_g = rows_of(cut_rows[2], cut_rows[3]).reshape(1, -1)[:, : per[2]]
    shared_g = rows_of(cut_rows[3], cut_rows[3] + 3)[:, :heads]
    return (
        outputs[None],
        input_grads[None],
        in_grad[None],
        out_grad[None],
        taps_g[None, :CONV],
        taps_g[CONV:],
        norm_g,
        gate_g,
        shared_g[0:1],
        shared_g[1:2],
        shared_g[2:3],
    )


def solution(mesh):
    in_specs = (
        P(None, "fsdp", None),
        P(None, "fsdp", None),
        P(None, "fsdp"),
        P("section", "fsdp", None),
        P("section", "fsdp", None),
        P("section", None, "fsdp"),
        P("section", "fsdp"),
        P("section", "fsdp"),
        P("section", "fsdp"),
        P("section", None),
        P("section", None),
        P("section", None),
    )
    out_specs = (
        P("section", None, "fsdp", None),
        P("section", None, "fsdp", None),
        P("section", "fsdp", None),
        P("section", "fsdp", None),
        P("section", None, "fsdp"),
        P("section", "fsdp"),
        P("section", "fsdp"),
        P("section", "fsdp"),
        P("section", None),
        P("section", None),
        P("section", None),
    )
    return jax.shard_map(body, mesh=mesh, in_specs=in_specs, out_specs=out_specs, check_vma=False)
```
